256 devices in a mesh: dp: 8 (over x, y_hi), ctx: 32 (over z, y_lo, core).
Axes of the slice: x: 4, y: 4 (y_hi: 2, y_lo: 2; y = y_hi * 2 + y_lo), z: 8, core: 2. Of those that a mesh axis runs over, the one named last changes fastest.
Arguments:
- tokens: bfloat16 [8, 8192, 1536], P('dp', 'ctx'), may hold values from -40 to 40, as said below
- segments: int32 [8, 8192], P('dp'), may hold values from 0 to 7, never falling along the last dimension, each value on 1 to 1536 neighbouring positions
- w_query: bfloat16 [1536, 1536], replicated, as said below
- w_keyval: bfloat16 [1536, 512], replicated, as said below
- grad_context: bfloat16 [8, 8192, 1536], P('dp', 'ctx'), may hold values from -6 to 6
Outputs:
- context: bfloat16 [8, 8192, 1536], P('dp', 'ctx')
- grad_tokens: bfloat16 [8, 8192, 1536], P('dp', 'ctx')
- grad_query_w: bfloat16 [1536, 1536], P('ctx')
- grad_keyval_w: bfloat16 [1536, 512], P('ctx')
The draws below stay inside these ranges and needn't reach their ends.
Inputs may be any that keep to these rules, and one draw needn't show every extreme that they name: `segments`: document numbers never fall along a sequence; a document covers at most 1536 positions. `tokens`: activations of order one. `w_query`: a weight matrix of fan-in 1536. `w_keyval`: a weight matrix of fan-in 1536.
All inputs are finite; a program needn't handle non-finite values.
Results may differ from the reference program's by a relative error of at most 0.03.
The reference program's roundings to bfloat16 on the way (of `queries`, `keyval`, `probs_low`, `grad_scores`, `grad_queries` and `grad_keyval`) count: a program that leaves them out, or rounds other values in their place, can miss the bound.
Values may be sent and summed in bfloat16 or wider, within the bound.
No kernel may reach another device: no remote copies, remote signals or barrier semaphores. Data moves between devices by JAX's collectives and lax.ppermute only.
A program may use at most 128 MiB of HBM per device.

```python
import math
import jax
import jax.numpy as jnp
import numpy as np
from jax import lax

D = 1536
HEADS = 12
KV_HEADS = 2
HEAD_DIM = 128
WINDOW = 512
BLOCK = 128
TOK_DEV = 256
GROUPS = 8
SEQ = 8192
KV_COLS = 512
DOCS = 8
MOST = 1536


def draw_tokens(key, part):
    base = jax.random.fold_in(key, 11)
    first = jax.random.fold_in(base, 0)
    fifth = jax.random.fold_in(base, 4)
    values = jnp.clip(jax.random.normal(first, (GROUPS, SEQ, D), jnp.float32), -6.0, 6.0)
    block_count = SEQ // TOK_DEV
    pairing = jax.random.permutation(fifth, block_count)
    row_block = jnp.arange(SEQ, dtype=jnp.int32) // TOK_DEV
    col_block = jnp.arange(D, dtype=jnp.int32) // (D // block_count)
    spiked = pairing[row_block][:, None] == col_block[None, :]
    values = values * jnp.where(spiked, 3.0, 1.0)[None]
    return values.astype(jnp.bfloat16)


def weight_pair(key):
    first, second, third = jax.random.split(key, 3)
    kv_width = KV_HEADS * HEAD_DIM
    query_w = jnp.clip(jax.random.normal(first, (D, D), jnp.float32), -4.0, 4.0) / math.sqrt(D)
    value_w = jnp.clip(jax.random.normal(second, (D, kv_width), jnp.float32), -4.0, 4.0) / math.sqrt(D)
    key_w = jnp.clip(jax.random.normal(third, (D, kv_width), jnp.float32), -4.0, 4.0) / math.sqrt(D)
    return (query_w, jnp.concatenate([key_w, value_w], axis=1))


def draw_w_query(key, part):
    return weight_pair(jax.random.fold_in(key, 5))[0].astype(jnp.bfloat16)


def draw_w_keyval(key, part):
    return weight_pair(jax.random.fold_in(key, 5))[1].astype(jnp.bfloat16)


def levels(key, extent, pieces, smallest, high):
    def one(dim, shards_of):
        draws = jax.random.uniform(jax.random.fold_in(jax.random.fold_in(key, 6), dim), (shards_of,), jnp.float32, smallest / len(pieces), high / len(pieces))
        return jnp.repeat(jnp.exp(draws), extent[dim] // shards_of).reshape((-1,) + (1,) * (len(extent) - dim - 1))

    gain = one(*pieces[0])
    for cut in pieces[1:]:
        gain = gain * one(*cut)
    return gain


def profile(amount, total, reach, lean):
    loads = [(1 << 20) // math.isqrt(grade ** lean) + 1 for grade in range(2, amount + 1)]
    rest, holding = total - reach - (amount - 1), [1] * (amount - 1)
    while rest > 0:
        movable = [i for i in range(amount - 1) if holding[i] < reach]
        mass, left = sum([loads[i] for i in movable]), rest
        for i in movable:
            addition = min(reach - holding[i], max(1, left * loads[i] // mass), rest)
            holding[i] = holding[i] + addition
            rest = rest - addition
    return np.array([reach] + holding)


def uneven(key, number_of, total, bound, slope):
    if number_of == 2:
        one = jax.random.randint(key, (), max(1, total - bound), min(bound, total - 1) + 1)
        return jnp.stack([one, total - one])
    tallies = jnp.asarray(profile(number_of, total, bound, slope), jnp.int32)
    pairs = (number_of - 1) // 2
    source_of, sink = tallies[1:1 + 2 * pairs:2], tallies[2:2 + 2 * pairs:2]
    room = jnp.minimum(source_of - 1, bound - sink)
    moved = jax.random.randint(jax.random.fold_in(key, 1), (pairs,), 0, 1 << 20) % (room + 1)
    tallies = tallies.at[1:1 + 2 * pairs:2].set(source_of - moved).at[2:2 + 2 * pairs:2].set(sink + moved)
    return tallies[jax.random.permutation(jax.random.fold_in(key, 2), number_of)]


def gaussian(own_key, dims, width, limit, pieces=(), kind=jnp.bfloat16):
    drawn = width * jax.random.normal(own_key, dims, jnp.float32)
    if pieces:
        drawn = drawn * levels(own_key, dims, pieces, -0.22, 0.18)
    return jnp.clip(drawn, -limit, limit).astype(kind)


def setup_inputs(seed: int = 0) -> dict:
    arg_keys = jax.random.split(jax.random.key(seed), 6)
    tokens = draw_tokens(jax.random.fold_in(arg_keys[5], 71), 0)
    segments = jax.vmap(lambda own: jnp.searchsorted(jnp.cumsum(uneven(own, DOCS, SEQ, MOST, 1)), jnp.arange(SEQ), side="right"))(jax.random.split(arg_keys[1], GROUPS)).reshape((GROUPS, SEQ)).astype(jnp.int32)
    w_query = draw_w_query(jax.random.fold_in(arg_keys[5], 71), 0)
    w_keyval = draw_w_keyval(jax.random.fold_in(arg_keys[5], 71), 0)
    grad_context = gaussian(arg_keys[4], (GROUPS, SEQ, D), 1.0, 6.0, ((0, 8), (1, 32)))
    return dict(tokens=tokens, segments=segments, w_query=w_query, w_keyval=w_keyval, grad_context=grad_context)


def reference(tokens, segments, w_query, w_keyval, grad_context):
    halo_rows = WINDOW - BLOCK
    group_size = HEADS // KV_HEADS
    kv_width = KV_HEADS * HEAD_DIM
    score_scale = HEAD_DIM ** -0.5
    block_count = SEQ // BLOCK

    def per_group(weight_sum, items):
        hidden_in, doc_ids, grad_out = items
        queries = jnp.dot(hidden_in, w_query, preferred_element_type=jnp.float32).astype(jnp.bfloat16)
        keyval = jnp.dot(hidden_in, w_keyval, preferred_element_type=jnp.float32).astype(jnp.bfloat16)
        padded_kv = jnp.concatenate([jnp.zeros((halo_rows, KV_COLS), jnp.bfloat16), keyval], axis=0)
        padded_ids = jnp.concatenate([jnp.full((halo_rows,), -1, jnp.int32), doc_ids.astype(jnp.int32)], axis=0)

        def per_block(kv_grads, block_id):
            start = (block_id * BLOCK).astype(jnp.int32)
            query_blk = lax.dynamic_slice_in_dim(queries, start, BLOCK, 0).reshape(BLOCK, KV_HEADS, group_size, HEAD_DIM).astype(jnp.float32)
            out_blk = lax.dynamic_slice_in_dim(grad_out, start, BLOCK, 0).reshape(BLOCK, KV_HEADS, group_size, HEAD_DIM).astype(jnp.float32)
            kv_blk = lax.dynamic_slice_in_dim(padded_kv, start, WINDOW, 0)
            key_heads = kv_blk[:, :kv_width].reshape(WINDOW, KV_HEADS, HEAD_DIM).astype(jnp.float32)
            val_heads = kv_blk[:, kv_width:].reshape(WINDOW, KV_HEADS, HEAD_DIM).astype(jnp.float32)
            query_pos = start + jnp.arange(BLOCK, dtype=jnp.int32)
            key_pos = start - halo_rows + jnp.arange(WINDOW, dtype=jnp.int32)
            key_ids = lax.dynamic_slice_in_dim(padded_ids, start, WINDOW, 0)
            query_ids = lax.dynamic_slice_in_dim(doc_ids.astype(jnp.int32), start, BLOCK, 0)
            allowed = (key_pos[None, :] <= query_pos[:, None]) & (key_ids[None, :] == query_ids[:, None])
            scores = jnp.einsum("tgha,kga->ghtk", query_blk, key_heads) * score_scale
            masked = jnp.where(allowed[None, None], scores, -1e30)
            row_max = jnp.max(masked, axis=-1, keepdims=True)
            expo = jnp.exp(masked - row_max)
            attn_probs = expo / jnp.sum(expo, axis=-1, keepdims=True)
            probs_low = attn_probs.astype(jnp.bfloat16).astype(jnp.float32)
            ctx_heads = jnp.einsum("ghtk,kga->tgha", probs_low, val_heads).astype(jnp.bfloat16)
            row_delta = jnp.einsum("tgha,tgha->ght", out_blk, ctx_heads.astype(jnp.float32))
            grad_probs = jnp.einsum("tgha,kga->ghtk", out_blk, val_heads)
            grad_scores = (attn_probs * (grad_probs - row_delta[..., None]) * score_scale).astype(jnp.bfloat16).astype(jnp.float32)
            grad_q = jnp.einsum("ghtk,kga->tgha", grad_scores, key_heads).astype(jnp.bfloat16)
            grad_key = jnp.einsum("ghtk,tgha->kga", grad_scores, query_blk).reshape(WINDOW, kv_width)
            grad_val = jnp.einsum("ghtk,tgha->kga", probs_low, out_blk).reshape(WINDOW, kv_width)
            grad_kv = jnp.concatenate([grad_key, grad_val], axis=1)
            updated = lax.dynamic_slice_in_dim(kv_grads, start, WINDOW, 0) + grad_kv
            kv_grads = lax.dynamic_update_slice_in_dim(kv_grads, updated, start, 0)
            return kv_grads, (ctx_heads.reshape(BLOCK, D), grad_q.reshape(BLOCK, D))

        start_grads = jnp.zeros((halo_rows + SEQ, KV_COLS), jnp.float32)
        kv_grads, (ctx_blocks, grad_q_blocks) = lax.scan(per_block, start_grads, jnp.arange(block_count, dtype=jnp.int32))
        context = ctx_blocks.reshape(SEQ, D)
        grad_queries = grad_q_blocks.reshape(SEQ, D)
        grad_keyval = kv_grads[halo_rows:].astype(jnp.bfloat16)
        grad_in = jnp.dot(grad_queries, w_query.T, preferred_element_type=jnp.float32)
        grad_in = grad_in + jnp.dot(grad_keyval, w_keyval.T, preferred_element_type=jnp.float32)
        combined = jnp.concatenate([grad_queries, grad_keyval], axis=1)
        weight_sum = weight_sum + jnp.dot(hidden_in.T, combined, preferred_element_type=jnp.float32)
        return weight_sum, (context, grad_in.astype(jnp.bfloat16))

    start_sum = jnp.zeros((D, D + KV_COLS), jnp.float32)
    weight_sum, (contexts, grads_in) = lax.scan(per_group, start_sum, (tokens, segments, grad_context))
    weight_low = weight_sum.astype(jnp.bfloat16)
    return contexts, grads_in, weight_low[:, :D], weight_low[:, D:]
```

```python
import functools

import jax
import jax.numpy as jnp
from jax import lax
from jax.experimental import pallas as pl
from jax.experimental.pallas import tpu as pltpu
from jax.sharding import Mesh
from jax.sharding import PartitionSpec as P

HEAD_DIM = 128
GROUP = 6
KV_HEADS = 2
WINDOW = 512
BLOCK = 128
HALO = WINDOW - BLOCK
OWN = 256
PAIR = 2 * OWN
KEYS = HALO + PAIR
QCOLS = GROUP * HEAD_DIM
KVCOLS = 2 * HEAD_DIM
D = 1536
SCALE = HEAD_DIM ** (-0.5)
F32 = jnp.float32
BF16 = jnp.bfloat16
NT = (((1,), (1,)), ((), ()))
TN = (((0,), (0,)), ((), ()))
SUBS = 8
BIG = 48 * 1024 * 1024


def whole(shape):
    return pl.BlockSpec(shape, lambda *_: (0,) * len(shape))


def params():
    return pltpu.CompilerParams(vmem_limit_bytes=BIG)


def cost(flops, moved, trans=0):
    return pl.CostEstimate(flops=flops, bytes_accessed=moved, transcendentals=trans)


def nn(a, b):
    return jnp.dot(a, b, preferred_element_type=F32)


def nt(a, b):
    return lax.dot_general(a, b, NT, preferred_element_type=F32)


def tn(a, b):
    return lax.dot_general(a, b, TN, preferred_element_type=F32)


def project_own_body(core, x, wq, wk, wv, q, kv):
    xv = x[...]
    kv[...] = nn(xv, jnp.concatenate([wk[...], wv[...]], axis=1)).astype(BF16)
    q[...] = nn(xv, wq[...]).astype(BF16)


def project_own(core, x, w_query, w_keyval):
    return pl.pallas_call(
        project_own_body,
        grid_spec=pltpu.PrefetchScalarGridSpec(
            num_scalar_prefetch=1,
            grid=(1,),
            in_specs=[
                whole((OWN, D)),
                pl.BlockSpec((D, QCOLS), lambda i, c: (0, c[0])),
                pl.BlockSpec((D, HEAD_DIM), lambda i, c: (0, c[0])),
                pl.BlockSpec((D, HEAD_DIM), lambda i, c: (0, KV_HEADS + c[0])),
            ],
            out_specs=[whole((OWN, QCOLS)), whole((OWN, KVCOLS))],
        ),
        out_shape=[
            jax.ShapeDtypeStruct((OWN, QCOLS), BF16),
            jax.ShapeDtypeStruct((OWN, KVCOLS), BF16),
        ],
        compiler_params=params(),
        cost_estimate=cost(2 * OWN * D * 1024, 4 << 20),
        name="project_own",
    )(core, x, w_query, w_keyval, w_keyval)


def project_kv_body(core, x, kv_own, wk, wv, kv, sent):
    c = core[0]
    other = nn(x[...], jnp.concatenate([wk[...], wv[...]], axis=1)).astype(BF16)
    own = kv_own[...]
    low = jnp.where(c == 0, own, other)
    high = jnp.where(c == 0, other, own)
    kv[:OWN] = low
    kv[OWN:] = high
    sent[: HALO - OWN] = low[PAIR - HALO :]
    sent[HALO - OWN :] = high


def project_kv(core, x, kv_own, w_keyval):
    return pl.pallas_call(
        project_kv_body,
        grid_spec=pltpu.PrefetchScalarGridSpec(
            num_scalar_prefetch=1,
            grid=(1,),
            in_specs=[
                whole((OWN, D)),
                whole((OWN, KVCOLS)),
                pl.BlockSpec((D, HEAD_DIM), lambda i, c: (0, c[0])),
                pl.BlockSpec((D, HEAD_DIM), lambda i, c: (0, KV_HEADS + c[0])),
            ],
            out_specs=[whole((PAIR, KVCOLS)), whole((HALO, KVCOLS))],
        ),
        out_shape=[
            jax.ShapeDtypeStruct((PAIR, KVCOLS), BF16),
            jax.ShapeDtypeStruct((HALO, KVCOLS), BF16),
        ],
        compiler_params=params(),
        cost_estimate=cost(2 * OWN * D * KVCOLS, 2 << 20),
        name="project_kv",
    )(core, x, kv_own, w_keyval, w_keyval)


def project_q_body(core, x, wq, q):
    q[...] = nn(x[...], wq[...]).astype(BF16)


def project_q(core, x, w_query):
    return pl.pallas_call(
        project_q_body,
        grid_spec=pltpu.PrefetchScalarGridSpec(
            num_scalar_prefetch=1,
            grid=(1,),
            in_specs=[whole((OWN, D)), pl.BlockSpec((D, QCOLS), lambda i, c: (0, c[0]))],
            out_specs=whole((OWN, QCOLS)),
        ),
        out_shape=jax.ShapeDtypeStruct((OWN, QCOLS), BF16),
        compiler_params=params(),
        cost_estimate=cost(2 * OWN * D * QCOLS, 4 << 20),
        name="project_q",
    )(core, x, w_query)


def attend_body(
    place,
    q_own,
    q_oth,
    do_own,
    do_oth,
    kv,
    halo,
    segs,
    ctx_out,
    dq_out,
    dkv_out,
    sent_out,
    keys,
    vals_t,
    keys_t,
    ids,
    dkv,
):
    c = place[0]
    chip = place[1]
    b = pl.program_id(0)
    blocks = PAIR // BLOCK

    @pl.when(b == 0)
    def _():
        keys[:HALO] = halo[...]
        keys[HALO:] = kv[...]
        dkv[...] = jnp.zeros_like(dkv)
        for t in range(KEYS // BLOCK):
            rows = slice(t * BLOCK, (t + 1) * BLOCK)
            tile = keys[rows, :].astype(F32)
            keys_t[:, rows] = tile[:, :HEAD_DIM].T.astype(BF16)
            vals_t[:, rows] = tile[:, HEAD_DIM:].T.astype(BF16)
            row = chip * blocks - HALO // BLOCK + t
            line = segs[pl.ds(jnp.maximum(row, 0), 1), :]
            line = jnp.where(row >= 0, line, -1)
            ids[rows, :] = jnp.broadcast_to(line, (BLOCK, BLOCK)).T

    half = b // 2
    own = half == c
    inner = pl.multiple_of((b % 2) * BLOCK, BLOCK)
    here = pl.ds(inner, BLOCK)
    q_blk = jnp.where(own, q_own[here, :], q_oth[here, :])
    do_blk = jnp.where(own, do_own[here, :], do_oth[here, :])
    first = pl.multiple_of(b * BLOCK, BLOCK)
    win = pl.ds(first, WINDOW)
    k_win = keys[win, :HEAD_DIM]
    v_win = keys[win, HEAD_DIM:]
    kt_win = keys_t[:, win]
    vt_win = vals_t[:, win]
    query_ids = segs[pl.ds(chip * blocks + b, 1), :]
    j_pos = lax.broadcasted_iota(jnp.int32, (WINDOW, BLOCK), 0)
    i_pos = lax.broadcasted_iota(jnp.int32, (WINDOW, BLOCK), 1)
    seen = (ids[win, :] == query_ids) & (j_pos <= i_pos + HALO)
    seen2 = jnp.concatenate([seen, seen], axis=1)
    dk = jnp.zeros((WINDOW, HEAD_DIM), F32)
    dv = jnp.zeros((WINDOW, HEAD_DIM), F32)
    ctx_parts = []
    dq_parts = []
    for pair in range(GROUP // 2):
        h0 = slice(2 * pair * HEAD_DIM, (2 * pair + 1) * HEAD_DIM)
        h1 = slice((2 * pair + 1) * HEAD_DIM, (2 * pair + 2) * HEAD_DIM)
        q2 = jnp.concatenate([q_blk[:, h0], q_blk[:, h1]], axis=0)
        do2 = jnp.concatenate([do_blk[:, h0], do_blk[:, h1]], axis=0)
        scores = jnp.where(seen2, nt(k_win, q2) * SCALE, -1e30)
        top = jnp.max(scores, axis=0, keepdims=True)
        expo = jnp.exp(scores - top)
        probs = expo * (1.0 / jnp.sum(expo, axis=0, keepdims=True))
        probs_low = probs.astype(BF16)
        ctx_t = nn(vt_win, probs_low).astype(BF16).astype(F32)
        delta = jnp.sum(do2.astype(F32).T * ctx_t, axis=0, keepdims=True)
        dp = nt(v_win, do2)
        ds = (probs * (dp - delta) * SCALE).astype(BF16)
        dv = dv + nn(probs_low, do2)
        dk = dk + nn(ds, q2)
        dq2 = nn(kt_win, ds).T
        ctx2 = ctx_t.T
        ctx_parts += [ctx2[:BLOCK], ctx2[BLOCK:]]
        dq_parts += [dq2[:BLOCK], dq2[BLOCK:]]
    to = pl.ds(pl.multiple_of(jnp.where(own, 0, OWN) + inner, BLOCK), BLOCK)
    ctx_out[to, :] = jnp.concatenate(ctx_parts, axis=1).astype(BF16)
    dq_out[to, :] = jnp.concatenate(dq_parts, axis=1).astype(BF16)
    dkv[win, :] += jnp.concatenate([dk, dv], axis=1)

    @pl.when(b == blocks - 1)
    def _():
        sent_out[...] = dkv[:HALO, :].astype(BF16)
        dkv_out[...] = dkv[HALO:, :]


def attend(place, q_own, q_oth, do_own, do_oth, kv, halo, segs):
    return pl.pallas_call(
        attend_body,
        grid_spec=pltpu.PrefetchScalarGridSpec(
            num_scalar_prefetch=1,
            grid=(PAIR // BLOCK,),
            in_specs=[
                whole((OWN, QCOLS)),
                whole((OWN, QCOLS)),
                pl.BlockSpec((OWN, QCOLS), lambda i, p: (0, p[0])),
                whole((OWN, QCOLS)),
                whole((PAIR, KVCOLS)),
                whole((HALO, KVCOLS)),
                whole(segs.shape),
            ],
            out_specs=[
                whole((PAIR, QCOLS)),
                whole((PAIR, QCOLS)),
                whole((PAIR, KVCOLS)),
                whole((HALO, KVCOLS)),
            ],
            scratch_shapes=[
                pltpu.VMEM((KEYS, KVCOLS), BF16),
                pltpu.VMEM((HEAD_DIM, KEYS), BF16),
                pltpu.VMEM((HEAD_DIM, KEYS), BF16),
                pltpu.VMEM((KEYS, BLOCK), jnp.int32),
                pltpu.VMEM((KEYS, KVCOLS), F32),
            ],
        ),
        out_shape=[
            jax.ShapeDtypeStruct((PAIR, QCOLS), BF16),
            jax.ShapeDtypeStruct((PAIR, QCOLS), BF16),
            jax.ShapeDtypeStruct((PAIR, KVCOLS), F32),
            jax.ShapeDtypeStruct((HALO, KVCOLS), BF16),
        ],
        compiler_params=params(),
        cost_estimate=cost(2 * PAIR * WINDOW * QCOLS * 6, 4 << 20, PAIR * WINDOW * GROUP),
        name="attend",
    )(place, q_own, q_oth, do_own, do_oth, kv, halo, segs)


def spread(value, out, zs):
    rows = D // (2 * zs)
    low = value.astype(BF16)
    for s in range(2):
        for z in range(zs):
            for y in range(2):
                start = (z * 2 + y) * rows
                out[s * 2 + y, z * rows : (z + 1) * rows, :] = low[
                    start : start + rows, s * HEAD_DIM : (s + 1) * HEAD_DIM
                ]


def weight_q_body(x_own, x_oth, g, out):
    spread(tn(x_own[...], g[:OWN]) + tn(x_oth[...], g[OWN:]), out, 8)


def weight_q(x_own, x_oth, dq):
    return pl.pallas_call(
        weight_q_body,
        grid=(3,),
        in_specs=[
            whole((OWN, D)),
            whole((OWN, D)),
            pl.BlockSpec((PAIR, 256), lambda i: (0, i)),
        ],
        out_specs=pl.BlockSpec((4, D // 2, HEAD_DIM), lambda i: (i, 0, 0)),
        out_shape=jax.ShapeDtypeStruct((16, D // 2, HEAD_DIM), BF16),
        compiler_params=params(),
        cost_estimate=cost(2 * PAIR * D * QCOLS, 4 << 20),
        name="weight_q",
    )(x_own, x_oth, dq)


def weight_kv_body(place, x_own, x_oth, dkv, arrived, before, out, g_out):
    c = place[0]
    low = dkv[:OWN]
    skip = PAIR - HALO
    low = jnp.concatenate([low[:skip], low[skip:] + arrived[: OWN - skip].astype(F32)], axis=0)
    high = dkv[OWN:] + arrived[OWN - skip :].astype(F32)
    low = low.astype(BF16)
    high = high.astype(BF16)
    own = jnp.where(c == 0, low, high)
    oth = jnp.where(c == 0, high, low)
    g_out[:OWN] = own
    g_out[OWN:] = oth
    spread(tn(x_own[...], own) + tn(x_oth[...], oth), out, 8)


def weight_kv(place, x_own, x_oth, dkv, arrived, before):
    return pl.pallas_call(
        weight_kv_body,
        grid_spec=pltpu.PrefetchScalarGridSpec(
            num_scalar_prefetch=1,
            grid=(1,),
            in_specs=[
                whole((OWN, D)),
                whole((OWN, D)),
                whole((PAIR, KVCOLS)),
                whole((HALO, KVCOLS)),
                pl.BlockSpec(memory_space=pl.ANY),
            ],
            out_specs=[
                pl.BlockSpec((4, D // 2, HEAD_DIM), lambda i, p: (3, 0, 0)),
                whole((PAIR, KVCOLS)),
            ],
        ),
        out_shape=[
            jax.ShapeDtypeStruct((16, D // 2, HEAD_DIM), BF16),
            jax.ShapeDtypeStruct((PAIR, KVCOLS), BF16),
        ],
        input_output_aliases={5: 0},
        compiler_params=params(),
        cost_estimate=cost(2 * PAIR * D * KVCOLS, 3 << 20),
        name="weight_kv",
    )(place, x_own, x_oth, dkv, arrived, before)


def ordered(first, own, oth):
    return jnp.where(
        first, jnp.concatenate([own, oth], axis=1), jnp.concatenate([oth, own], axis=1)
    )


def grad_tokens_body(place, dq, dkv, ctx, dq_in, dkv_in, ctx_in, wq, wkv, out, ctx_out):
    first = place[0] == 0
    dq_full = ordered(first, dq[...], dq_in[...])
    kv = dkv[...]
    kv_in = dkv_in[...]
    keys = ordered(first, kv[:, :HEAD_DIM], kv_in[:, :HEAD_DIM])
    vals = ordered(first, kv[:, HEAD_DIM:], kv_in[:, HEAD_DIM:])
    kv_full = jnp.concatenate([keys, vals], axis=1)
    out[...] = (nt(dq_full, wq[...]) + nt(kv_full, wkv[...])).astype(BF16)

    @pl.when(pl.program_id(0) == 0)
    def _():
        ctx_out[...] = ordered(first, ctx[...], ctx_in[...])


def grad_tokens(place, dq, dkv, ctx, dq_in, dkv_in, ctx_in, w_query, w_keyval):
    step = 512
    return pl.pallas_call(
        grad_tokens_body,
        grid_spec=pltpu.PrefetchScalarGridSpec(
            num_scalar_prefetch=1,
            grid=(D // step,),
            in_specs=[
                whole((OWN, QCOLS)),
                whole((OWN, KVCOLS)),
                whole((OWN, QCOLS)),
                whole((OWN, QCOLS)),
                whole((OWN, KVCOLS)),
                whole((OWN, QCOLS)),
                pl.BlockSpec((step, D), lambda i, p: (i, 0)),
                pl.BlockSpec((step, 512), lambda i, p: (i, 0)),
            ],
            out_specs=[
                pl.BlockSpec((OWN, step), lambda i, p: (0, i)),
                whole((OWN, D)),
            ],
        ),
        out_shape=[
            jax.ShapeDtypeStruct((OWN, D), BF16),
            jax.ShapeDtypeStruct((OWN, D), BF16),
        ],
        compiler_params=params(),
        cost_estimate=cost(2 * OWN * D * 2048, 8 << 20),
        name="grad_tokens",
    )(place, dq, dkv, ctx, dq_in, dkv_in, ctx_in, w_query, w_keyval)


def swap(value):
    return lax.ppermute(value, "c", [(0, 1), (1, 0)])


def shards(tokens, segments, w_query, w_keyval, grad_context):
    x_own = tokens[0]
    core = lax.axis_index("c")
    chip = lax.axis_index(("z", "yl"))
    place = jnp.stack([core, chip]).astype(jnp.int32)
    away = lax.dynamic_slice_in_dim(grad_context[0], (1 - core) * QCOLS, QCOLS, 1)
    x_oth = swap(x_own)
    do_oth = swap(away)
    count = 32
    ring = ("z", "yl", "c")
    q_own, kv_own = project_own(place, x_own, w_query, w_keyval)
    kv, kv_sent = project_kv(place, x_oth, kv_own, w_keyval)
    halo = lax.ppermute(kv_sent, ring, [(i, i + 2) for i in range(count - 2)])
    q_oth = project_q(place, x_oth, w_query)
    segs = segments.reshape(-1, BLOCK)
    ctx, dq, dkv, dkv_sent = attend(
        place, q_own, q_oth, grad_context[0], do_oth, kv, halo, segs
    )
    arrived = lax.ppermute(dkv_sent, ring, [(i + 2, i) for i in range(count - 2)])
    ctx_in = swap(ctx[OWN:])
    dq_in = swap(dq[OWN:])
    partial = weight_q(x_own, x_oth, dq)
    partial, dkv_low = weight_kv(place, x_own, x_oth, dkv, arrived, partial)
    dkv_in = swap(dkv_low[OWN:])
    grad_in, context = grad_tokens(
        place, dq[:OWN], dkv_low[:OWN], ctx[:OWN], dq_in, dkv_in, ctx_in, w_query, w_keyval
    )
    pieces = lax.all_to_all(partial, ("x", "yh", "yl"), 0, 0)
    plane = jnp.sum(pieces.astype(F32), axis=0).astype(BF16)
    columns = lax.all_to_all(plane.reshape(8, 96, HEAD_DIM), "z", 0, 0)
    mine = jnp.sum(columns.astype(F32), axis=0).astype(BF16).reshape(1, 2, 48, HEAD_DIM)
    copies = jnp.broadcast_to(mine, (SUBS, 2, 48, HEAD_DIM)).reshape(16, 48, HEAD_DIM)
    final = lax.all_to_all(copies, ("x", "yh", "c"), 0, 0).reshape(SUBS, 2, 48, HEAD_DIM)
    query_w = final[:GROUP].transpose(2, 1, 0, 3).reshape(48, D)
    keyval_w = final[GROUP:].transpose(2, 0, 1, 3).reshape(48, 512)
    return context[None], grad_in[None], query_w, keyval_w


def solution(mesh):
    fine = Mesh(mesh.devices.reshape(4, 2, 8, 2, 2), ("x", "yh", "z", "yl", "c"))
    dp = ("x", "yh")
    ctx = ("z", "yl", "c")
    return jax.shard_map(
        shards,
        mesh=fine,
        in_specs=(P(dp, ctx, None), P(dp, None), P(), P(), P(dp, ctx, None)),
        out_specs=(P(dp, ctx, None), P(dp, ctx, None), P(ctx, None), P(ctx, None)),
        check_vma=False,
    )
```

```python
import functools

import jax
import jax.numpy as jnp
from jax import lax
from jax.experimental import pallas as pl
from jax.experimental.pallas import tpu as pltpu
from jax.sharding import Mesh
from jax.sharding import PartitionSpec as P

HEAD_DIM = 128
GROUP = 6
KV_HEADS = 2
WINDOW = 512
BLOCK = 128
HALO = WINDOW - BLOCK
OWN = 256
PAIR = 2 * OWN
KEYS = HALO + PAIR
QCOLS = GROUP * HEAD_DIM
KVCOLS = 2 * HEAD_DIM
D = 1536
SCALE = HEAD_DIM ** (-0.5)
F32 = jnp.float32
BF16 = jnp.bfloat16
NT = (((1,), (1,)), ((), ()))
TN = (((0,), (0,)), ((), ()))
WIDE = 512
REST = 256
SLAB = 24
BIG = 60 * 1024 * 1024
MID = 12 * 1024 * 1024


def whole(shape):
    return pl.BlockSpec(shape, lambda *_: (0,) * len(shape))


def params(limit=BIG):
    return pltpu.CompilerParams(vmem_limit_bytes=limit)


def cost(flops, moved, trans=0):
    return pl.CostEstimate(flops=flops, bytes_accessed=moved, transcendentals=trans)


def nn(a, b):
    return jnp.dot(a, b, preferred_element_type=F32)


def nt(a, b):
    return lax.dot_general(a, b, NT, preferred_element_type=F32)


def tn(a, b):
    return lax.dot_general(a, b, TN, preferred_element_type=F32)


def project_own_body(core, x, wq, wk, wv, q, kv):
    xv = x[...]
    q[...] = nn(xv, wq[...]).astype(BF16)

    @pl.when(pl.program_id(0) == 0)
    def _():
        kv[...] = nn(xv, jnp.concatenate([wk[...], wv[...]], axis=1)).astype(BF16)


def project_own(core, x, w_query, w_keyval):
    return pl.pallas_call(
        project_own_body,
        grid_spec=pltpu.PrefetchScalarGridSpec(
            num_scalar_prefetch=1,
            grid=(3,),
            in_specs=[
                whole((OWN, D)),
                pl.BlockSpec((D, 256), lambda i, c: (0, 3 * c[0] + i)),
                pl.BlockSpec((D, HEAD_DIM), lambda i, c: (0, c[0])),
                pl.BlockSpec((D, HEAD_DIM), lambda i, c: (0, KV_HEADS + c[0])),
            ],
            out_specs=[pl.BlockSpec((OWN, 256), lambda i, c: (0, i)), whole((OWN, KVCOLS))],
        ),
        out_shape=[
            jax.ShapeDtypeStruct((OWN, QCOLS), BF16),
            jax.ShapeDtypeStruct((OWN, KVCOLS), BF16),
        ],
        compiler_params=params(),
        cost_estimate=cost(2 * OWN * D * 1024, 4 << 20),
        name="project_own",
    )(core, x, w_query, w_keyval, w_keyval)


def project_kv_body(core, x, kv_own, wk, wv, kv, sent):
    c = core[0]
    other = nn(x[...], jnp.concatenate([wk[...], wv[...]], axis=1)).astype(BF16)
    own = kv_own[...]
    low = jnp.where(c == 0, own, other)
    high = jnp.where(c == 0, other, own)
    kv[:OWN] = low
    kv[OWN:] = high
    sent[: HALO - OWN] = low[PAIR - HALO :]
    sent[HALO - OWN :] = high


def project_kv(core, x, kv_own, w_keyval):
    return pl.pallas_call(
        project_kv_body,
        grid_spec=pltpu.PrefetchScalarGridSpec(
            num_scalar_prefetch=1,
            grid=(1,),
            in_specs=[
                whole((OWN, D)),
                whole((OWN, KVCOLS)),
                pl.BlockSpec((D, HEAD_DIM), lambda i, c: (0, c[0])),
                pl.BlockSpec((D, HEAD_DIM), lambda i, c: (0, KV_HEADS + c[0])),
            ],
            out_specs=[whole((PAIR, KVCOLS)), whole((HALO, KVCOLS))],
        ),
        out_shape=[
            jax.ShapeDtypeStruct((PAIR, KVCOLS), BF16),
            jax.ShapeDtypeStruct((HALO, KVCOLS), BF16),
        ],
        compiler_params=params(),
        cost_estimate=cost(2 * OWN * D * KVCOLS, 2 << 20),
        name="project_kv",
    )(core, x, kv_own, w_keyval, w_keyval)


def project_q_body(core, x, wq, q):
    q[...] = nn(x[...], wq[...]).astype(BF16)


def project_q(core, x, w_query):
    return pl.pallas_call(
        project_q_body,
        grid_spec=pltpu.PrefetchScalarGridSpec(
            num_scalar_prefetch=1,
            grid=(3,),
            in_specs=[whole((OWN, D)), pl.BlockSpec((D, 256), lambda i, c: (0, 3 * c[0] + i))],
            out_specs=pl.BlockSpec((OWN, 256), lambda i, c: (0, i)),
        ),
        out_shape=jax.ShapeDtypeStruct((OWN, QCOLS), BF16),
        compiler_params=params(),
        cost_estimate=cost(2 * OWN * D * QCOLS, 4 << 20),
        name="project_q",
    )(core, x, w_query)


def attend_body(
    start,
    width,
    more,
    place,
    q_own,
    q_oth,
    do_own,
    do_oth,
    kv,
    halo,
    segs,
    *rest,
):
    if more:
        dkv_in, mix_own, mix_oth, dkv_out, sent_out, keys, vals_t, keys_t, bias, dkv = rest
    else:
        mix_own, mix_oth, dkv_out, keys, vals_t, keys_t, bias, dkv = rest
    c = place[0]
    chip = place[1]
    b = pl.program_id(0)
    blocks = PAIR // BLOCK

    @pl.when(b == 0)
    def _():
        keys[:HALO] = halo[...]
        keys[HALO:] = kv[...]
        if more:
            dkv[...] = dkv_in[...]
        else:
            dkv[...] = jnp.zeros_like(dkv)
        for t in range(KEYS // BLOCK):
            rows = slice(t * BLOCK, (t + 1) * BLOCK)
            tile = keys[rows, :].astype(F32)
            keys_t[:, rows] = tile[:, :HEAD_DIM].T.astype(BF16)
            vals_t[:, rows] = tile[:, HEAD_DIM:].T.astype(BF16)
            row = chip * blocks - HALO // BLOCK + t
            line = segs[pl.ds(jnp.maximum(row, 0), 1), :]
            line = jnp.where(row >= 0, line, -1)
            bias[rows, :] = jnp.broadcast_to(line, (BLOCK, BLOCK)).T

    half = b // 2
    own = half == c
    inner = pl.multiple_of((b % 2) * BLOCK, BLOCK)
    here = pl.ds(inner, BLOCK)
    q_blk = jnp.where(own, q_own[here, :], q_oth[here, :])
    do_cols = slice(start, start + width)
    do_blk = jnp.where(own, do_own[here, do_cols], do_oth[here, do_cols])
    first = pl.multiple_of(b * BLOCK, BLOCK)
    win = pl.ds(first, WINDOW)
    k_win = keys[win, :HEAD_DIM]
    v_win = keys[win, HEAD_DIM:]
    kt_win = keys_t[:, win]
    vt_win = vals_t[:, win]
    query_ids = segs[pl.ds(chip * blocks + b, 1), :]
    j_pos = lax.broadcasted_iota(jnp.int32, (WINDOW, BLOCK), 0)
    i_pos = lax.broadcasted_iota(jnp.int32, (WINDOW, BLOCK), 1)
    seen = (bias[win, :] == query_ids) & (j_pos <= i_pos + HALO)
    seen2 = jnp.concatenate([seen, seen], axis=1)
    dk = jnp.zeros((WINDOW, HEAD_DIM), F32)
    dv = jnp.zeros((WINDOW, HEAD_DIM), F32)
    ctx_parts = []
    dq_parts = []
    for pair in range(width // 256):
        h0 = slice(2 * pair * HEAD_DIM, (2 * pair + 1) * HEAD_DIM)
        h1 = slice((2 * pair + 1) * HEAD_DIM, (2 * pair + 2) * HEAD_DIM)
        q2 = jnp.concatenate([q_blk[:, h0], q_blk[:, h1]], axis=0)
        do2 = jnp.concatenate([do_blk[:, h0], do_blk[:, h1]], axis=0)
        scores = jnp.where(seen2, nt(k_win, q2) * SCALE, -1e30)
        top = jnp.max(scores, axis=0, keepdims=True)
        expo = jnp.exp(scores - top)
        probs = expo * (1.0 / jnp.sum(expo, axis=0, keepdims=True))
        probs_low = probs.astype(BF16)
        ctx_t = nn(vt_win, probs_low).astype(BF16).astype(F32)
        delta = jnp.sum(do2.astype(F32).T * ctx_t, axis=0, keepdims=True)
        dp = nt(v_win, do2)
        ds = (probs * (dp - delta) * SCALE).astype(BF16)
        dv = dv + nn(probs_low, do2)
        dk = dk + nn(ds, q2)
        dq2 = nn(kt_win, ds).T
        ctx2 = ctx_t.T
        ctx_parts += [ctx2[:BLOCK], ctx2[BLOCK:]]
        dq_parts += [dq2[:BLOCK], dq2[BLOCK:]]
    mix = jnp.concatenate(ctx_parts + dq_parts, axis=1).astype(BF16)

    @pl.when(own)
    def _():
        mix_own[here, :] = mix

    @pl.when(jnp.logical_not(own))
    def _():
        mix_oth[here, :] = mix

    dkv[win, :] += jnp.concatenate([dk, dv], axis=1)

    @pl.when(b == blocks - 1)
    def _():
        if more:
            sent_out[...] = dkv[:HALO, :].astype(BF16)
            dkv_out[...] = dkv[HALO:, :]
        else:
            dkv_out[...] = dkv[...]


def attend(place, q_own, q_oth, do_own, do_oth, kv, halo, segs, dkv=None):
    more = dkv is not None
    start, width = (WIDE, REST) if more else (0, WIDE)
    mix = jax.ShapeDtypeStruct((OWN, 2 * width), BF16)
    outs = [mix, mix, jax.ShapeDtypeStruct((PAIR if more else KEYS, KVCOLS), F32)]
    if more:
        outs.append(jax.ShapeDtypeStruct((HALO, KVCOLS), BF16))
    extra = [dkv] if more else []
    return pl.pallas_call(
        functools.partial(attend_body, start, width, more),
        grid_spec=pltpu.PrefetchScalarGridSpec(
            num_scalar_prefetch=1,
            grid=(PAIR // BLOCK,),
            in_specs=[
                pl.BlockSpec((OWN, width), lambda i, p: (0, start // width)),
                pl.BlockSpec((OWN, width), lambda i, p: (0, start // width)),
                pl.BlockSpec((OWN, QCOLS), lambda i, p: (0, p[0])),
                pl.BlockSpec((OWN, QCOLS), lambda i, p: (0, p[0])),
                whole((PAIR, KVCOLS)),
                whole((HALO, KVCOLS)),
                whole(segs.shape),
            ]
            + [whole(v.shape) for v in extra],
            out_specs=[whole(o.shape) for o in outs],
            scratch_shapes=[
                pltpu.VMEM((KEYS, KVCOLS), BF16),
                pltpu.VMEM((HEAD_DIM, KEYS), BF16),
                pltpu.VMEM((HEAD_DIM, KEYS), BF16),
                pltpu.VMEM((KEYS, BLOCK), jnp.int32),
                pltpu.VMEM((KEYS, KVCOLS), F32),
            ],
        ),
        out_shape=outs,
        compiler_params=params(),
        cost_estimate=cost(2 * PAIR * WINDOW * width * 6, 4 << 20, PAIR * WINDOW * 6),
        name="attend_last" if more else "attend_first",
    )(place, q_own, q_oth, do_own, do_oth, kv, halo, segs, *extra)


def spread(value, out):
    for s in range(2):
        for y in range(4):
            for z in range(8):
                for core in range(2):
                    row = z * 192 + (y % 2) * 96 + core * 48 + (y // 2) * SLAB
                    piece = value[row : row + SLAB, s * HEAD_DIM : (s + 1) * HEAD_DIM]
                    out[s * 4 + y, z, core] = piece.astype(BF16)


PIECES = (16, 8, 2, SLAB, HEAD_DIM)


def weight_body(x_own, x_oth, g_own, g_oth, out):
    spread(tn(x_own[...], g_own[...]) + tn(x_oth[...], g_oth[...]), out)


def weight(x_own, x_oth, mix_own, mix_oth, first, steps):
    return pl.pallas_call(
        weight_body,
        grid=(steps,),
        in_specs=[
            whole((OWN, D)),
            whole((OWN, D)),
            pl.BlockSpec((OWN, 256), lambda i: (0, first + i)),
            pl.BlockSpec((OWN, 256), lambda i: (0, first + i)),
        ],
        out_specs=pl.BlockSpec((8,) + PIECES[1:], lambda i: (i, 0, 0, 0, 0)),
        out_shape=jax.ShapeDtypeStruct(PIECES, BF16),
        compiler_params=params(),
        cost_estimate=cost(2 * PAIR * D * 256 * steps, 4 << 20),
        name="weight_q",
    )(x_own, x_oth, mix_own, mix_oth)


def weight_kv_body(place, x_own, x_oth, dkv, arrived, before, out, own_out, oth_out):
    c = place[0]
    low = dkv[:OWN]
    skip = PAIR - HALO
    low = jnp.concatenate([low[:skip], low[skip:] + arrived[: OWN - skip].astype(F32)], axis=0)
    high = dkv[OWN:] + arrived[OWN - skip :].astype(F32)
    low = low.astype(BF16)
    high = high.astype(BF16)
    own = jnp.where(c == 0, low, high)
    oth = jnp.where(c == 0, high, low)
    own_out[...] = own
    oth_out[...] = oth
    spread(tn(x_own[...], own) + tn(x_oth[...], oth), out)


def weight_kv(place, x_own, x_oth, dkv, arrived, before):
    return pl.pallas_call(
        weight_kv_body,
        grid_spec=pltpu.PrefetchScalarGridSpec(
            num_scalar_prefetch=1,
            grid=(1,),
            in_specs=[
                whole((OWN, D)),
                whole((OWN, D)),
                whole((PAIR, KVCOLS)),
                whole((HALO, KVCOLS)),
                pl.BlockSpec(memory_space=pl.ANY),
            ],
            out_specs=[
                pl.BlockSpec((8,) + PIECES[1:], lambda i, p: (1, 0, 0, 0, 0)),
                whole((OWN, KVCOLS)),
                whole((OWN, KVCOLS)),
            ],
        ),
        out_shape=[
            jax.ShapeDtypeStruct(PIECES, BF16),
            jax.ShapeDtypeStruct((OWN, KVCOLS), BF16),
            jax.ShapeDtypeStruct((OWN, KVCOLS), BF16),
        ],
        input_output_aliases={5: 0},
        compiler_params=params(),
        cost_estimate=cost(2 * PAIR * D * KVCOLS, 3 << 20),
        name="weight_kv",
    )(place, x_own, x_oth, dkv, arrived, before)


def ordered(first, own, oth):
    return jnp.where(
        first, jnp.concatenate([own, oth], axis=1), jnp.concatenate([oth, own], axis=1)
    )


def grad_tokens_body(place, wide, slim, dkv, wide_in, slim_in, dkv_in, wq, wkv, out, ctx_out):
    first = place[0] == 0
    dq = jnp.concatenate([wide[:, WIDE:], slim[:, REST:]], axis=1)
    dq_in = jnp.concatenate([wide_in[:, WIDE:], slim_in[:, REST:]], axis=1)
    dq_full = ordered(first, dq, dq_in)
    kv = dkv[...]
    kv_in = dkv_in[...]
    keys = ordered(first, kv[:, :HEAD_DIM], kv_in[:, :HEAD_DIM])
    vals = ordered(first, kv[:, HEAD_DIM:], kv_in[:, HEAD_DIM:])
    kv_full = jnp.concatenate([keys, vals], axis=1)
    out[...] = (nt(dq_full, wq[...]) + nt(kv_full, wkv[...])).astype(BF16)

    @pl.when(pl.program_id(0) == 0)
    def _():
        ctx = jnp.concatenate([wide[:, :WIDE], slim[:, :REST]], axis=1)
        ctx_in = jnp.concatenate([wide_in[:, :WIDE], slim_in[:, :REST]], axis=1)
        ctx_out[...] = ordered(first, ctx, ctx_in)


def grad_tokens(place, wide, slim, dkv, wide_in, slim_in, dkv_in, w_query, w_keyval):
    step = 512
    return pl.pallas_call(
        grad_tokens_body,
        grid_spec=pltpu.PrefetchScalarGridSpec(
            num_scalar_prefetch=1,
            grid=(D // step,),
            in_specs=[whole(v.shape) for v in (wide, slim, dkv, wide_in, slim_in, dkv_in)]
            + [
                pl.BlockSpec((step, D), lambda i, p: (i, 0)),
                pl.BlockSpec((step, 512), lambda i, p: (i, 0)),
            ],
            out_specs=[
                pl.BlockSpec((OWN, step), lambda i, p: (0, i)),
                whole((OWN, D)),
            ],
        ),
        out_shape=[
            jax.ShapeDtypeStruct((OWN, D), BF16),
            jax.ShapeDtypeStruct((OWN, D), BF16),
        ],
        compiler_params=params(),
        cost_estimate=cost(2 * OWN * D * 2048, 8 << 20),
        name="grad_tokens",
    )(place, wide, slim, dkv, wide_in, slim_in, dkv_in, w_query, w_keyval)


PLANE = (8, 2, SLAB, HEAD_DIM)


def sum_first_body(pieces, after, out):
    out[...] = jnp.sum(pieces[...].astype(F32), axis=0).astype(BF16)


def sum_first(pieces, after):
    return pl.pallas_call(
        sum_first_body,
        grid=(4,),
        in_specs=[
            pl.BlockSpec((16, 2) + PIECES[2:], lambda i: (0, i, 0, 0, 0)),
            pl.BlockSpec(memory_space=pl.ANY),
        ],
        out_specs=pl.BlockSpec((2,) + PLANE[1:], lambda i: (i, 0, 0, 0)),
        out_shape=jax.ShapeDtypeStruct(PLANE, BF16),
        compiler_params=params(MID),
        cost_estimate=cost(16 * 8 * 2 * SLAB * HEAD_DIM, 2 << 20),
        name="sum_first",
    )(pieces, after)


def sum_last_body(pieces, plane, out):
    out[:, :, 0] = plane[...]
    out[:, :, 1] = jnp.sum(pieces[...].astype(F32), axis=0).astype(BF16)


def sum_last(pieces, plane):
    return pl.pallas_call(
        sum_last_body,
        grid=(4,),
        in_specs=[
            pl.BlockSpec((16, 2) + PIECES[2:], lambda i: (0, i, 0, 0, 0)),
            pl.BlockSpec((2,) + PLANE[1:], lambda i: (i, 0, 0, 0)),
        ],
        out_specs=pl.BlockSpec((2, 2, 2, SLAB, HEAD_DIM), lambda i: (i, 0, 0, 0, 0)),
        out_shape=jax.ShapeDtypeStruct((8, 2, 2, SLAB, HEAD_DIM), BF16),
        compiler_params=params(MID),
        cost_estimate=cost(16 * 8 * 2 * SLAB * HEAD_DIM, 2 << 20),
        name="sum_last",
    )(pieces, plane)


def sum_line_body(lines, out):
    out[...] = jnp.sum(lines[...].astype(F32), axis=0).astype(BF16)


def sum_line(lines):
    return pl.pallas_call(
        sum_line_body,
        in_specs=[pl.BlockSpec(memory_space=pltpu.VMEM)],
        out_specs=pl.BlockSpec(memory_space=pltpu.VMEM),
        out_shape=jax.ShapeDtypeStruct(lines.shape[1:], BF16),
        compiler_params=params(MID),
        name="sum_line",
    )(lines)


def finish_body(place, near, far, *rest):
    near_in, far_in, (query_w, keyval_w) = rest[:3], rest[3:6], rest[6:]
    x = place[2]
    flip = place[3] == 1
    nears = [near] + list(near_in)
    fars = [far] + list(far_in)
    for source in range(4):
        for core in range(2):
            for part in range(2):
                one = nears[0][core, part]
                two = fars[0][core, part]
                for d in range(1, 4):
                    hit = (source + d) % 4 == x
                    one = jnp.where(hit, nears[d][core, part], one)
                    two = jnp.where(hit, fars[d][core, part], two)
                one = one.astype(F32)
                two = two.astype(F32)
                rows = jnp.concatenate(
                    [jnp.where(flip, two, one), jnp.where(flip, one, two)], axis=0
                ).astype(BF16)
                if part == 0 or source < 2:
                    at = (core * GROUP + part * 4 + source) * HEAD_DIM
                    query_w[:, at : at + HEAD_DIM] = rows
                else:
                    at = ((source - 2) * KV_HEADS + core) * HEAD_DIM
                    keyval_w[:, at : at + HEAD_DIM] = rows


def finish(place, near, far, near_in, far_in):
    vmem = pl.BlockSpec(memory_space=pltpu.VMEM)
    return pl.pallas_call(
        finish_body,
        in_specs=[pl.BlockSpec(memory_space=pltpu.SMEM)] + [vmem] * 8,
        out_specs=[vmem, vmem],
        out_shape=[
            jax.ShapeDtypeStruct((48, D), BF16),
            jax.ShapeDtypeStruct((48, 512), BF16),
        ],
        compiler_params=params(MID),
        name="finish",
    )(place, near, far, *near_in, *far_in)


def swap(value):
    return lax.ppermute(value, "c", [(0, 1), (1, 0)])


def shards(tokens, segments, w_query, w_keyval, grad_context):
    x_own = tokens[0]
    do_own = grad_context[0]
    place = jnp.stack(
        [lax.axis_index("c"), lax.axis_index(("z", "yl")), lax.axis_index("x"), lax.axis_index("yh")]
    ).astype(jnp.int32)
    x_oth = swap(x_own)
    do_oth = swap(do_own)
    count = 32
    ring = ("z", "yl", "c")
    q_own, kv_own = project_own(place, x_own, w_query, w_keyval)
    kv, kv_sent = project_kv(place, x_oth, kv_own, w_keyval)
    halo = lax.ppermute(kv_sent, ring, [(i, i + 2) for i in range(count - 2)])
    q_oth = project_q(place, x_oth, w_query)
    segs = segments.reshape(-1, BLOCK)
    inputs = (place, q_own, q_oth, do_own, do_oth, kv, halo, segs)
    wide, wide_oth, dkv = attend(*inputs)
    pieces = weight(x_own, x_oth, wide, wide_oth, 2, 2)
    pieces = lax.all_to_all(pieces, ("x", "yh", "yl"), 0, 0)
    slim, slim_oth, dkv, dkv_sent = attend(*inputs, dkv)
    arrived = lax.ppermute(dkv_sent, ring, [(i + 2, i) for i in range(count - 2)])
    wide_in = swap(wide_oth)
    slim_in = swap(slim_oth)
    last = weight(x_own, x_oth, slim, slim_oth, 1, 1)
    last, dkv_own, dkv_oth = weight_kv(place, x_own, x_oth, dkv, arrived, last)
    last = lax.all_to_all(last, ("x", "yh", "yl"), 0, 0)
    dkv_in = swap(dkv_oth)
    grad_in, context = grad_tokens(
        place, wide, slim, dkv_own, wide_in, slim_in, dkv_in, w_query, w_keyval
    )
    plane = sum_first(pieces, grad_in)
    plane = sum_last(last, plane)
    lines = lax.all_to_all(plane.reshape(16, 2, SLAB, HEAD_DIM), ("z", "c"), 0, 0)
    near = sum_line(lines.reshape(8, 2, 2, SLAB, HEAD_DIM))
    far = lax.ppermute(near, "yh", [(0, 1), (1, 0)])
    turns = [[(i, (i + d) % 4) for i in range(4)] for d in range(1, 4)]
    near_in = [lax.ppermute(near, "x", turn) for turn in turns]
    far_in = [lax.ppermute(far, "x", turn) for turn in turns]
    query_w, keyval_w = finish(place, near, far, near_in, far_in)
    return context[None], grad_in[None], query_w, keyval_w


def solution(mesh):
    fine = Mesh(mesh.devices.reshape(4, 2, 8, 2, 2), ("x", "yh", "z", "yl", "c"))
    dp = ("x", "yh")
    ctx = ("z", "yl", "c")
    return jax.shard_map(
        shards,
        mesh=fine,
        in_specs=(P(dp, ctx, None), P(dp, None), P(), P(), P(dp, ctx, None)),
        out_specs=(P(dp, ctx, None), P(dp, ctx, None), P(ctx, None), P(ctx, None)),
        check_vma=False,
    )
```

```python
import functools

import jax
import jax.numpy as jnp
from jax import lax
from jax.experimental import pallas as pl
from jax.experimental.pallas import tpu as pltpu
from jax.sharding import Mesh
from jax.sharding import PartitionSpec as P

HEAD_DIM = 128
GROUP = 6
KV_HEADS = 2
WINDOW = 512
BLOCK = 128
HALO = WINDOW - BLOCK
OWN = 256
PAIR = 2 * OWN
KEYS = HALO + PAIR
QCOLS = GROUP * HEAD_DIM
KVCOLS = 2 * HEAD_DIM
D = 1536
DOCS = 8
SCALE = HEAD_DIM ** (-0.5)
LOG2E = 1.4426950408889634
F32 = jnp.float32
BF16 = jnp.bfloat16
NT = (((1,), (1,)), ((), ()))
TN = (((0,), (0,)), ((), ()))
ROWS = 48
PIECES = (32, 4, 2, ROWS, HEAD_DIM)
LIMIT = 24 * 1024 * 1024
VM = pl.BlockSpec(memory_space=pltpu.VMEM)
ANY = pl.BlockSpec(memory_space=pl.ANY)


def params():
    return pltpu.CompilerParams(vmem_limit_bytes=LIMIT)


def cost(flops, moved, trans=0):
    return pl.CostEstimate(flops=flops, bytes_accessed=moved, transcendentals=trans)


def shape(dims, dtype=BF16):
    return jax.ShapeDtypeStruct(dims, dtype)


def nn(a, b):
    return jnp.dot(a, b, preferred_element_type=F32)


def nt(a, b):
    return lax.dot_general(a, b, NT, preferred_element_type=F32)


def tn(a, b):
    return lax.dot_general(a, b, TN, preferred_element_type=F32)


def eye(size):
    row = lax.broadcasted_iota(jnp.int32, (size, size), 0)
    col = lax.broadcasted_iota(jnp.int32, (size, size), 1)
    return jnp.where(row == col, 1.0, 0.0).astype(BF16)


def columns(start, width=HEAD_DIM):
    return pl.ds(pl.multiple_of(start, HEAD_DIM), width)


def project_own_body(x, wkv, wq, x_here, wkv_here, wq_here, q, kv, sems):
    c = lax.axis_index("c")
    chunk = 512
    copies = [
        pltpu.make_async_copy(x, x_here, sems.at[0]),
        pltpu.make_async_copy(wkv, wkv_here, sems.at[1]),
    ]
    for j in range(D // chunk):
        rows = pl.ds(j * chunk, chunk)
        copies.append(
            pltpu.make_async_copy(
                wq.at[rows, columns(c * QCOLS, QCOLS)], wq_here.at[rows], sems.at[2 + j]
            )
        )
    for copy in copies:
        copy.start()
    copies[0].wait()
    copies[1].wait()
    kv[...] = nn(x_here[...], head_columns(wkv_here, c)).astype(BF16)
    total = jnp.zeros((OWN, QCOLS), F32)
    for j in range(D // chunk):
        rows = slice(j * chunk, (j + 1) * chunk)
        copies[2 + j].wait()
        total = total + nn(x_here[:, rows], wq_here[rows, :])
    q[...] = total.astype(BF16)


def head_columns(wkv, c):
    keys_w = wkv[:, columns(c * HEAD_DIM)]
    vals_w = wkv[:, columns((KV_HEADS + c) * HEAD_DIM)]
    return jnp.concatenate([keys_w, vals_w], axis=1)


def project_own(x, w_keyval, w_query):
    return pl.pallas_call(
        project_own_body,
        in_specs=[ANY] * 3,
        out_specs=[VM] * 5,
        out_shape=[
            pltpu.VMEM((OWN, D), BF16),
            pltpu.VMEM((D, 512), BF16),
            pltpu.VMEM((D, QCOLS), BF16),
            shape((OWN, QCOLS)),
            shape((OWN, KVCOLS)),
        ],
        scratch_shapes=[pltpu.SemaphoreType.DMA((5,))],
        compiler_params=params(),
        cost_estimate=cost(2 * OWN * D * 1024, 5 << 20),
        name="project_own",
    )(*(pltpu.with_memory_space_constraint(v, pltpu.HBM) for v in (x, w_keyval, w_query)))


def project_kv_body(x_oth, kv_own, w, kv, sent):
    c = lax.axis_index("c")
    own = kv_own[...]
    oth = nn(x_oth[...], head_columns(w, c)).astype(BF16)
    low = jnp.where(c == 0, own, oth)
    high = jnp.where(c == 0, oth, own)
    kv[:OWN] = low
    kv[OWN:] = high
    sent[: HALO - OWN] = low[PAIR - HALO :]
    sent[HALO - OWN :] = high


def project_kv(x_oth, kv_own, w_keyval):
    return pl.pallas_call(
        project_kv_body,
        in_specs=[VM] * 3,
        out_specs=[VM] * 2,
        out_shape=[shape((PAIR, KVCOLS)), shape((HALO, KVCOLS))],
        compiler_params=params(),
        cost_estimate=cost(2 * OWN * D * KVCOLS, 2 << 20),
        name="project_kv",
    )(x_oth, kv_own, w_keyval)


def project_q_body(x_oth, q_own, w, q):
    q[:OWN] = q_own[...]
    for j in range(3):
        cols = slice(j * 256, (j + 1) * 256)
        q[OWN:, cols] = nn(x_oth[...], w[:, cols]).astype(BF16)


def project_q(x_oth, q_own, w_query):
    return pl.pallas_call(
        project_q_body,
        in_specs=[VM] * 3,
        out_specs=VM,
        out_shape=shape((PAIR, QCOLS)),
        compiler_params=params(),
        cost_estimate=cost(2 * OWN * D * QCOLS, 4 << 20),
        name="project_q",
    )(x_oth, q_own, w_query)


def attend_block(b, c, chip, q, do_own, do_oth, keys, keys_t, vals_t, starts, segs, ones):
    half, inner = b // 2, (b % 2) * BLOCK
    own = half == c
    here = slice(inner, inner + BLOCK)
    q_rows = pl.ds(pl.multiple_of(jnp.where(own, 0, OWN) + inner, BLOCK), BLOCK)
    win = slice(b * BLOCK, b * BLOCK + WINDOW)
    k_win = keys[win, :HEAD_DIM]
    v_win = keys[win, HEAD_DIM:]
    v_more = jnp.concatenate([v_win, ones[:HEAD_DIM, :HEAD_DIM]], axis=0)
    kt_win = keys_t[:, win]
    vt_win = vals_t[:, win]
    line = segs[pl.ds(chip * (PAIR // BLOCK) + b, 1), :]
    lowest = jnp.zeros_like(line)
    for d in range(DOCS):
        lowest = jnp.where(line == d, starts[d], lowest)
    j_pos = lax.broadcasted_iota(jnp.int32, (WINDOW, BLOCK), 0)
    i_pos = lax.broadcasted_iota(jnp.int32, (WINDOW, BLOCK), 1)
    seen = (j_pos + b * BLOCK >= lowest) & (j_pos <= i_pos + HALO)
    bias = jnp.where(seen, 0.0, -1e30)
    bias = jnp.concatenate([bias, bias], axis=1)
    dk = jnp.zeros((WINDOW, HEAD_DIM), F32)
    dv = jnp.zeros((WINDOW, HEAD_DIM), F32)
    ctx_parts = []
    dq_parts = []
    for pair in range(GROUP // 2):
        at = pair * 256
        q_two = q[q_rows, at : at + 256]
        do_cols = columns(c * QCOLS + at, 256)
        do_two = jnp.where(own, do_own[here, do_cols], do_oth[here, do_cols])
        q2 = jnp.concatenate([q_two[:, :HEAD_DIM], q_two[:, HEAD_DIM:]], axis=0)
        do2 = jnp.concatenate([do_two[:, :HEAD_DIM], do_two[:, HEAD_DIM:]], axis=0)
        scores = nt(k_win, q2) + bias
        top = jnp.max(scores, axis=0, keepdims=True)
        expo = jnp.exp2((scores - top) * (SCALE * LOG2E))
        probs = expo * (1.0 / jnp.sum(expo, axis=0, keepdims=True))
        probs_low = probs.astype(BF16)
        ctx_t = nn(vt_win, probs_low).astype(BF16)
        dp = nt(v_more, do2)
        delta = jnp.sum(dp[WINDOW:] * ctx_t.astype(F32), axis=0, keepdims=True)
        ds = (probs * (dp[:WINDOW] - delta) * SCALE).astype(BF16)
        dv = dv + nn(probs_low, do2)
        dk = dk + nn(ds, q2)
        dq_t = nn(kt_win, ds).astype(BF16)
        turned = nt(ones, jnp.concatenate([ctx_t, dq_t], axis=0)).astype(BF16)
        ctx_parts += [turned[:BLOCK, :HEAD_DIM], turned[BLOCK:, :HEAD_DIM]]
        dq_parts += [turned[:BLOCK, HEAD_DIM:], turned[BLOCK:, HEAD_DIM:]]
    return jnp.concatenate(ctx_parts + dq_parts, axis=1), jnp.concatenate([dk, dv], axis=1)


def turn_keys(ones, keys, keys_t, vals_t, rows):
    small = ones[:HEAD_DIM, :HEAD_DIM]
    keys_t[:, rows] = nt(small, keys[rows, :HEAD_DIM]).astype(BF16)
    vals_t[:, rows] = nt(small, keys[rows, HEAD_DIM:]).astype(BF16)


def document_starts(chip, segs):
    lines = []
    for t in range(KEYS // BLOCK):
        row = chip * (PAIR // BLOCK) - HALO // BLOCK + t
        line = segs[pl.ds(jnp.maximum(row, 0), 1), :]
        lines.append(jnp.where(row >= 0, line, -1))
    lines = jnp.concatenate(lines, axis=0)
    return [jnp.sum(jnp.where(lines < d, 1, 0)) for d in range(DOCS)]


def attend_last_body(q, do_own, do_oth, kv, segs, mix, dkv, keys, keys_t, vals_t):
    c = lax.axis_index("c")
    chip = lax.axis_index(("zh", "zl", "yl"))
    ones = eye(256)
    keys[HALO:] = kv[...]
    turn_keys(ones, keys, keys_t, vals_t, slice(HALO, KEYS))
    starts = document_starts(chip, segs)
    mix_block, dkv[...] = attend_block(
        3, c, chip, q, do_own, do_oth, keys, keys_t, vals_t, starts, segs, ones
    )
    mix[...] = mix_block


def attend_last(q, do_own, do_oth, kv, segs):
    return pl.pallas_call(
        attend_last_body,
        in_specs=[VM] * 5,
        out_specs=[VM] * 2,
        out_shape=[shape((BLOCK, 2 * QCOLS)), shape((WINDOW, KVCOLS), F32)],
        scratch_shapes=[
            pltpu.VMEM((KEYS, KVCOLS), BF16),
            pltpu.VMEM((HEAD_DIM, KEYS), BF16),
            pltpu.VMEM((HEAD_DIM, KEYS), BF16),
        ],
        compiler_params=params(),
        cost_estimate=cost(2 * BLOCK * WINDOW * QCOLS * 6, 3 << 20, BLOCK * WINDOW * GROUP),
        name="attend_last",
    )(q, do_own, do_oth, kv, segs)


def attend_body(
    q,
    do_own,
    do_oth,
    kv,
    halo,
    segs,
    mix_last,
    dkv_last,
    mix_own,
    mix_oth,
    dkv_out,
    sent_out,
    keys,
    keys_t,
    vals_t,
    dkv,
):
    c = lax.axis_index("c")
    chip = lax.axis_index(("zh", "zl", "yl"))
    ones = eye(256)
    keys[:HALO] = halo[...]
    keys[HALO:] = kv[...]
    turn_keys(ones, keys, keys_t, vals_t, slice(0, KEYS))
    starts = document_starts(chip, segs)
    dkv[:HALO] = jnp.zeros((HALO, KVCOLS), F32)
    dkv[HALO:] = dkv_last[...]

    def put(b, value):
        own = b // 2 == c
        here = slice((b % 2) * BLOCK, (b % 2 + 1) * BLOCK)

        @pl.when(own)
        def _():
            mix_own[here, :] = value

        @pl.when(jnp.logical_not(own))
        def _():
            mix_oth[here, :] = value

    for b in range(3):
        mix, grads = attend_block(
            b, c, chip, q, do_own, do_oth, keys, keys_t, vals_t, starts, segs, ones
        )
        dkv[b * BLOCK : b * BLOCK + WINDOW, :] += grads
        put(b, mix)
    put(3, mix_last[...])
    sent_out[...] = dkv[:HALO, :].astype(BF16)
    dkv_out[...] = dkv[HALO:, :]


def attend(q, do_own, do_oth, kv, halo, segs, mix_last, dkv_last):
    return pl.pallas_call(
        attend_body,
        in_specs=[VM] * 8,
        out_specs=[VM] * 4,
        out_shape=[
            shape((OWN, 2 * QCOLS)),
            shape((OWN, 2 * QCOLS)),
            shape((PAIR, KVCOLS), F32),
            shape((HALO, KVCOLS)),
        ],
        scratch_shapes=[
            pltpu.VMEM((KEYS, KVCOLS), BF16),
            pltpu.VMEM((HEAD_DIM, KEYS), BF16),
            pltpu.VMEM((HEAD_DIM, KEYS), BF16),
            pltpu.VMEM((KEYS, KVCOLS), F32),
        ],
        compiler_params=params(),
        cost_estimate=cost(3 * 2 * BLOCK * WINDOW * QCOLS * 6, 5 << 20, 3 * BLOCK * WINDOW * 6),
        name="attend",
    )(q, do_own, do_oth, kv, halo, segs, mix_last, dkv_last)


def spread(value, held):
    for s in range(2):
        for y in range(2):
            for zl in range(2):
                for zh in range(4):
                    for core in range(2):
                        row = (zh * 2 + zl) * 192 + y * 96 + core * ROWS
                        piece = value[row : row + ROWS, s * HEAD_DIM : (s + 1) * HEAD_DIM]
                        held[s * 4 + y * 2 + zl, zh, core] = piece.astype(BF16)


def weight_q_body(x_own, x_oth, mix_own, mix_oth, out, held, sems):
    copies = []
    for j in range(3):
        cols = slice(QCOLS + j * 256, QCOLS + (j + 1) * 256)
        value = tn(x_own[...], mix_own[:, cols]) + tn(x_oth[...], mix_oth[:, cols])
        spread(value, held.at[j])
        copy = pltpu.make_async_copy(held.at[j], out.at[pl.ds(8 * j, 8)], sems.at[j])
        copy.start()
        copies.append(copy)
    for copy in copies:
        copy.wait()


def weight_q(x_own, x_oth, mix_own, mix_oth):
    return pl.pallas_call(
        weight_q_body,
        in_specs=[VM] * 4,
        out_specs=ANY,
        out_shape=pltpu.HBM(PIECES, BF16),
        scratch_shapes=[
            pltpu.VMEM((3, 8) + PIECES[1:], BF16),
            pltpu.SemaphoreType.DMA((3,)),
        ],
        compiler_params=params(),
        cost_estimate=cost(2 * PAIR * D * QCOLS, 4 << 20),
        name="weight_q",
    )(x_own, x_oth, mix_own, mix_oth)


def weight_kv_body(x_own, x_oth, dkv, arrived, before, out, own_out, oth_out, held, sem):
    c = lax.axis_index("c")
    low = dkv[:OWN]
    skip = PAIR - HALO
    low = jnp.concatenate([low[:skip], low[skip:] + arrived[: OWN - skip].astype(F32)], axis=0)
    high = dkv[OWN:] + arrived[OWN - skip :].astype(F32)
    low = low.astype(BF16)
    high = high.astype(BF16)
    own = jnp.where(c == 0, low, high)
    oth = jnp.where(c == 0, high, low)
    own_out[...] = own
    oth_out[...] = oth
    spread(tn(x_own[...], own) + tn(x_oth[...], oth), held)
    copy = pltpu.make_async_copy(held, out.at[pl.ds(24, 8)], sem)
    copy.start()
    copy.wait()


def weight_kv(x_own, x_oth, dkv, arrived, before):
    return pl.pallas_call(
        weight_kv_body,
        in_specs=[VM] * 4 + [ANY],
        out_specs=[ANY, VM, VM],
        out_shape=[pltpu.HBM(PIECES, BF16), shape((OWN, KVCOLS)), shape((OWN, KVCOLS))],
        scratch_shapes=[pltpu.VMEM((8,) + PIECES[1:], BF16), pltpu.SemaphoreType.DMA],
        input_output_aliases={4: 0},
        compiler_params=params(),
        cost_estimate=cost(2 * PAIR * D * KVCOLS, 3 << 20),
        name="weight_kv",
    )(x_own, x_oth, dkv, arrived, before)


def ordered(first, own, oth):
    return jnp.where(
        first, jnp.concatenate([own, oth], axis=1), jnp.concatenate([oth, own], axis=1)
    )


def grad_tokens_body(mix, dkv, mix_in, dkv_in, wq, wkv, out, ctx_out, done):
    done[...] = jnp.zeros_like(done)
    first = lax.axis_index("c") == 0
    dq = ordered(first, mix[:, QCOLS:], mix_in[:, QCOLS:])
    kv = dkv[...]
    kv_in = dkv_in[...]
    keys = ordered(first, kv[:, :HEAD_DIM], kv_in[:, :HEAD_DIM])
    vals = ordered(first, kv[:, HEAD_DIM:], kv_in[:, HEAD_DIM:])
    kv_full = jnp.concatenate([keys, vals], axis=1)
    for j in range(3):
        rows = slice(j * 512, (j + 1) * 512)
        out[:, rows] = (nt(dq, wq[rows, :]) + nt(kv_full, wkv[rows, :])).astype(BF16)
    ctx_out[...] = ordered(first, mix[:, :QCOLS], mix_in[:, :QCOLS])


def grad_tokens(mix, dkv, mix_in, dkv_in, w_query, w_keyval):
    return pl.pallas_call(
        grad_tokens_body,
        in_specs=[VM] * 6,
        out_specs=[VM] * 3,
        out_shape=[shape((OWN, D)), shape((OWN, D)), shape((8, 128), F32)],
        compiler_params=params(),
        cost_estimate=cost(2 * OWN * D * 2048, 8 << 20),
        name="grad_tokens",
    )(mix, dkv, mix_in, dkv_in, w_query, w_keyval)


def sum_plane_body(pieces, after, out):
    out[...] = jnp.sum(pieces[...].astype(F32), axis=0).astype(BF16)


def sum_plane(pieces, after):
    return pl.pallas_call(
        sum_plane_body,
        in_specs=[VM, VM],
        out_specs=VM,
        out_shape=shape(PIECES[1:]),
        compiler_params=params(),
        cost_estimate=cost(32 * 8 * ROWS * HEAD_DIM, 3 << 20),
        name="sum_plane",
    )(pieces, after)


def sum_line_body(lines, out):
    total = jnp.sum(lines[...].astype(F32), axis=0).astype(BF16)
    for s in range(8):
        out[s] = total


def sum_line(lines):
    return pl.pallas_call(
        sum_line_body,
        in_specs=[VM],
        out_specs=VM,
        out_shape=shape((8, 2, ROWS, HEAD_DIM)),
        compiler_params=params(),
        name="sum_line",
    )(lines)


def finish_body(blocks, query_w, keyval_w):
    for s in range(8):
        for core in range(2):
            if s < GROUP:
                at = (core * GROUP + s) * HEAD_DIM
                query_w[:, at : at + HEAD_DIM] = blocks[s, core]
            else:
                at = ((s - GROUP) * KV_HEADS + core) * HEAD_DIM
                keyval_w[:, at : at + HEAD_DIM] = blocks[s, core]


def finish(blocks):
    return pl.pallas_call(
        finish_body,
        in_specs=[VM],
        out_specs=[VM, VM],
        out_shape=[shape((ROWS, D)), shape((ROWS, 512))],
        compiler_params=params(),
        name="finish",
    )(blocks)


def swap(value):
    return lax.ppermute(value, "c", [(0, 1), (1, 0)])


def shards(tokens, segments, w_query, w_keyval, grad_context):
    x_own = tokens[0]
    do_own = grad_context[0]
    x_oth = swap(x_own)
    do_oth = swap(do_own)
    count = 32
    ring = ("zh", "zl", "yl", "c")
    x_own, wkv_here, wq_here, q_own, kv_own = project_own(x_own, w_keyval, w_query)
    kv, kv_sent = project_kv(x_oth, kv_own, wkv_here)
    halo = lax.ppermute(kv_sent, ring, [(i, i + 2) for i in range(count - 2)])
    q = project_q(x_oth, q_own, wq_here)
    segs = segments.reshape(-1, BLOCK)
    mix_last, dkv_last = attend_last(q, do_own, do_oth, kv, segs)
    mix, mix_oth, dkv, dkv_sent = attend(q, do_own, do_oth, kv, halo, segs, mix_last, dkv_last)
    arrived = lax.ppermute(dkv_sent, ring, [(i + 2, i) for i in range(count - 2)])
    pieces = weight_q(x_own, x_oth, mix, mix_oth)
    pieces, dkv_own, dkv_oth = weight_kv(x_own, x_oth, dkv, arrived, pieces)
    pieces = lax.all_to_all(pieces, ("x", "yh", "yl", "zl"), 0, 0)
    mix_in = swap(mix_oth)
    dkv_in = swap(dkv_oth)
    grad_in, context, done = grad_tokens(mix, dkv_own, mix_in, dkv_in, w_query, w_keyval)
    plane = sum_plane(pieces, done)
    lines = lax.all_to_all(plane.reshape(8, ROWS, HEAD_DIM), ("zh", "c"), 0, 0)
    blocks = sum_line(lines.reshape(4, 2, ROWS, HEAD_DIM))
    blocks = lax.all_to_all(blocks, ("x", "yh"), 0, 0)
    query_w, keyval_w = finish(blocks)
    return context[None], grad_in[None], query_w, keyval_w


def solution(mesh):
    fine = Mesh(mesh.devices.reshape(4, 2, 4, 2, 2, 2), ("x", "yh", "zh", "zl", "yl", "c"))
    dp = ("x", "yh")
    ctx = ("zh", "zl", "yl", "c")
    return jax.shard_map(
        shards,
        mesh=fine,
        in_specs=(P(dp, ctx, None), P(dp, None), P(), P(), P(dp, ctx, None)),
        out_specs=(P(dp, ctx, None), P(dp, ctx, None), P(ctx, None), P(ctx, None)),
        check_vma=False,
    )
```

```python
import functools

import jax
import jax.numpy as jnp
from jax import lax
from jax.experimental import pallas as pl
from jax.experimental.pallas import tpu as pltpu
from jax.sharding import Mesh
from jax.sharding import PartitionSpec as P

HEAD_DIM = 128
GROUP = 6
KV_HEADS = 2
WINDOW = 512
BLOCK = 128
HALO = WINDOW - BLOCK
OWN = 256
PAIR = 2 * OWN
KEYS = HALO + PAIR
QCOLS = GROUP * HEAD_DIM
KVCOLS = 2 * HEAD_DIM
D = 1536
DOCS = 8
SCALE = HEAD_DIM ** (-0.5)
LOG2E = 1.4426950408889634
F32 = jnp.float32
BF16 = jnp.bfloat16
NT = (((1,), (1,)), ((), ()))
TN = (((0,), (0,)), ((), ()))
ROWS = 48
SLAB = 24
WIDE = 512
REST = 256
PIECES = (32, 4, 2, SLAB, HEAD_DIM)
LIMIT = 24 * 1024 * 1024
VM = pl.BlockSpec(memory_space=pltpu.VMEM)
ANY = pl.BlockSpec(memory_space=pl.ANY)


def params():
    return pltpu.CompilerParams(vmem_limit_bytes=LIMIT)


def cost(flops, moved, trans=0):
    return pl.CostEstimate(flops=flops, bytes_accessed=moved, transcendentals=trans)


def shape(dims, dtype=BF16):
    return jax.ShapeDtypeStruct(dims, dtype)


def nn(a, b):
    return jnp.dot(a, b, preferred_element_type=F32)


def nt(a, b):
    return lax.dot_general(a, b, NT, preferred_element_type=F32)


def tn(a, b):
    return lax.dot_general(a, b, TN, preferred_element_type=F32)


def eye(size):
    row = lax.broadcasted_iota(jnp.int32, (size, size), 0)
    col = lax.broadcasted_iota(jnp.int32, (size, size), 1)
    return jnp.where(row == col, 1.0, 0.0).astype(BF16)


def columns(start, width=HEAD_DIM):
    return pl.ds(pl.multiple_of(start, HEAD_DIM), width)


def project_own_body(x, wkv, wq, x_here, wkv_here, wq_here, q, kv, sems):
    c = lax.axis_index("c")
    chunk = 512
    copies = [
        pltpu.make_async_copy(x, x_here, sems.at[0]),
        pltpu.make_async_copy(wkv, wkv_here, sems.at[1]),
    ]
    for j in range(D // chunk):
        rows = pl.ds(j * chunk, chunk)
        copies.append(
            pltpu.make_async_copy(
                wq.at[rows, columns(c * QCOLS, QCOLS)], wq_here.at[rows], sems.at[2 + j]
            )
        )
    for copy in copies:
        copy.start()
    copies[0].wait()
    copies[1].wait()
    kv[...] = nn(x_here[...], head_columns(wkv_here, c)).astype(BF16)
    total = jnp.zeros((OWN, QCOLS), F32)
    for j in range(D // chunk):
        rows = slice(j * chunk, (j + 1) * chunk)
        copies[2 + j].wait()
        total = total + nn(x_here[:, rows], wq_here[rows, :])
    q[...] = total.astype(BF16)


def head_columns(wkv, c):
    keys_w = wkv[:, columns(c * HEAD_DIM)]
    vals_w = wkv[:, columns((KV_HEADS + c) * HEAD_DIM)]
    return jnp.concatenate([keys_w, vals_w], axis=1)


def project_own(x, w_keyval, w_query):
    return pl.pallas_call(
        project_own_body,
        in_specs=[ANY] * 3,
        out_specs=[VM] * 5,
        out_shape=[
            pltpu.VMEM((OWN, D), BF16),
            pltpu.VMEM((D, 512), BF16),
            pltpu.VMEM((D, QCOLS), BF16),
            shape((OWN, QCOLS)),
            shape((OWN, KVCOLS)),
        ],
        scratch_shapes=[pltpu.SemaphoreType.DMA((5,))],
        compiler_params=params(),
        cost_estimate=cost(2 * OWN * D * 1024, 5 << 20),
        name="project_own",
    )(*(pltpu.with_memory_space_constraint(v, pltpu.HBM) for v in (x, w_keyval, w_query)))


def project_kv_body(x_oth, kv_own, w, kv, sent):
    c = lax.axis_index("c")
    own = kv_own[...]
    oth = nn(x_oth[...], head_columns(w, c)).astype(BF16)
    low = jnp.where(c == 0, own, oth)
    high = jnp.where(c == 0, oth, own)
    kv[:OWN] = low
    kv[OWN:] = high
    sent[: HALO - OWN] = low[PAIR - HALO :]
    sent[HALO - OWN :] = high


def project_kv(x_oth, kv_own, w_keyval):
    return pl.pallas_call(
        project_kv_body,
        in_specs=[VM] * 3,
        out_specs=[VM] * 2,
        out_shape=[shape((PAIR, KVCOLS)), shape((HALO, KVCOLS))],
        compiler_params=params(),
        cost_estimate=cost(2 * OWN * D * KVCOLS, 2 << 20),
        name="project_kv",
    )(x_oth, kv_own, w_keyval)


def project_q_body(x_oth, q_own, w, q):
    q[:OWN] = q_own[...]
    for j in range(3):
        cols = slice(j * 256, (j + 1) * 256)
        q[OWN:, cols] = nn(x_oth[...], w[:, cols]).astype(BF16)


def project_q(x_oth, q_own, w_query):
    return pl.pallas_call(
        project_q_body,
        in_specs=[VM] * 3,
        out_specs=VM,
        out_shape=shape((PAIR, QCOLS)),
        compiler_params=params(),
        cost_estimate=cost(2 * OWN * D * QCOLS, 4 << 20),
        name="project_q",
    )(x_oth, q_own, w_query)


def attend_block(b, pairs, c, q, do_own, do_oth, keys, keys_t, vals_t, low, ones):
    half, inner = b // 2, (b % 2) * BLOCK
    own = half == c
    here = slice(inner, inner + BLOCK)
    q_rows = pl.ds(pl.multiple_of(jnp.where(own, 0, OWN) + inner, BLOCK), BLOCK)
    win = slice(b * BLOCK, b * BLOCK + WINDOW)
    k_win = keys[win, :HEAD_DIM]
    v_win = keys[win, HEAD_DIM:]
    v_more = jnp.concatenate([v_win, ones[:HEAD_DIM, :HEAD_DIM]], axis=0)
    kt_win = keys_t[:, win]
    vt_win = vals_t[:, win]
    j_pos = lax.broadcasted_iota(jnp.int32, (WINDOW, BLOCK), 0)
    i_pos = lax.broadcasted_iota(jnp.int32, (WINDOW, BLOCK), 1)
    seen = (j_pos + b * BLOCK >= low[b : b + 1, :]) & (j_pos <= i_pos + HALO)
    bias = jnp.where(seen, 0.0, -1e30)
    bias = jnp.concatenate([bias, bias], axis=1)
    q2s, do2s = [], []
    for pair in pairs:
        at = pair * 256
        q_two = q[q_rows, at : at + 256]
        do_cols = columns(c * QCOLS + at, 256)
        do_two = jnp.where(own, do_own[here, do_cols], do_oth[here, do_cols])
        q2s.append(jnp.concatenate([q_two[:, :HEAD_DIM], q_two[:, HEAD_DIM:]], axis=0))
        do2s.append(jnp.concatenate([do_two[:, :HEAD_DIM], do_two[:, HEAD_DIM:]], axis=0))
    raw = [nt(k_win, q2) for q2 in q2s]
    probs = []
    for scores in raw:
        scores = scores + bias
        top = jnp.max(scores, axis=0, keepdims=True)
        expo = jnp.exp2((scores - top) * (SCALE * LOG2E))
        probs.append(expo * (1.0 / jnp.sum(expo, axis=0, keepdims=True)))
    lows = [p.astype(BF16) for p in probs]
    dps = [nt(v_more, do2) for do2 in do2s]
    ctx_ts = [nn(vt_win, p).astype(BF16) for p in lows]
    deltas = [
        jnp.sum(dp[WINDOW:] * ctx_t.astype(F32), axis=0, keepdims=True)
        for dp, ctx_t in zip(dps, ctx_ts)
    ]
    dvs = [nn(p, do2) for p, do2 in zip(lows, do2s)]
    dss = [
        (p * (dp[:WINDOW] - delta) * SCALE).astype(BF16)
        for p, dp, delta in zip(probs, dps, deltas)
    ]
    dks = [nn(ds, q2) for ds, q2 in zip(dss, q2s)]
    dq_ts = [nn(kt_win, ds).astype(BF16) for ds in dss]
    ctx_parts, dq_parts = [], []
    for ctx_t, dq_t in zip(ctx_ts, dq_ts):
        turned = nt(ones, jnp.concatenate([ctx_t, dq_t], axis=0)).astype(BF16)
        ctx_parts += [turned[:BLOCK, :HEAD_DIM], turned[BLOCK:, :HEAD_DIM]]
        dq_parts += [turned[:BLOCK, HEAD_DIM:], turned[BLOCK:, HEAD_DIM:]]
    grads = jnp.concatenate([sum(dks[1:], dks[0]), sum(dvs[1:], dvs[0])], axis=1)
    return ctx_parts, dq_parts, grads


def turn_keys(ones, keys, keys_t, vals_t, rows):
    small = ones[:HEAD_DIM, :HEAD_DIM]
    keys_t[:, rows] = nt(small, keys[rows, :HEAD_DIM]).astype(BF16)
    vals_t[:, rows] = nt(small, keys[rows, HEAD_DIM:]).astype(BF16)


def lowest_keys(chip, segs, low):
    lines = []
    for t in range(KEYS // BLOCK):
        row = chip * (PAIR // BLOCK) - HALO // BLOCK + t
        line = segs[pl.ds(jnp.maximum(row, 0), 1), :]
        lines.append(jnp.where(row >= 0, line, -1))
    own = jnp.concatenate(lines[HALO // BLOCK :], axis=0)
    lines = jnp.concatenate(lines, axis=0)
    first = jnp.zeros_like(own)
    for d in range(DOCS):
        first = jnp.where(own == d, jnp.sum(jnp.where(lines < d, 1, 0)), first)
    low[: PAIR // BLOCK, :] = first


def attend_last_body(
    q, do_own, do_oth, kv, segs, wide, slim, dkv, low, keys, keys_t, vals_t
):
    c = lax.axis_index("c")
    chip = lax.axis_index(("zh", "zl", "yl"))
    ones = eye(256)
    keys[HALO:] = kv[...]
    turn_keys(ones, keys, keys_t, vals_t, slice(HALO, KEYS))
    lowest_keys(chip, segs, low)
    ctx, dq, dkv[...] = attend_block(
        3, range(3), c, q, do_own, do_oth, keys, keys_t, vals_t, low, ones
    )
    wide[...] = jnp.concatenate(ctx[:4] + dq[:4], axis=1)
    slim[...] = jnp.concatenate(ctx[4:] + dq[4:], axis=1)


KEY_SCRATCH = [
    pltpu.VMEM((KEYS, KVCOLS), BF16),
    pltpu.VMEM((HEAD_DIM, KEYS), BF16),
    pltpu.VMEM((HEAD_DIM, KEYS), BF16),
]


def attend_last(q, do_own, do_oth, kv, segs):
    return pl.pallas_call(
        attend_last_body,
        in_specs=[VM] * 5,
        out_specs=[VM] * 4,
        out_shape=[
            shape((BLOCK, 2 * WIDE)),
            shape((BLOCK, 2 * REST)),
            shape((WINDOW, KVCOLS), F32),
            shape((8, BLOCK), jnp.int32),
        ],
        scratch_shapes=KEY_SCRATCH,
        compiler_params=params(),
        cost_estimate=cost(2 * BLOCK * WINDOW * QCOLS * 6, 3 << 20, BLOCK * WINDOW * GROUP),
        name="attend_last",
    )(q, do_own, do_oth, kv, segs)


def put(c, b, mix_own, mix_oth, value):
    own = b // 2 == c
    here = slice((b % 2) * BLOCK, (b % 2 + 1) * BLOCK)

    @pl.when(own)
    def _():
        mix_own[here, :] = value

    @pl.when(jnp.logical_not(own))
    def _():
        mix_oth[here, :] = value


def attend_rest(pairs, q, do_own, do_oth, kv, halo, low, mix_last, mix_own, mix_oth, dkv, held):
    keys, keys_t, vals_t = held
    c = lax.axis_index("c")
    ones = eye(256)
    keys[:HALO] = halo[...]
    keys[HALO:] = kv[...]
    turn_keys(ones, keys, keys_t, vals_t, slice(0, KEYS))
    put(c, 3, mix_own, mix_oth, mix_last[...])
    for b in range(3):
        ctx, dq, grads = attend_block(
            b, pairs, c, q, do_own, do_oth, keys, keys_t, vals_t, low, ones
        )
        dkv[b * BLOCK : b * BLOCK + WINDOW, :] += grads
        put(c, b, mix_own, mix_oth, jnp.concatenate(ctx + dq, axis=1))


def attend_wide_body(q, do_own, do_oth, kv, halo, low, mix_last, dkv_in, *rest):
    mix_own, mix_oth, dkv, *held = rest
    dkv[:HALO] = jnp.zeros((HALO, KVCOLS), F32)
    dkv[HALO:] = dkv_in[...]
    attend_rest(
        range(2), q, do_own, do_oth, kv, halo, low, mix_last, mix_own, mix_oth, dkv, held
    )


def attend_wide(q, do_own, do_oth, kv, halo, low, mix_last, dkv_in):
    return pl.pallas_call(
        attend_wide_body,
        in_specs=[VM] * 8,
        out_specs=[VM] * 3,
        out_shape=[
            shape((OWN, 2 * WIDE)),
            shape((OWN, 2 * WIDE)),
            shape((KEYS, KVCOLS), F32),
        ],
        scratch_shapes=KEY_SCRATCH,
        compiler_params=params(),
        cost_estimate=cost(3 * 2 * BLOCK * WINDOW * WIDE * 6, 5 << 20, 3 * BLOCK * WINDOW * 4),
        name="attend_wide",
    )(q, do_own, do_oth, kv, halo, low, mix_last, dkv_in)


def attend_slim_body(q, do_own, do_oth, kv, halo, low, mix_last, dkv_in, *rest):
    mix_own, mix_oth, dkv_out, sent, dkv, *held = rest
    dkv[...] = dkv_in[...]
    attend_rest(
        range(2, 3), q, do_own, do_oth, kv, halo, low, mix_last, mix_own, mix_oth, dkv, held
    )
    sent[...] = dkv[:HALO, :].astype(BF16)
    dkv_out[...] = dkv[HALO:, :]


def attend_slim(q, do_own, do_oth, kv, halo, low, mix_last, dkv_in):
    return pl.pallas_call(
        attend_slim_body,
        in_specs=[VM] * 8,
        out_specs=[VM] * 4,
        out_shape=[
            shape((OWN, 2 * REST)),
            shape((OWN, 2 * REST)),
            shape((PAIR, KVCOLS), F32),
            shape((HALO, KVCOLS)),
        ],
        scratch_shapes=[pltpu.VMEM((KEYS, KVCOLS), F32)] + KEY_SCRATCH,
        compiler_params=params(),
        cost_estimate=cost(3 * 2 * BLOCK * WINDOW * REST * 6, 5 << 20, 3 * BLOCK * WINDOW * 2),
        name="attend_slim",
    )(q, do_own, do_oth, kv, halo, low, mix_last, dkv_in)


def spread(value, held):
    for s in range(2):
        for yh in range(2):
            for yl in range(2):
                for zl in range(2):
                    for zh in range(4):
                        for core in range(2):
                            row = (zh * 2 + zl) * 192 + yl * 96 + core * ROWS + yh * SLAB
                            piece = value[row : row + SLAB, s * HEAD_DIM : (s + 1) * HEAD_DIM]
                            held[s * 8 + yh * 4 + yl * 2 + zl, zh, core] = piece.astype(BF16)


def weight_q_body(first, kept, x_own, x_oth, mix_own, mix_oth, *rest):
    keep, out, copied = rest[: kept - 2], rest[kept - 2], rest[kept - 1 : -2]
    held, sems = rest[-2:]
    steps = held.shape[0]
    copies = []
    if copied:
        for i, (source, target) in enumerate(zip((mix_own, mix_oth) + keep, copied)):
            copies.append(pltpu.make_async_copy(source, target, sems.at[steps + i]))
            copies[-1].start()
    for j in range(steps):
        cols = slice(first + j * 256, first + (j + 1) * 256)
        value = tn(x_own[...], mix_own[:, cols]) + tn(x_oth[...], mix_oth[:, cols])
        spread(value, held.at[j])
        copy = pltpu.make_async_copy(held.at[j], out.at[pl.ds(16 * j, 16)], sems.at[j])
        copy.start()
        copies.append(copy)
    for copy in copies:
        copy.wait()


def weight_q(x_own, x_oth, mix_own, mix_oth, *keep):
    width = mix_own.shape[1] // 2
    steps = width // 256
    copied = (mix_own, mix_oth) + keep if keep else ()
    return pl.pallas_call(
        functools.partial(weight_q_body, width, len(keep) + 2),
        in_specs=[VM] * (4 + len(keep)),
        out_specs=[ANY] * (1 + len(copied)),
        out_shape=[pltpu.HBM(PIECES, BF16)] + [pltpu.HBM(v.shape, v.dtype) for v in copied],
        scratch_shapes=[
            pltpu.VMEM((steps, 16) + PIECES[1:], BF16),
            pltpu.SemaphoreType.DMA((steps + len(copied),)),
        ],
        compiler_params=params(),
        cost_estimate=cost(2 * PAIR * D * width, 4 << 20),
        name="weight_q",
    )(x_own, x_oth, mix_own, mix_oth, *keep)


def weight_kv_body(x_own, x_oth, dkv, arrived, before, out, own_out, oth_out, held, sem):
    c = lax.axis_index("c")
    low = dkv[:OWN]
    skip = PAIR - HALO
    low = jnp.concatenate([low[:skip], low[skip:] + arrived[: OWN - skip].astype(F32)], axis=0)
    high = dkv[OWN:] + arrived[OWN - skip :].astype(F32)
    low = low.astype(BF16)
    high = high.astype(BF16)
    own = jnp.where(c == 0, low, high)
    oth = jnp.where(c == 0, high, low)
    own_out[...] = own
    oth_out[...] = oth
    spread(tn(x_own[...], own) + tn(x_oth[...], oth), held)
    copy = pltpu.make_async_copy(held, out.at[pl.ds(16, 16)], sem)
    copy.start()
    copy.wait()


def weight_kv(x_own, x_oth, dkv, arrived, before):
    return pl.pallas_call(
        weight_kv_body,
        in_specs=[VM] * 4 + [ANY],
        out_specs=[ANY, VM, VM],
        out_shape=[pltpu.HBM(PIECES, BF16), shape((OWN, KVCOLS)), shape((OWN, KVCOLS))],
        scratch_shapes=[pltpu.VMEM((16,) + PIECES[1:], BF16), pltpu.SemaphoreType.DMA],
        input_output_aliases={4: 0},
        compiler_params=params(),
        cost_estimate=cost(2 * PAIR * D * KVCOLS, 3 << 20),
        name="weight_kv",
    )(x_own, x_oth, dkv, arrived, before)


def ordered(first, own, oth):
    return jnp.where(
        first, jnp.concatenate([own, oth], axis=1), jnp.concatenate([oth, own], axis=1)
    )


def grad_tokens_body(wide, slim, dkv, wide_in, slim_in, dkv_in, wq, wkv, out, ctx_out, done):
    done[...] = jnp.zeros_like(done)
    first = lax.axis_index("c") == 0
    dq = jnp.concatenate([wide[:, WIDE:], slim[:, REST:]], axis=1)
    dq_in = jnp.concatenate([wide_in[:, WIDE:], slim_in[:, REST:]], axis=1)
    dq = ordered(first, dq, dq_in)
    kv = dkv[...]
    kv_in = dkv_in[...]
    keys = ordered(first, kv[:, :HEAD_DIM], kv_in[:, :HEAD_DIM])
    vals = ordered(first, kv[:, HEAD_DIM:], kv_in[:, HEAD_DIM:])
    kv_full = jnp.concatenate([keys, vals], axis=1)
    for j in range(3):
        rows = slice(j * 512, (j + 1) * 512)
        out[:, rows] = (nt(dq, wq[rows, :]) + nt(kv_full, wkv[rows, :])).astype(BF16)
    ctx = jnp.concatenate([wide[:, :WIDE], slim[:, :REST]], axis=1)
    ctx_in = jnp.concatenate([wide_in[:, :WIDE], slim_in[:, :REST]], axis=1)
    ctx_out[...] = ordered(first, ctx, ctx_in)


def grad_tokens(wide, slim, dkv, wide_in, slim_in, dkv_in, w_query, w_keyval):
    return pl.pallas_call(
        grad_tokens_body,
        in_specs=[VM] * 8,
        out_specs=[VM] * 3,
        out_shape=[shape((OWN, D)), shape((OWN, D)), shape((8, 128), F32)],
        compiler_params=params(),
        cost_estimate=cost(2 * OWN * D * 2048, 8 << 20),
        name="grad_tokens",
    )(wide, slim, dkv, wide_in, slim_in, dkv_in, w_query, w_keyval)


def sum_first_body(pieces, after, out):
    out[...] = jnp.sum(pieces[...].astype(F32), axis=0).astype(BF16)


def sum_first(pieces, after):
    return pl.pallas_call(
        sum_first_body,
        in_specs=[VM, VM],
        out_specs=VM,
        out_shape=shape(PIECES[1:]),
        compiler_params=params(),
        cost_estimate=cost(32 * 8 * SLAB * HEAD_DIM, 2 << 20),
        name="sum_first",
    )(pieces, after)


def sum_last_body(pieces, plane, out):
    out[:, :, 0] = plane[...]
    out[:, :, 1] = jnp.sum(pieces[...].astype(F32), axis=0).astype(BF16)


def sum_last(pieces, plane):
    return pl.pallas_call(
        sum_last_body,
        in_specs=[VM, VM],
        out_specs=VM,
        out_shape=shape((4, 2, 2, SLAB, HEAD_DIM)),
        compiler_params=params(),
        cost_estimate=cost(32 * 8 * SLAB * HEAD_DIM, 2 << 20),
        name="sum_last",
    )(pieces, plane)


def sum_line_body(lines, out):
    total = jnp.sum(lines[...].astype(F32), axis=0).astype(BF16)
    for s in range(8):
        out[s] = total


def sum_line(lines):
    return pl.pallas_call(
        sum_line_body,
        in_specs=[VM],
        out_specs=VM,
        out_shape=shape((8, 2, 2, SLAB, HEAD_DIM)),
        compiler_params=params(),
        name="sum_line",
    )(lines)


def finish_body(blocks, query_w, keyval_w):
    for x in range(4):
        for core in range(2):
            for part in range(2):
                rows = jnp.concatenate(
                    [blocks[2 * x, core, part].astype(F32), blocks[2 * x + 1, core, part].astype(F32)],
                    axis=0,
                ).astype(BF16)
                if part == 0 or x < 2:
                    at = (core * GROUP + part * 4 + x) * HEAD_DIM
                    query_w[:, at : at + HEAD_DIM] = rows
                else:
                    at = ((x - 2) * KV_HEADS + core) * HEAD_DIM
                    keyval_w[:, at : at + HEAD_DIM] = rows


def finish(blocks):
    return pl.pallas_call(
        finish_body,
        in_specs=[VM],
        out_specs=[VM, VM],
        out_shape=[shape((ROWS, D)), shape((ROWS, 512))],
        compiler_params=params(),
        name="finish",
    )(blocks)


def swap(value):
    return lax.ppermute(value, "c", [(0, 1), (1, 0)])


def shards(tokens, segments, w_query, w_keyval, grad_context):
    x_own = tokens[0]
    do_own = grad_context[0]
    x_oth = swap(x_own)
    do_oth = swap(do_own)
    count = 32
    ring = ("zh", "zl", "yl", "c")
    x_own, wkv_here, wq_here, q_own, kv_own = project_own(x_own, w_keyval, w_query)
    kv, kv_sent = project_kv(x_oth, kv_own, wkv_here)
    halo = lax.ppermute(kv_sent, ring, [(i, i + 2) for i in range(count - 2)])
    q = project_q(x_oth, q_own, wq_here)
    segs = segments.reshape(-1, BLOCK)
    wide_last, slim_last, dkv, low = attend_last(q, do_own, do_oth, kv, segs)
    wide, wide_oth, dkv = attend_wide(q, do_own, do_oth, kv, halo, low, wide_last, dkv)
    target = ("x", "yh", "yl", "zl")
    pieces, wide, wide_oth, dkv = weight_q(x_own, x_oth, wide, wide_oth, dkv)
    pieces = lax.all_to_all(pieces, target, 0, 0)
    slim, slim_oth, dkv, dkv_sent = attend_slim(
        q, do_own, do_oth, kv, halo, low, slim_last, dkv
    )
    arrived = lax.ppermute(dkv_sent, ring, [(i + 2, i) for i in range(count - 2)])
    (last,) = weight_q(x_own, x_oth, slim, slim_oth)
    last, dkv_own, dkv_oth = weight_kv(x_own, x_oth, dkv, arrived, last)
    last = lax.all_to_all(last, target, 0, 0)
    wide_in = swap(wide_oth)
    slim_in = swap(slim_oth)
    dkv_in = swap(dkv_oth)
    grad_in, context, done = grad_tokens(
        wide, slim, dkv_own, wide_in, slim_in, dkv_in, w_query, w_keyval
    )
    plane = sum_last(last, sum_first(pieces, done))
    lines = lax.all_to_all(plane.reshape(8, 2, SLAB, HEAD_DIM), ("zh", "c"), 0, 0)
    blocks = sum_line(lines.reshape(4, 2, 2, SLAB, HEAD_DIM))
    blocks = lax.all_to_all(blocks, ("x", "yh"), 0, 0)
    query_w, keyval_w = finish(blocks)
    return context[None], grad_in[None], query_w, keyval_w


def solution(mesh):
    fine = Mesh(mesh.devices.reshape(4, 2, 4, 2, 2, 2), ("x", "yh", "zh", "zl", "yl", "c"))
    dp = ("x", "yh")
    ctx = ("zh", "zl", "yl", "c")
    return jax.shard_map(
        shards,
        mesh=fine,
        in_specs=(P(dp, ctx, None), P(dp, None), P(), P(), P(dp, ctx, None)),
        out_specs=(P(dp, ctx, None), P(dp, ctx, None), P(ctx, None), P(ctx, None)),
        check_vma=False,
    )
```

```python
import functools

import jax
import jax.numpy as jnp
from jax import lax
from jax.experimental import pallas as pl
from jax.experimental.pallas import tpu as pltpu
from jax.sharding import Mesh
from jax.sharding import PartitionSpec as P

HEAD_DIM = 128
GROUP = 6
KV_HEADS = 2
WINDOW = 512
BLOCK = 128
HALO = WINDOW - BLOCK
OWN = 256
PAIR = 2 * OWN
KEYS = HALO + PAIR
QCOLS = GROUP * HEAD_DIM
KVCOLS = 2 * HEAD_DIM
D = 1536
DOCS = 8
SCALE = HEAD_DIM ** (-0.5)
LOG2E = 1.4426950408889634
F32 = jnp.float32
BF16 = jnp.bfloat16
NT = (((1,), (1,)), ((), ()))
TN = (((0,), (0,)), ((), ()))
ROWS = 48
PIECES = (32, 4, 2, ROWS, HEAD_DIM)
LIMIT = 24 * 1024 * 1024
VM = pl.BlockSpec(memory_space=pltpu.VMEM)
ANY = pl.BlockSpec(memory_space=pl.ANY)


def params():
    return pltpu.CompilerParams(vmem_limit_bytes=LIMIT)


def cost(flops, moved, trans=0):
    return pl.CostEstimate(flops=flops, bytes_accessed=moved, transcendentals=trans)


def shape(dims, dtype=BF16):
    return jax.ShapeDtypeStruct(dims, dtype)


def nn(a, b):
    return jnp.dot(a, b, preferred_element_type=F32)


def nt(a, b):
    return lax.dot_general(a, b, NT, preferred_element_type=F32)


def tn(a, b):
    return lax.dot_general(a, b, TN, preferred_element_type=F32)


def eye(size):
    row = lax.broadcasted_iota(jnp.int32, (size, size), 0)
    col = lax.broadcasted_iota(jnp.int32, (size, size), 1)
    return jnp.where(row == col, 1.0, 0.0).astype(BF16)


def columns(start, width=HEAD_DIM):
    return pl.ds(pl.multiple_of(start, HEAD_DIM), width)


def project_own_body(x, wkv, wq, x_here, wkv_here, wq_here, q, kv, sems):
    c = lax.axis_index("c")
    chunk = 512
    copies = [
        pltpu.make_async_copy(x, x_here, sems.at[0]),
        pltpu.make_async_copy(wkv, wkv_here, sems.at[1]),
    ]
    for j in range(D // chunk):
        rows = pl.ds(j * chunk, chunk)
        copies.append(
            pltpu.make_async_copy(
                wq.at[rows, columns(c * QCOLS, QCOLS)], wq_here.at[rows], sems.at[2 + j]
            )
        )
    for copy in copies:
        copy.start()
    copies[0].wait()
    copies[1].wait()
    kv[...] = nn(x_here[...], head_columns(wkv_here, c)).astype(BF16)
    total = jnp.zeros((OWN, QCOLS), F32)
    for j in range(D // chunk):
        rows = slice(j * chunk, (j + 1) * chunk)
        copies[2 + j].wait()
        total = total + nn(x_here[:, rows], wq_here[rows, :])
    q[...] = total.astype(BF16)


def head_columns(wkv, c):
    keys_w = wkv[:, columns(c * HEAD_DIM)]
    vals_w = wkv[:, columns((KV_HEADS + c) * HEAD_DIM)]
    return jnp.concatenate([keys_w, vals_w], axis=1)


def project_own(x, w_keyval, w_query):
    return pl.pallas_call(
        project_own_body,
        in_specs=[ANY] * 3,
        out_specs=[VM] * 5,
        out_shape=[
            pltpu.VMEM((OWN, D), BF16),
            pltpu.VMEM((D, 512), BF16),
            pltpu.VMEM((D, QCOLS), BF16),
            shape((OWN, QCOLS)),
            shape((OWN, KVCOLS)),
        ],
        scratch_shapes=[pltpu.SemaphoreType.DMA((5,))],
        compiler_params=params(),
        cost_estimate=cost(2 * OWN * D * 1024, 5 << 20),
        name="project_own",
    )(*(pltpu.with_memory_space_constraint(v, pltpu.HBM) for v in (x, w_keyval, w_query)))


def project_kv_body(x_oth, kv_own, w, kv, sent):
    c = lax.axis_index("c")
    own = kv_own[...]
    oth = nn(x_oth[...], head_columns(w, c)).astype(BF16)
    low = jnp.where(c == 0, own, oth)
    high = jnp.where(c == 0, oth, own)
    kv[:OWN] = low
    kv[OWN:] = high
    sent[: HALO - OWN] = low[PAIR - HALO :]
    sent[HALO - OWN :] = high


def project_kv(x_oth, kv_own, w_keyval):
    return pl.pallas_call(
        project_kv_body,
        in_specs=[VM] * 3,
        out_specs=[VM] * 2,
        out_shape=[shape((PAIR, KVCOLS)), shape((HALO, KVCOLS))],
        compiler_params=params(),
        cost_estimate=cost(2 * OWN * D * KVCOLS, 2 << 20),
        name="project_kv",
    )(x_oth, kv_own, w_keyval)


def project_q_body(x_oth, q_own, w, q):
    q[:OWN] = q_own[...]
    for j in range(3):
        cols = slice(j * 256, (j + 1) * 256)
        q[OWN:, cols] = nn(x_oth[...], w[:, cols]).astype(BF16)


def project_q(x_oth, q_own, w_query):
    return pl.pallas_call(
        project_q_body,
        in_specs=[VM] * 3,
        out_specs=VM,
        out_shape=shape((PAIR, QCOLS)),
        compiler_params=params(),
        cost_estimate=cost(2 * OWN * D * QCOLS, 4 << 20),
        name="project_q",
    )(x_oth, q_own, w_query)


def attend_block(b, pairs, c, q, do_own, do_oth, keys, keys_t, vals_t, low, ones):
    half, inner = b // 2, (b % 2) * BLOCK
    own = half == c
    here = slice(inner, inner + BLOCK)
    q_rows = pl.ds(pl.multiple_of(jnp.where(own, 0, OWN) + inner, BLOCK), BLOCK)
    win = slice(b * BLOCK, b * BLOCK + WINDOW)
    k_win = keys[win, :HEAD_DIM]
    v_win = keys[win, HEAD_DIM:]
    v_more = jnp.concatenate([v_win, ones[:HEAD_DIM, :HEAD_DIM]], axis=0)
    kt_win = keys_t[:, win]
    vt_win = vals_t[:, win]
    j_pos = lax.broadcasted_iota(jnp.int32, (WINDOW, BLOCK), 0)
    i_pos = lax.broadcasted_iota(jnp.int32, (WINDOW, BLOCK), 1)
    seen = (j_pos + b * BLOCK >= low[b : b + 1, :]) & (j_pos <= i_pos + HALO)
    bias = jnp.where(seen, 0.0, -1e30)
    bias = jnp.concatenate([bias, bias], axis=1)
    q2s, do2s = [], []
    for pair in pairs:
        at = pair * 256
        q_two = q[q_rows, at : at + 256]
        do_cols = columns(c * QCOLS + at, 256)
        do_two = jnp.where(own, do_own[here, do_cols], do_oth[here, do_cols])
        q2s.append(jnp.concatenate([q_two[:, :HEAD_DIM], q_two[:, HEAD_DIM:]], axis=0))
        do2s.append(jnp.concatenate([do_two[:, :HEAD_DIM], do_two[:, HEAD_DIM:]], axis=0))
    raw = [nt(k_win, q2) for q2 in q2s]
    probs = []
    for scores in raw:
        scores = scores + bias
        top = jnp.max(scores, axis=0, keepdims=True)
        expo = jnp.exp2((scores - top) * (SCALE * LOG2E))
        probs.append(expo * (1.0 / jnp.sum(expo, axis=0, keepdims=True)))
    lows = [p.astype(BF16) for p in probs]
    dps = [nt(v_more, do2) for do2 in do2s]
    ctx_ts = [nn(vt_win, p).astype(BF16) for p in lows]
    deltas = [
        jnp.sum(dp[WINDOW:] * ctx_t.astype(F32), axis=0, keepdims=True)
        for dp, ctx_t in zip(dps, ctx_ts)
    ]
    dvs = [nn(p, do2) for p, do2 in zip(lows, do2s)]
    dss = [
        (p * (dp[:WINDOW] - delta) * SCALE).astype(BF16)
        for p, dp, delta in zip(probs, dps, deltas)
    ]
    dks = [nn(ds, q2) for ds, q2 in zip(dss, q2s)]
    dq_ts = [nn(kt_win, ds).astype(BF16) for ds in dss]
    ctx_parts, dq_parts = [], []
    for ctx_t, dq_t in zip(ctx_ts, dq_ts):
        turned = nt(ones, jnp.concatenate([ctx_t, dq_t], axis=0)).astype(BF16)
        ctx_parts += [turned[:BLOCK, :HEAD_DIM], turned[BLOCK:, :HEAD_DIM]]
        dq_parts += [turned[:BLOCK, HEAD_DIM:], turned[BLOCK:, HEAD_DIM:]]
    grads = jnp.concatenate([sum(dks[1:], dks[0]), sum(dvs[1:], dvs[0])], axis=1)
    return ctx_parts, dq_parts, grads


def turn_keys(ones, keys, keys_t, vals_t, rows):
    small = ones[:HEAD_DIM, :HEAD_DIM]
    keys_t[:, rows] = nt(small, keys[rows, :HEAD_DIM]).astype(BF16)
    vals_t[:, rows] = nt(small, keys[rows, HEAD_DIM:]).astype(BF16)


def lowest_keys(chip, segs, low):
    lines = []
    for t in range(KEYS // BLOCK):
        row = chip * (PAIR // BLOCK) - HALO // BLOCK + t
        line = segs[pl.ds(jnp.maximum(row, 0), 1), :]
        lines.append(jnp.where(row >= 0, line, -1))
    own = jnp.concatenate(lines[HALO // BLOCK :], axis=0)
    lines = jnp.concatenate(lines, axis=0)
    first = jnp.zeros_like(own)
    for d in range(DOCS):
        first = jnp.where(own == d, jnp.sum(jnp.where(lines < d, 1, 0)), first)
    low[: PAIR // BLOCK, :] = first


KEY_SCRATCH = [
    pltpu.VMEM((KEYS, KVCOLS), BF16),
    pltpu.VMEM((HEAD_DIM, KEYS), BF16),
    pltpu.VMEM((HEAD_DIM, KEYS), BF16),
]


def attend_last_body(q, do_own, do_oth, kv, segs, mix, dkv, low, keys, keys_t, vals_t):
    c = lax.axis_index("c")
    chip = lax.axis_index(("zh", "zl", "yl"))
    ones = eye(256)
    keys[HALO:] = kv[...]
    turn_keys(ones, keys, keys_t, vals_t, slice(HALO, KEYS))
    lowest_keys(chip, segs, low)
    ctx, dq, dkv[...] = attend_block(
        3, range(3), c, q, do_own, do_oth, keys, keys_t, vals_t, low, ones
    )
    mix[...] = jnp.concatenate(ctx + dq, axis=1)


def attend_last(q, do_own, do_oth, kv, segs):
    return pl.pallas_call(
        attend_last_body,
        in_specs=[VM] * 5,
        out_specs=[VM] * 3,
        out_shape=[
            shape((BLOCK, 2 * QCOLS)),
            shape((WINDOW, KVCOLS), F32),
            shape((8, BLOCK), jnp.int32),
        ],
        scratch_shapes=KEY_SCRATCH,
        compiler_params=params(),
        cost_estimate=cost(2 * BLOCK * WINDOW * QCOLS * 6, 3 << 20, BLOCK * WINDOW * GROUP),
        name="attend_last",
    )(q, do_own, do_oth, kv, segs)


def put(c, b, mix_own, mix_oth, value):
    own = b // 2 == c
    here = slice((b % 2) * BLOCK, (b % 2 + 1) * BLOCK)

    @pl.when(own)
    def _():
        mix_own[here, :] = value

    @pl.when(jnp.logical_not(own))
    def _():
        mix_oth[here, :] = value


def attend_body(q, do_own, do_oth, kv, halo, low, mix_last, dkv_last, *rest):
    mix_own, mix_oth, dkv_out, sent, keys, keys_t, vals_t, dkv = rest
    c = lax.axis_index("c")
    ones = eye(256)
    keys[:HALO] = halo[...]
    keys[HALO:] = kv[...]
    turn_keys(ones, keys, keys_t, vals_t, slice(0, KEYS))
    dkv[:HALO] = jnp.zeros((HALO, KVCOLS), F32)
    dkv[HALO:] = dkv_last[...]
    put(c, 3, mix_own, mix_oth, mix_last[...])
    for b in range(3):
        ctx, dq, grads = attend_block(
            b, range(3), c, q, do_own, do_oth, keys, keys_t, vals_t, low, ones
        )
        dkv[b * BLOCK : b * BLOCK + WINDOW, :] += grads
        put(c, b, mix_own, mix_oth, jnp.concatenate(ctx + dq, axis=1))
    sent[...] = dkv[:HALO, :].astype(BF16)
    dkv_out[...] = dkv[HALO:, :]


def attend(q, do_own, do_oth, kv, halo, low, mix_last, dkv_last):
    return pl.pallas_call(
        attend_body,
        in_specs=[VM] * 8,
        out_specs=[VM] * 4,
        out_shape=[
            shape((OWN, 2 * QCOLS)),
            shape((OWN, 2 * QCOLS)),
            shape((PAIR, KVCOLS), F32),
            shape((HALO, KVCOLS)),
        ],
        scratch_shapes=KEY_SCRATCH + [pltpu.VMEM((KEYS, KVCOLS), F32)],
        compiler_params=params(),
        cost_estimate=cost(3 * 2 * BLOCK * WINDOW * QCOLS * 6, 5 << 20, 3 * BLOCK * WINDOW * 6),
        name="attend",
    )(q, do_own, do_oth, kv, halo, low, mix_last, dkv_last)


def spread(value, held):
    for s in range(2):
        for y in range(2):
            for zl in range(2):
                for zh in range(4):
                    for core in range(2):
                        row = (zh * 2 + zl) * 192 + y * 96 + core * ROWS
                        piece = value[row : row + ROWS, s * HEAD_DIM : (s + 1) * HEAD_DIM]
                        held[s * 4 + y * 2 + zl, zh, core] = piece.astype(BF16)


def weight_q_body(x_own, x_oth, mix_own, mix_oth, out, held, sems):
    copies = []
    for j in range(3):
        cols = slice(QCOLS + j * 256, QCOLS + (j + 1) * 256)
        value = tn(x_own[...], mix_own[:, cols]) + tn(x_oth[...], mix_oth[:, cols])
        spread(value, held.at[j])
        copy = pltpu.make_async_copy(held.at[j], out.at[pl.ds(8 * j, 8)], sems.at[j])
        copy.start()
        copies.append(copy)
    for copy in copies:
        copy.wait()


def weight_q(x_own, x_oth, mix_own, mix_oth):
    return pl.pallas_call(
        weight_q_body,
        in_specs=[VM] * 4,
        out_specs=ANY,
        out_shape=pltpu.HBM(PIECES, BF16),
        scratch_shapes=[
            pltpu.VMEM((3, 8) + PIECES[1:], BF16),
            pltpu.SemaphoreType.DMA((3,)),
        ],
        compiler_params=params(),
        cost_estimate=cost(2 * PAIR * D * QCOLS, 4 << 20),
        name="weight_q",
    )(x_own, x_oth, mix_own, mix_oth)


def weight_kv_body(x_own, x_oth, dkv, arrived, before, out, own_out, oth_out, held, sem):
    c = lax.axis_index("c")
    low = dkv[:OWN]
    skip = PAIR - HALO
    low = jnp.concatenate([low[:skip], low[skip:] + arrived[: OWN - skip].astype(F32)], axis=0)
    high = dkv[OWN:] + arrived[OWN - skip :].astype(F32)
    low = low.astype(BF16)
    high = high.astype(BF16)
    own = jnp.where(c == 0, low, high)
    oth = jnp.where(c == 0, high, low)
    own_out[...] = own
    oth_out[...] = oth
    spread(tn(x_own[...], own) + tn(x_oth[...], oth), held)
    copy = pltpu.make_async_copy(held, out.at[pl.ds(24, 8)], sem)
    copy.start()
    copy.wait()


def weight_kv(x_own, x_oth, dkv, arrived, before):
    return pl.pallas_call(
        weight_kv_body,
        in_specs=[VM] * 4 + [ANY],
        out_specs=[ANY, VM, VM],
        out_shape=[pltpu.HBM(PIECES, BF16), shape((OWN, KVCOLS)), shape((OWN, KVCOLS))],
        scratch_shapes=[pltpu.VMEM((8,) + PIECES[1:], BF16), pltpu.SemaphoreType.DMA],
        input_output_aliases={4: 0},
        compiler_params=params(),
        cost_estimate=cost(2 * PAIR * D * KVCOLS, 3 << 20),
        name="weight_kv",
    )(x_own, x_oth, dkv, arrived, before)


def ordered(first, own, oth):
    return jnp.where(
        first, jnp.concatenate([own, oth], axis=1), jnp.concatenate([oth, own], axis=1)
    )


def grad_tokens_body(mix, dkv, mix_in, dkv_in, wq, wkv, out, ctx_out, done):
    done[...] = jnp.zeros_like(done)
    first = lax.axis_index("c") == 0
    dq = ordered(first, mix[:, QCOLS:], mix_in[:, QCOLS:])
    kv = dkv[...]
    kv_in = dkv_in[...]
    keys = ordered(first, kv[:, :HEAD_DIM], kv_in[:, :HEAD_DIM])
    vals = ordered(first, kv[:, HEAD_DIM:], kv_in[:, HEAD_DIM:])
    kv_full = jnp.concatenate([keys, vals], axis=1)
    for j in range(3):
        rows = slice(j * 512, (j + 1) * 512)
        out[:, rows] = (nt(dq, wq[rows, :]) + nt(kv_full, wkv[rows, :])).astype(BF16)
    ctx_out[...] = ordered(first, mix[:, :QCOLS], mix_in[:, :QCOLS])


def grad_tokens(mix, dkv, mix_in, dkv_in, w_query, w_keyval):
    return pl.pallas_call(
        grad_tokens_body,
        in_specs=[VM] * 6,
        out_specs=[VM] * 3,
        out_shape=[shape((OWN, D)), shape((OWN, D)), shape((8, 128), F32)],
        compiler_params=params(),
        cost_estimate=cost(2 * OWN * D * 2048, 8 << 20),
        name="grad_tokens",
    )(mix, dkv, mix_in, dkv_in, w_query, w_keyval)


def sum_plane_body(pieces, after, out):
    out[...] = jnp.sum(pieces[...].astype(F32), axis=0).astype(BF16)


def sum_plane(pieces, after):
    return pl.pallas_call(
        sum_plane_body,
        in_specs=[VM, VM],
        out_specs=VM,
        out_shape=shape(PIECES[1:]),
        compiler_params=params(),
        cost_estimate=cost(32 * 8 * ROWS * HEAD_DIM, 3 << 20),
        name="sum_plane",
    )(pieces, after)


def sum_line_body(lines, out):
    total = jnp.sum(lines[...].astype(F32), axis=0).astype(BF16)
    for s in range(8):
        out[s] = total


def sum_line(lines):
    return pl.pallas_call(
        sum_line_body,
        in_specs=[VM],
        out_specs=VM,
        out_shape=shape((8, 2, ROWS, HEAD_DIM)),
        compiler_params=params(),
        name="sum_line",
    )(lines)


def finish_body(blocks, query_w, keyval_w):
    for s in range(8):
        for core in range(2):
            if s < GROUP:
                at = (core * GROUP + s) * HEAD_DIM
                query_w[:, at : at + HEAD_DIM] = blocks[s, core]
            else:
                at = ((s - GROUP) * KV_HEADS + core) * HEAD_DIM
                keyval_w[:, at : at + HEAD_DIM] = blocks[s, core]


def finish(blocks):
    return pl.pallas_call(
        finish_body,
        in_specs=[VM],
        out_specs=[VM, VM],
        out_shape=[shape((ROWS, D)), shape((ROWS, 512))],
        compiler_params=params(),
        name="finish",
    )(blocks)


def swap(value):
    return lax.ppermute(value, "c", [(0, 1), (1, 0)])


def shards(tokens, segments, w_query, w_keyval, grad_context):
    x_own = tokens[0]
    do_own = grad_context[0]
    x_oth = swap(x_own)
    do_oth = swap(do_own)
    count = 32
    ring = ("zh", "zl", "yl", "c")
    x_own, wkv_here, wq_here, q_own, kv_own = project_own(x_own, w_keyval, w_query)
    kv, kv_sent = project_kv(x_oth, kv_own, wkv_here)
    halo = lax.ppermute(kv_sent, ring, [(i, i + 2) for i in range(count - 2)])
    q = project_q(x_oth, q_own, wq_here)
    segs = segments.reshape(-1, BLOCK)
    mix_last, dkv_last, low = attend_last(q, do_own, do_oth, kv, segs)
    mix, mix_oth, dkv, dkv_sent = attend(q, do_own, do_oth, kv, halo, low, mix_last, dkv_last)
    arrived = lax.ppermute(dkv_sent, ring, [(i + 2, i) for i in range(count - 2)])
    pieces = weight_q(x_own, x_oth, mix, mix_oth)
    pieces, dkv_own, dkv_oth = weight_kv(x_own, x_oth, dkv, arrived, pieces)
    pieces = lax.all_to_all(pieces, ("x", "yh", "yl", "zl"), 0, 0)
    mix_in = swap(mix_oth)
    dkv_in = swap(dkv_oth)
    grad_in, context, done = grad_tokens(mix, dkv_own, mix_in, dkv_in, w_query, w_keyval)
    plane = sum_plane(pieces, done)
    lines = lax.all_to_all(plane.reshape(8, ROWS, HEAD_DIM), ("zh", "c"), 0, 0)
    blocks = sum_line(lines.reshape(4, 2, ROWS, HEAD_DIM))
    blocks = lax.all_to_all(blocks, ("x", "yh"), 0, 0)
    query_w, keyval_w = finish(blocks)
    return context[None], grad_in[None], query_w, keyval_w


def solution(mesh):
    fine = Mesh(mesh.devices.reshape(4, 2, 4, 2, 2, 2), ("x", "yh", "zh", "zl", "yl", "c"))
    dp = ("x", "yh")
    ctx = ("zh", "zl", "yl", "c")
    return jax.shard_map(
        shards,
        mesh=fine,
        in_specs=(P(dp, ctx, None), P(dp, None), P(), P(), P(dp, ctx, None)),
        out_specs=(P(dp, ctx, None), P(dp, ctx, None), P(ctx, None), P(ctx, None)),
        check_vma=False,
    )
```

```python
import functools

import jax
import jax.numpy as jnp
from jax import lax
from jax.experimental import pallas as pl
from jax.experimental.pallas import tpu as pltpu
from jax.sharding import Mesh
from jax.sharding import PartitionSpec as P

HEAD_DIM = 128
GROUP = 6
KV_HEADS = 2
WINDOW = 512
BLOCK = 128
HALO = WINDOW - BLOCK
OWN = 256
PAIR = 2 * OWN
KEYS = HALO + PAIR
QCOLS = GROUP * HEAD_DIM
KVCOLS = 2 * HEAD_DIM
D = 1536
DOCS = 8
SCALE = HEAD_DIM ** (-0.5)
LOG2E = 1.4426950408889634
F32 = jnp.float32
BF16 = jnp.bfloat16
NT = (((1,), (1,)), ((), ()))
TN = (((0,), (0,)), ((), ()))
ROWS = 48
KEEP = 384
PIECES = (16, 4, 2, ROWS, HEAD_DIM)
LIMIT = 24 * 1024 * 1024
VM = pl.BlockSpec(memory_space=pltpu.VMEM)
ANY = pl.BlockSpec(memory_space=pl.ANY)


def params():
    return pltpu.CompilerParams(vmem_limit_bytes=LIMIT)


def cost(flops, moved, trans=0):
    return pl.CostEstimate(flops=flops, bytes_accessed=moved, transcendentals=trans)


def shape(dims, dtype=BF16):
    return jax.ShapeDtypeStruct(dims, dtype)


def nn(a, b):
    return jnp.dot(a, b, preferred_element_type=F32)


def nt(a, b):
    return lax.dot_general(a, b, NT, preferred_element_type=F32)


def tn(a, b):
    return lax.dot_general(a, b, TN, preferred_element_type=F32)


def eye(size):
    row = lax.broadcasted_iota(jnp.int32, (size, size), 0)
    col = lax.broadcasted_iota(jnp.int32, (size, size), 1)
    return jnp.where(row == col, 1.0, 0.0).astype(BF16)


def columns(start, width=HEAD_DIM):
    return pl.ds(pl.multiple_of(start, HEAD_DIM), width)


def project_own_body(x, wkv, wq, x_here, wkv_here, wq_here, q, kv, sems):
    c = lax.axis_index("c")
    chunk = 512
    copies = [
        pltpu.make_async_copy(x, x_here, sems.at[0]),
        pltpu.make_async_copy(wkv, wkv_here, sems.at[1]),
    ]
    for j in range(D // chunk):
        rows = pl.ds(j * chunk, chunk)
        copies.append(
            pltpu.make_async_copy(
                wq.at[rows, columns(c * QCOLS, QCOLS)], wq_here.at[rows], sems.at[2 + j]
            )
        )
    for copy in copies:
        copy.start()
    copies[0].wait()
    copies[1].wait()
    kv[...] = nn(x_here[...], head_columns(wkv_here, c)).astype(BF16)
    total = jnp.zeros((OWN, QCOLS), F32)
    for j in range(D // chunk):
        rows = slice(j * chunk, (j + 1) * chunk)
        copies[2 + j].wait()
        total = total + nn(x_here[:, rows], wq_here[rows, :])
    q[...] = total.astype(BF16)


def head_columns(wkv, c):
    keys_w = wkv[:, columns(c * HEAD_DIM)]
    vals_w = wkv[:, columns((KV_HEADS + c) * HEAD_DIM)]
    return jnp.concatenate([keys_w, vals_w], axis=1)


def project_own(x, w_keyval, w_query):
    return pl.pallas_call(
        project_own_body,
        in_specs=[ANY] * 3,
        out_specs=[VM] * 5,
        out_shape=[
            pltpu.VMEM((OWN, D), BF16),
            pltpu.VMEM((D, 512), BF16),
            pltpu.VMEM((D, QCOLS), BF16),
            shape((OWN, QCOLS)),
            shape((OWN, KVCOLS)),
        ],
        scratch_shapes=[pltpu.SemaphoreType.DMA((5,))],
        compiler_params=params(),
        cost_estimate=cost(2 * OWN * D * 1024, 5 << 20),
        name="project_own",
    )(*(pltpu.with_memory_space_constraint(v, pltpu.HBM) for v in (x, w_keyval, w_query)))


def project_kv_body(x_oth, kv_own, w, kv, sent):
    c = lax.axis_index("c")
    own = kv_own[...]
    oth = nn(x_oth[...], head_columns(w, c)).astype(BF16)
    low = jnp.where(c == 0, own, oth)
    high = jnp.where(c == 0, oth, own)
    kv[:OWN] = low
    kv[OWN:] = high
    sent[: HALO - OWN] = low[PAIR - HALO :]
    sent[HALO - OWN :] = high


def project_kv(x_oth, kv_own, w_keyval):
    return pl.pallas_call(
        project_kv_body,
        in_specs=[VM] * 3,
        out_specs=[VM] * 2,
        out_shape=[shape((PAIR, KVCOLS)), shape((HALO, KVCOLS))],
        compiler_params=params(),
        cost_estimate=cost(2 * OWN * D * KVCOLS, 2 << 20),
        name="project_kv",
    )(x_oth, kv_own, w_keyval)


def project_q_body(x_oth, q_own, w, q):
    q[:OWN] = q_own[...]
    for j in range(3):
        cols = slice(j * 256, (j + 1) * 256)
        q[OWN:, cols] = nn(x_oth[...], w[:, cols]).astype(BF16)


def project_q(x_oth, q_own, w_query):
    return pl.pallas_call(
        project_q_body,
        in_specs=[VM] * 3,
        out_specs=VM,
        out_shape=shape((PAIR, QCOLS)),
        compiler_params=params(),
        cost_estimate=cost(2 * OWN * D * QCOLS, 4 << 20),
        name="project_q",
    )(x_oth, q_own, w_query)


def attend_block(b, pairs, c, q, do_own, do_oth, keys, keys_t, vals_t, low, ones):
    half, inner = b // 2, (b % 2) * BLOCK
    own = half == c
    here = slice(inner, inner + BLOCK)
    q_rows = pl.ds(pl.multiple_of(jnp.where(own, 0, OWN) + inner, BLOCK), BLOCK)
    win = slice(b * BLOCK, b * BLOCK + WINDOW)
    k_win = keys[win, :HEAD_DIM]
    v_win = keys[win, HEAD_DIM:]
    v_more = jnp.concatenate([v_win, ones[:HEAD_DIM, :HEAD_DIM]], axis=0)
    kt_win = keys_t[:, win]
    vt_win = vals_t[:, win]
    j_pos = lax.broadcasted_iota(jnp.int32, (WINDOW, BLOCK), 0)
    i_pos = lax.broadcasted_iota(jnp.int32, (WINDOW, BLOCK), 1)
    seen = (j_pos + b * BLOCK >= low[b : b + 1, :]) & (j_pos <= i_pos + HALO)
    bias = jnp.where(seen, 0.0, -1e30)
    bias = jnp.concatenate([bias, bias], axis=1)
    q2s, do2s = [], []
    for pair in pairs:
        at = pair * 256
        q_two = q[q_rows, at : at + 256]
        do_cols = columns(c * QCOLS + at, 256)
        do_two = jnp.where(own, do_own[here, do_cols], do_oth[here, do_cols])
        q2s.append(jnp.concatenate([q_two[:, :HEAD_DIM], q_two[:, HEAD_DIM:]], axis=0))
        do2s.append(jnp.concatenate([do_two[:, :HEAD_DIM], do_two[:, HEAD_DIM:]], axis=0))
    raw = [nt(k_win, q2) for q2 in q2s]
    probs = []
    for scores in raw:
        scores = scores + bias
        top = jnp.max(scores, axis=0, keepdims=True)
        expo = jnp.exp2((scores - top) * (SCALE * LOG2E))
        probs.append(expo * (1.0 / jnp.sum(expo, axis=0, keepdims=True)))
    lows = [p.astype(BF16) for p in probs]
    dps = [nt(v_more, do2) for do2 in do2s]
    ctx_ts = [nn(vt_win, p).astype(BF16) for p in lows]
    deltas = [
        jnp.sum(dp[WINDOW:] * ctx_t.astype(F32), axis=0, keepdims=True)
        for dp, ctx_t in zip(dps, ctx_ts)
    ]
    dvs = [nn(p, do2) for p, do2 in zip(lows, do2s)]
    dss = [
        (p * (dp[:WINDOW] - delta) * SCALE).astype(BF16)
        for p, dp, delta in zip(probs, dps, deltas)
    ]
    dks = [nn(ds, q2) for ds, q2 in zip(dss, q2s)]
    dq_ts = [nn(kt_win, ds).astype(BF16) for ds in dss]
    ctx_parts, dq_parts = [], []
    for ctx_t, dq_t in zip(ctx_ts, dq_ts):
        turned = nt(ones, jnp.concatenate([ctx_t, dq_t], axis=0)).astype(BF16)
        ctx_parts += [turned[:BLOCK, :HEAD_DIM], turned[BLOCK:, :HEAD_DIM]]
        dq_parts += [turned[:BLOCK, HEAD_DIM:], turned[BLOCK:, HEAD_DIM:]]
    grads = jnp.concatenate([sum(dks[1:], dks[0]), sum(dvs[1:], dvs[0])], axis=1)
    return ctx_parts, dq_parts, grads


def turn_keys(ones, keys, keys_t, vals_t, rows):
    small = ones[:HEAD_DIM, :HEAD_DIM]
    keys_t[:, rows] = nt(small, keys[rows, :HEAD_DIM]).astype(BF16)
    vals_t[:, rows] = nt(small, keys[rows, HEAD_DIM:]).astype(BF16)


def lowest_keys(chip, segs, low):
    lines = []
    for t in range(KEYS // BLOCK):
        row = chip * (PAIR // BLOCK) - HALO // BLOCK + t
        line = segs[pl.ds(jnp.maximum(row, 0), 1), :]
        lines.append(jnp.where(row >= 0, line, -1))
    own = jnp.concatenate(lines[HALO // BLOCK :], axis=0)
    lines = jnp.concatenate(lines, axis=0)
    first = jnp.zeros_like(own)
    for d in range(DOCS):
        first = jnp.where(own == d, jnp.sum(jnp.where(lines < d, 1, 0)), first)
    low[: PAIR // BLOCK, :] = first


KEY_SCRATCH = [
    pltpu.VMEM((KEYS, KVCOLS), BF16),
    pltpu.VMEM((HEAD_DIM, KEYS), BF16),
    pltpu.VMEM((HEAD_DIM, KEYS), BF16),
]


def attend_last_body(q, do_own, do_oth, kv, segs, mix, dkv, low, keys, keys_t, vals_t):
    c = lax.axis_index("c")
    chip = lax.axis_index(("zh", "zl", "yl"))
    ones = eye(256)
    keys[HALO:] = kv[...]
    turn_keys(ones, keys, keys_t, vals_t, slice(HALO, KEYS))
    lowest_keys(chip, segs, low)
    ctx, dq, dkv[...] = attend_block(
        3, range(3), c, q, do_own, do_oth, keys, keys_t, vals_t, low, ones
    )
    mix[...] = jnp.concatenate(ctx + dq, axis=1)


def attend_last(q, do_own, do_oth, kv, segs):
    return pl.pallas_call(
        attend_last_body,
        in_specs=[VM] * 5,
        out_specs=[VM] * 3,
        out_shape=[
            shape((BLOCK, 2 * QCOLS)),
            shape((WINDOW, KVCOLS), F32),
            shape((8, BLOCK), jnp.int32),
        ],
        scratch_shapes=KEY_SCRATCH,
        compiler_params=params(),
        cost_estimate=cost(2 * BLOCK * WINDOW * QCOLS * 6, 3 << 20, BLOCK * WINDOW * GROUP),
        name="attend_last",
    )(q, do_own, do_oth, kv, segs)


def put(b, outs, value):
    mix_own, mix_oth, kept, sent = outs
    own = b // 2 == lax.axis_index("c")
    here = slice((b % 2) * BLOCK, (b % 2 + 1) * BLOCK)

    @pl.when(own)
    def _():
        mix_own[here, :] = value

    @pl.when(jnp.logical_not(own))
    def _():
        mix_oth[here, :] = value

    first = lax.axis_index("xl") == 0
    rows = pl.ds(pl.multiple_of(jnp.where(own, 0, OWN) + (b % 2) * BLOCK, BLOCK), BLOCK)
    one = value[:, QCOLS : QCOLS + KEEP]
    two = value[:, QCOLS + KEEP :]
    kept[rows, :] = jnp.where(first, one, two)
    sent[rows, :] = jnp.where(first, two, one)


def attend_body(q, do_own, do_oth, kv, halo, low, mix_last, dkv_last, *rest):
    *outs, dkv_out, dkv_sent, keys, keys_t, vals_t, dkv = rest
    c = lax.axis_index("c")
    ones = eye(256)
    keys[:HALO] = halo[...]
    keys[HALO:] = kv[...]
    turn_keys(ones, keys, keys_t, vals_t, slice(0, KEYS))
    dkv[:HALO] = jnp.zeros((HALO, KVCOLS), F32)
    dkv[HALO:] = dkv_last[...]
    put(3, outs, mix_last[...])
    for b in range(3):
        ctx, dq, grads = attend_block(
            b, range(3), c, q, do_own, do_oth, keys, keys_t, vals_t, low, ones
        )
        dkv[b * BLOCK : b * BLOCK + WINDOW, :] += grads
        put(b, outs, jnp.concatenate(ctx + dq, axis=1))
    dkv_sent[...] = dkv[:HALO, :].astype(BF16)
    dkv_out[...] = dkv[HALO:, :]


def attend(q, do_own, do_oth, kv, halo, low, mix_last, dkv_last):
    return pl.pallas_call(
        attend_body,
        in_specs=[VM] * 8,
        out_specs=[VM] * 6,
        out_shape=[
            shape((OWN, 2 * QCOLS)),
            shape((OWN, 2 * QCOLS)),
            shape((PAIR, KEEP)),
            shape((PAIR, KEEP)),
            shape((PAIR, KVCOLS), F32),
            shape((HALO, KVCOLS)),
        ],
        scratch_shapes=KEY_SCRATCH + [pltpu.VMEM((KEYS, KVCOLS), F32)],
        compiler_params=params(),
        cost_estimate=cost(3 * 2 * BLOCK * WINDOW * QCOLS * 6, 5 << 20, 3 * BLOCK * WINDOW * 6),
        name="attend",
    )(q, do_own, do_oth, kv, halo, low, mix_last, dkv_last)


def total_kv_body(dkv, arrived, own_out, oth_out, kept, sent):
    c = lax.axis_index("c")
    low = dkv[:OWN]
    skip = PAIR - HALO
    low = jnp.concatenate([low[:skip], low[skip:] + arrived[: OWN - skip].astype(F32)], axis=0)
    high = dkv[OWN:] + arrived[OWN - skip :].astype(F32)
    low = low.astype(BF16)
    high = high.astype(BF16)
    own = jnp.where(c == 0, low, high)
    oth = jnp.where(c == 0, high, low)
    own_out[...] = own
    oth_out[...] = oth
    first = lax.axis_index("xl") == 0
    for rows, value in ((slice(0, OWN), own), (slice(OWN, PAIR), oth)):
        kept[rows, :] = jnp.where(first, value[:, :HEAD_DIM], value[:, HEAD_DIM:])
        sent[rows, :] = jnp.where(first, value[:, HEAD_DIM:], value[:, :HEAD_DIM])


def total_kv(dkv, arrived):
    return pl.pallas_call(
        total_kv_body,
        in_specs=[VM] * 2,
        out_specs=[VM] * 4,
        out_shape=[shape((OWN, KVCOLS))] * 2 + [shape((PAIR, HEAD_DIM))] * 2,
        compiler_params=params(),
        cost_estimate=cost(1, 1),
        name="total_kv",
    )(dkv, arrived)


def chunks(width):
    return [slice(at, min(at + 256, width)) for at in range(0, width, 256)]


def weight_near_body(x_own, x_oth, g, out):
    for cols in chunks(g.shape[1]):
        out[:, cols] = tn(x_own[...], g[:OWN, cols]) + tn(x_oth[...], g[OWN:, cols])


def weight_near(x_own, x_oth, g):
    width = g.shape[1]
    return pl.pallas_call(
        weight_near_body,
        in_specs=[VM] * 3,
        out_specs=VM,
        out_shape=shape((D, width), F32),
        compiler_params=params(),
        cost_estimate=cost(20 * PAIR * D * width, 30 << 20),
        name="weight_near",
    )(x_own, x_oth, g)


def relay_body(value, after, out):
    del value, after, out


def relay(value, after):
    return pl.pallas_call(
        relay_body,
        in_specs=[VM] * 2,
        out_specs=VM,
        out_shape=shape(value.shape),
        input_output_aliases={0: 0},
        compiler_params=params(),
        cost_estimate=cost(1, 1),
        name="relay",
    )(value, after)


def spread(value, held, block):
    for s in range(value.shape[1] // HEAD_DIM):
        for y in range(2):
            for zl in range(2):
                for zh in range(4):
                    for core in range(2):
                        row = (zh * 2 + zl) * 192 + y * 96 + core * ROWS
                        piece = value[row : row + ROWS, s * HEAD_DIM : (s + 1) * HEAD_DIM]
                        held[(block + s) * 4 + y * 2 + zl, zh, core] = piece.astype(BF16)


def weight_far_body(start, x_own, x_oth, near, g, *rest):
    out, held, sems = rest[-3:]
    copies = []
    for i, cols in enumerate(chunks(g.shape[1])):
        value = near[:, cols] + tn(x_own[...], g[:OWN, cols]) + tn(x_oth[...], g[OWN:, cols])
        spread(value, held, 2 * i)
        count = (cols.stop - cols.start) // 32
        copies.append(
            pltpu.make_async_copy(
                held.at[pl.ds(8 * i, count)], out.at[pl.ds(start + 8 * i, count)], sems.at[i]
            )
        )
        copies[-1].start()
    for copy in copies:
        copy.wait()


def weight_far(x_own, x_oth, near, g, before=None):
    width = g.shape[1]
    extra = [] if before is None else [before]
    return pl.pallas_call(
        functools.partial(weight_far_body, 0 if before is None else 12),
        in_specs=[VM] * 4 + [ANY] * len(extra),
        out_specs=ANY,
        out_shape=pltpu.HBM(PIECES, BF16),
        scratch_shapes=[
            pltpu.VMEM((width // 32,) + PIECES[1:], BF16),
            pltpu.SemaphoreType.DMA((2,)),
        ],
        input_output_aliases={4: 0} if extra else {},
        compiler_params=params(),
        cost_estimate=cost(2 * PAIR * D * width, 4 << 20),
        name="weight_far",
    )(x_own, x_oth, near, g, *extra)


def ordered(first, own, oth):
    return jnp.where(
        first, jnp.concatenate([own, oth], axis=1), jnp.concatenate([oth, own], axis=1)
    )


def grad_tokens_body(mix, dkv, mix_in, dkv_in, wq, wkv, out, ctx_out, done):
    done[...] = jnp.zeros_like(done)
    first = lax.axis_index("c") == 0
    dq = ordered(first, mix[:, QCOLS:], mix_in[:, QCOLS:])
    kv = dkv[...]
    kv_in = dkv_in[...]
    keys = ordered(first, kv[:, :HEAD_DIM], kv_in[:, :HEAD_DIM])
    vals = ordered(first, kv[:, HEAD_DIM:], kv_in[:, HEAD_DIM:])
    kv_full = jnp.concatenate([keys, vals], axis=1)
    for j in range(3):
        rows = slice(j * 512, (j + 1) * 512)
        out[:, rows] = (nt(dq, wq[rows, :]) + nt(kv_full, wkv[rows, :])).astype(BF16)
    ctx_out[...] = ordered(first, mix[:, :QCOLS], mix_in[:, :QCOLS])


def grad_tokens(mix, dkv, mix_in, dkv_in, w_query, w_keyval):
    return pl.pallas_call(
        grad_tokens_body,
        in_specs=[VM] * 6,
        out_specs=[VM] * 3,
        out_shape=[shape((OWN, D)), shape((OWN, D)), shape((8, 128), F32)],
        compiler_params=params(),
        cost_estimate=cost(2 * OWN * D * 2048, 8 << 20),
        name="grad_tokens",
    )(mix, dkv, mix_in, dkv_in, w_query, w_keyval)


def sum_plane_body(pieces, after, out):
    out[...] = jnp.sum(pieces[...].astype(F32), axis=0).astype(BF16)


def sum_plane(pieces, after):
    return pl.pallas_call(
        sum_plane_body,
        in_specs=[VM, VM],
        out_specs=VM,
        out_shape=shape(PIECES[1:]),
        compiler_params=params(),
        cost_estimate=cost(16 * 8 * ROWS * HEAD_DIM, 2 << 20),
        name="sum_plane",
    )(pieces, after)


def sum_line_body(lines, out):
    total = jnp.sum(lines[...].astype(F32), axis=0).astype(BF16)
    for s in range(8):
        out[s] = total


def sum_line(lines):
    return pl.pallas_call(
        sum_line_body,
        in_specs=[VM],
        out_specs=VM,
        out_shape=shape((8, 2, ROWS, HEAD_DIM)),
        compiler_params=params(),
        name="sum_line",
    )(lines)


def finish_body(blocks, query_w, keyval_w):
    for xh in range(2):
        for xl in range(2):
            for yh in range(2):
                for core in range(2):
                    rows = blocks[(xh * 2 + xl) * 2 + yh, core]
                    block = xh * 2 + yh
                    if block < 3:
                        at = (core * GROUP + xl * 3 + block) * HEAD_DIM
                        query_w[:, at : at + HEAD_DIM] = rows
                    else:
                        at = (xl * KV_HEADS + core) * HEAD_DIM
                        keyval_w[:, at : at + HEAD_DIM] = rows


def finish(blocks):
    return pl.pallas_call(
        finish_body,
        in_specs=[VM],
        out_specs=[VM, VM],
        out_shape=[shape((ROWS, D)), shape((ROWS, 512))],
        compiler_params=params(),
        name="finish",
    )(blocks)


def swap(value, axis="c"):
    return lax.ppermute(value, axis, [(0, 1), (1, 0)])


def shards(tokens, segments, w_query, w_keyval, grad_context):
    x_own = tokens[0]
    do_own = grad_context[0]
    x_oth = swap(x_own)
    do_oth = swap(do_own)
    far_own = swap(x_own, "xl")
    count = 32
    ring = ("zh", "zl", "yl", "c")
    x_own, wkv_here, wq_here, q_own, kv_own = project_own(x_own, w_keyval, w_query)
    kv, kv_sent = project_kv(x_oth, kv_own, wkv_here)
    halo = lax.ppermute(kv_sent, ring, [(i, i + 2) for i in range(count - 2)])
    q = project_q(x_oth, q_own, wq_here)
    segs = segments.reshape(-1, BLOCK)
    mix_last, dkv_last, low = attend_last(q, do_own, do_oth, kv, segs)
    mix, mix_oth, kept, sent, dkv, dkv_sent = attend(
        q, do_own, do_oth, kv, halo, low, mix_last, dkv_last
    )
    arrived = lax.ppermute(dkv_sent, ring, [(i + 2, i) for i in range(count - 2)])
    far = swap(sent, "xl")
    far_own = relay(far_own, kept)
    far_oth = swap(far_own)
    near = weight_near(x_own, x_oth, kept)
    dkv_own, dkv_oth, kept_kv, sent_kv = total_kv(dkv, arrived)
    far_kv = swap(sent_kv, "xl")
    near_kv = weight_near(x_own, x_oth, kept_kv)
    pieces = weight_far(far_own, far_oth, near, far)
    pieces = weight_far(far_own, far_oth, near_kv, far_kv, pieces)
    pieces = lax.all_to_all(pieces, ("xh", "yh", "yl", "zl"), 0, 0)
    mix_in = swap(mix_oth)
    dkv_in = swap(dkv_oth)
    grad_in, context, done = grad_tokens(mix, dkv_own, mix_in, dkv_in, w_query, w_keyval)
    plane = sum_plane(pieces, done)
    lines = lax.all_to_all(plane.reshape(8, ROWS, HEAD_DIM), ("zh", "c"), 0, 0)
    blocks = sum_line(lines.reshape(4, 2, ROWS, HEAD_DIM))
    blocks = lax.all_to_all(blocks, ("xh", "xl", "yh"), 0, 0)
    query_w, keyval_w = finish(blocks)
    return context[None], grad_in[None], query_w, keyval_w


def solution(mesh):
    names = ("xh", "xl", "yh", "zh", "zl", "yl", "c")
    fine = Mesh(mesh.devices.reshape(2, 2, 2, 4, 2, 2, 2), names)
    dp, ctx = names[:3], names[3:]
    return jax.shard_map(
        shards,
        mesh=fine,
        in_specs=(P(dp, ctx, None), P(dp, None), P(), P(), P(dp, ctx, None)),
        out_specs=(P(dp, ctx, None), P(dp, ctx, None), P(ctx, None), P(ctx, None)),
        check_vma=False,
    )
```

```python
import functools

import jax
import jax.numpy as jnp
from jax import lax
from jax.experimental import pallas as pl
from jax.experimental.pallas import tpu as pltpu
from jax.sharding import Mesh
from jax.sharding import PartitionSpec as P

HEAD_DIM = 128
GROUP = 6
KV_HEADS = 2
WINDOW = 512
BLOCK = 128
HALO = WINDOW - BLOCK
OWN = 256
PAIR = 2 * OWN
KEYS = HALO + PAIR
QCOLS = GROUP * HEAD_DIM
KVCOLS = 2 * HEAD_DIM
D = 1536
DOCS = 8
SCALE = HEAD_DIM ** (-0.5)
LOG2E = 1.4426950408889634
F32 = jnp.float32
BF16 = jnp.bfloat16
NT = (((1,), (1,)), ((), ()))
TN = (((0,), (0,)), ((), ()))
ROWS = 48
KEEP = 384
PIECES = (16, 4, 2, ROWS, HEAD_DIM)
LIMIT = 24 * 1024 * 1024
VM = pl.BlockSpec(memory_space=pltpu.VMEM)
ANY = pl.BlockSpec(memory_space=pl.ANY)


def params():
    return pltpu.CompilerParams(vmem_limit_bytes=LIMIT)


def cost(flops, moved, trans=0):
    return pl.CostEstimate(flops=flops, bytes_accessed=moved, transcendentals=trans)


def shape(dims, dtype=BF16):
    return jax.ShapeDtypeStruct(dims, dtype)


def nn(a, b):
    return jnp.dot(a, b, preferred_element_type=F32)


def nt(a, b):
    return lax.dot_general(a, b, NT, preferred_element_type=F32)


def tn(a, b):
    return lax.dot_general(a, b, TN, preferred_element_type=F32)


def eye(size):
    row = lax.broadcasted_iota(jnp.int32, (size, size), 0)
    col = lax.broadcasted_iota(jnp.int32, (size, size), 1)
    return jnp.where(row == col, 1.0, 0.0).astype(BF16)


def columns(start, width=HEAD_DIM):
    return pl.ds(pl.multiple_of(start, HEAD_DIM), width)


def project_own_body(x, wkv, wq, x_here, wkv_here, wq_here, q, kv, sems):
    c = lax.axis_index("c")
    chunk = 512
    copies = [
        pltpu.make_async_copy(x, x_here, sems.at[0]),
        pltpu.make_async_copy(wkv, wkv_here, sems.at[1]),
    ]
    for j in range(D // chunk):
        rows = pl.ds(j * chunk, chunk)
        copies.append(
            pltpu.make_async_copy(
                wq.at[rows, columns(c * QCOLS, QCOLS)], wq_here.at[rows], sems.at[2 + j]
            )
        )
    for copy in copies:
        copy.start()
    copies[0].wait()
    copies[1].wait()
    kv[...] = nn(x_here[...], head_columns(wkv_here, c)).astype(BF16)
    total = jnp.zeros((OWN, QCOLS), F32)
    for j in range(D // chunk):
        rows = slice(j * chunk, (j + 1) * chunk)
        copies[2 + j].wait()
        total = total + nn(x_here[:, rows], wq_here[rows, :])
    q[...] = total.astype(BF16)


def head_columns(wkv, c):
    keys_w = wkv[:, columns(c * HEAD_DIM)]
    vals_w = wkv[:, columns((KV_HEADS + c) * HEAD_DIM)]
    return jnp.concatenate([keys_w, vals_w], axis=1)


def project_own(x, w_keyval, w_query):
    return pl.pallas_call(
        project_own_body,
        in_specs=[ANY] * 3,
        out_specs=[VM] * 5,
        out_shape=[
            pltpu.VMEM((OWN, D), BF16),
            pltpu.VMEM((D, 512), BF16),
            pltpu.VMEM((D, QCOLS), BF16),
            shape((OWN, QCOLS)),
            shape((OWN, KVCOLS)),
        ],
        scratch_shapes=[pltpu.SemaphoreType.DMA((5,))],
        compiler_params=params(),
        cost_estimate=cost(2 * OWN * D * 1024, 5 << 20),
        name="project_own",
    )(*(pltpu.with_memory_space_constraint(v, pltpu.HBM) for v in (x, w_keyval, w_query)))


def project_kv_body(x_oth, kv_own, w, kv, sent):
    c = lax.axis_index("c")
    own = kv_own[...]
    oth = nn(x_oth[...], head_columns(w, c)).astype(BF16)
    low = jnp.where(c == 0, own, oth)
    high = jnp.where(c == 0, oth, own)
    kv[:OWN] = low
    kv[OWN:] = high
    sent[: HALO - OWN] = low[PAIR - HALO :]
    sent[HALO - OWN :] = high


def project_kv(x_oth, kv_own, w_keyval):
    return pl.pallas_call(
        project_kv_body,
        in_specs=[VM] * 3,
        out_specs=[VM] * 2,
        out_shape=[shape((PAIR, KVCOLS)), shape((HALO, KVCOLS))],
        compiler_params=params(),
        cost_estimate=cost(2 * OWN * D * KVCOLS, 2 << 20),
        name="project_kv",
    )(x_oth, kv_own, w_keyval)


def project_q_body(x_oth, q_own, w, q):
    q[:OWN] = q_own[...]
    for j in range(3):
        cols = slice(j * 256, (j + 1) * 256)
        q[OWN:, cols] = nn(x_oth[...], w[:, cols]).astype(BF16)


def project_q(x_oth, q_own, w_query):
    return pl.pallas_call(
        project_q_body,
        in_specs=[VM] * 3,
        out_specs=VM,
        out_shape=shape((PAIR, QCOLS)),
        compiler_params=params(),
        cost_estimate=cost(2 * OWN * D * QCOLS, 4 << 20),
        name="project_q",
    )(x_oth, q_own, w_query)


def attend_block(b, pairs, c, q, do_own, do_oth, keys, keys_t, vals_t, low, ones):
    half, inner = b // 2, (b % 2) * BLOCK
    own = half == c
    here = slice(inner, inner + BLOCK)
    q_rows = pl.ds(pl.multiple_of(jnp.where(own, 0, OWN) + inner, BLOCK), BLOCK)
    win = slice(b * BLOCK, b * BLOCK + WINDOW)
    k_win = keys[win, :HEAD_DIM]
    v_win = keys[win, HEAD_DIM:]
    v_more = jnp.concatenate([v_win, ones[:HEAD_DIM, :HEAD_DIM]], axis=0)
    kt_win = keys_t[:, win]
    vt_win = vals_t[:, win]
    j_pos = lax.broadcasted_iota(jnp.int32, (WINDOW, BLOCK), 0)
    i_pos = lax.broadcasted_iota(jnp.int32, (WINDOW, BLOCK), 1)
    seen = (j_pos + b * BLOCK >= low[b : b + 1, :]) & (j_pos <= i_pos + HALO)
    bias = jnp.where(seen, 0.0, -1e30)
    bias = jnp.concatenate([bias, bias], axis=1)
    q2s, do2s = [], []
    for pair in pairs:
        at = pair * 256
        q_two = q[q_rows, at : at + 256]
        do_cols = columns(c * QCOLS + at, 256)
        do_two = jnp.where(own, do_own[here, do_cols], do_oth[here, do_cols])
        q2s.append(jnp.concatenate([q_two[:, :HEAD_DIM], q_two[:, HEAD_DIM:]], axis=0))
        do2s.append(jnp.concatenate([do_two[:, :HEAD_DIM], do_two[:, HEAD_DIM:]], axis=0))
    raw = [nt(k_win, q2) for q2 in q2s]
    probs = []
    for scores in raw:
        scores = scores + bias
        top = jnp.max(scores, axis=0, keepdims=True)
        expo = jnp.exp2((scores - top) * (SCALE * LOG2E))
        probs.append(expo * (1.0 / jnp.sum(expo, axis=0, keepdims=True)))
    lows = [p.astype(BF16) for p in probs]
    dps = [nt(v_more, do2) for do2 in do2s]
    ctx_ts = [nn(vt_win, p).astype(BF16) for p in lows]
    deltas = [
        jnp.sum(dp[WINDOW:] * ctx_t.astype(F32), axis=0, keepdims=True)
        for dp, ctx_t in zip(dps, ctx_ts)
    ]
    dvs = [nn(p, do2) for p, do2 in zip(lows, do2s)]
    dss = [
        (p * (dp[:WINDOW] - delta) * SCALE).astype(BF16)
        for p, dp, delta in zip(probs, dps, deltas)
    ]
    dks = [nn(ds, q2) for ds, q2 in zip(dss, q2s)]
    dq_ts = [nn(kt_win, ds).astype(BF16) for ds in dss]
    ctx_parts, dq_parts = [], []
    for ctx_t, dq_t in zip(ctx_ts, dq_ts):
        turned = nt(ones, jnp.concatenate([ctx_t, dq_t], axis=0)).astype(BF16)
        ctx_parts += [turned[:BLOCK, :HEAD_DIM], turned[BLOCK:, :HEAD_DIM]]
        dq_parts += [turned[:BLOCK, HEAD_DIM:], turned[BLOCK:, HEAD_DIM:]]
    grads = jnp.concatenate([sum(dks[1:], dks[0]), sum(dvs[1:], dvs[0])], axis=1)
    return ctx_parts, dq_parts, grads


def turn_keys(ones, keys, keys_t, vals_t, rows):
    small = ones[:HEAD_DIM, :HEAD_DIM]
    keys_t[:, rows] = nt(small, keys[rows, :HEAD_DIM]).astype(BF16)
    vals_t[:, rows] = nt(small, keys[rows, HEAD_DIM:]).astype(BF16)


def lowest_keys(chip, segs, low):
    lines = []
    for t in range(KEYS // BLOCK):
        row = chip * (PAIR // BLOCK) - HALO // BLOCK + t
        line = segs[pl.ds(jnp.maximum(row, 0), 1), :]
        lines.append(jnp.where(row >= 0, line, -1))
    own = jnp.concatenate(lines[HALO // BLOCK :], axis=0)
    lines = jnp.concatenate(lines, axis=0)
    first = jnp.zeros_like(own)
    for d in range(DOCS):
        first = jnp.where(own == d, jnp.sum(jnp.where(lines < d, 1, 0)), first)
    low[: PAIR // BLOCK, :] = first


KEY_SCRATCH = [
    pltpu.VMEM((KEYS, KVCOLS), BF16),
    pltpu.VMEM((HEAD_DIM, KEYS), BF16),
    pltpu.VMEM((HEAD_DIM, KEYS), BF16),
]


def attend_last_body(q, do_own, do_oth, kv, segs, mix, dkv, low, keys, keys_t, vals_t):
    c = lax.axis_index("c")
    chip = lax.axis_index(("zh", "zl", "yl"))
    ones = eye(256)
    keys[HALO:] = kv[...]
    turn_keys(ones, keys, keys_t, vals_t, slice(HALO, KEYS))
    lowest_keys(chip, segs, low)
    ctx, dq, dkv[...] = attend_block(
        3, range(3), c, q, do_own, do_oth, keys, keys_t, vals_t, low, ones
    )
    mix[...] = jnp.concatenate(ctx + dq, axis=1)


def attend_last(q, do_own, do_oth, kv, segs):
    return pl.pallas_call(
        attend_last_body,
        in_specs=[VM] * 5,
        out_specs=[VM] * 3,
        out_shape=[
            shape((BLOCK, 2 * QCOLS)),
            shape((WINDOW, KVCOLS), F32),
            shape((8, BLOCK), jnp.int32),
        ],
        scratch_shapes=KEY_SCRATCH,
        compiler_params=params(),
        cost_estimate=cost(2 * BLOCK * WINDOW * QCOLS * 6, 3 << 20, BLOCK * WINDOW * GROUP),
        name="attend_last",
    )(q, do_own, do_oth, kv, segs)


def put(b, value, held, mix_own, mix_oth, kept, sent, sem):
    own = b // 2 == lax.axis_index("c")
    rows = pl.ds((b % 2) * BLOCK, BLOCK)
    held[b] = value

    @pl.when(own)
    def _():
        pltpu.make_async_copy(held.at[b], mix_own.at[rows], sem).start()

    @pl.when(jnp.logical_not(own))
    def _():
        pltpu.make_async_copy(held.at[b], mix_oth.at[rows], sem).start()

    first = lax.axis_index("xl") == 0
    rows = pl.ds(pl.multiple_of(jnp.where(own, 0, OWN) + (b % 2) * BLOCK, BLOCK), BLOCK)
    one = value[:, QCOLS : QCOLS + KEEP]
    two = value[:, QCOLS + KEEP :]
    kept[rows, :] = jnp.where(first, one, two)
    sent[rows, :] = jnp.where(first, two, one)


def attend_body(q, do_own, do_oth, kv, halo, low, mix_last, dkv_last, *rest):
    mix_own, mix_oth, kept, sent, dkv_out, dkv_sent, keys, keys_t, vals_t, dkv, held, sems = rest
    c = lax.axis_index("c")
    ones = eye(256)
    keys[:HALO] = halo[...]
    keys[HALO:] = kv[...]
    turn_keys(ones, keys, keys_t, vals_t, slice(0, KEYS))
    dkv[:HALO] = jnp.zeros((HALO, KVCOLS), F32)
    dkv[HALO:] = dkv_last[...]
    put(3, mix_last[...], held, mix_own, mix_oth, kept, sent, sems.at[3])
    for b in range(3):
        ctx, dq, grads = attend_block(
            b, range(3), c, q, do_own, do_oth, keys, keys_t, vals_t, low, ones
        )
        dkv[b * BLOCK : b * BLOCK + WINDOW, :] += grads
        put(b, jnp.concatenate(ctx + dq, axis=1), held, mix_own, mix_oth, kept, sent, sems.at[b])
    dkv_sent[...] = dkv[:HALO, :].astype(BF16)
    dkv_out[...] = dkv[HALO:, :]
    for b in range(4):
        pltpu.make_async_copy(held.at[b], mix_own.at[pl.ds(0, BLOCK)], sems.at[b]).wait()


def attend(q, do_own, do_oth, kv, halo, low, mix_last, dkv_last):
    return pl.pallas_call(
        attend_body,
        in_specs=[VM] * 8,
        out_specs=[ANY] * 2 + [VM] * 4,
        out_shape=[
            pltpu.HBM((OWN, 2 * QCOLS), BF16),
            pltpu.HBM((OWN, 2 * QCOLS), BF16),
            shape((PAIR, KEEP)),
            shape((PAIR, KEEP)),
            shape((PAIR, KVCOLS), F32),
            shape((HALO, KVCOLS)),
        ],
        scratch_shapes=KEY_SCRATCH
        + [
            pltpu.VMEM((KEYS, KVCOLS), F32),
            pltpu.VMEM((4, BLOCK, 2 * QCOLS), BF16),
            pltpu.SemaphoreType.DMA((4,)),
        ],
        compiler_params=params(),
        cost_estimate=cost(3 * 2 * BLOCK * WINDOW * QCOLS * 6, 5 << 20, 3 * BLOCK * WINDOW * 6),
        name="attend",
    )(q, do_own, do_oth, kv, halo, low, mix_last, dkv_last)


def total_kv_body(dkv, arrived, own_out, oth_out, kept, sent):
    c = lax.axis_index("c")
    low = dkv[:OWN]
    skip = PAIR - HALO
    low = jnp.concatenate([low[:skip], low[skip:] + arrived[: OWN - skip].astype(F32)], axis=0)
    high = dkv[OWN:] + arrived[OWN - skip :].astype(F32)
    low = low.astype(BF16)
    high = high.astype(BF16)
    own = jnp.where(c == 0, low, high)
    oth = jnp.where(c == 0, high, low)
    own_out[...] = own
    oth_out[...] = oth
    first = lax.axis_index("xl") == 0
    for rows, value in ((slice(0, OWN), own), (slice(OWN, PAIR), oth)):
        kept[rows, :] = jnp.where(first, value[:, :HEAD_DIM], value[:, HEAD_DIM:])
        sent[rows, :] = jnp.where(first, value[:, HEAD_DIM:], value[:, :HEAD_DIM])


def total_kv(dkv, arrived):
    return pl.pallas_call(
        total_kv_body,
        in_specs=[VM] * 2,
        out_specs=[VM] * 4,
        out_shape=[shape((OWN, KVCOLS))] * 2 + [shape((PAIR, HEAD_DIM))] * 2,
        compiler_params=params(),
        cost_estimate=cost(1, 1),
        name="total_kv",
    )(dkv, arrived)


def chunks(width):
    return [slice(at, min(at + 256, width)) for at in range(0, width, 256)]


def weight_near_body(x_own, x_oth, g, out):
    for cols in chunks(g.shape[1]):
        out[:, cols] = tn(x_own[...], g[:OWN, cols]) + tn(x_oth[...], g[OWN:, cols])


def weight_near(x_own, x_oth, g):
    width = g.shape[1]
    return pl.pallas_call(
        weight_near_body,
        in_specs=[VM] * 3,
        out_specs=VM,
        out_shape=shape((D, width), F32),
        compiler_params=params(),
        cost_estimate=cost(20 * PAIR * D * width, 30 << 20),
        name="weight_near",
    )(x_own, x_oth, g)


def relay_body(value, after, out):
    del value, after, out


def relay(value, after):
    return pl.pallas_call(
        relay_body,
        in_specs=[VM] * 2,
        out_specs=VM,
        out_shape=shape(value.shape),
        input_output_aliases={0: 0},
        compiler_params=params(),
        cost_estimate=cost(1, 1),
        name="relay",
    )(value, after)


def spread(value, held, block):
    for s in range(value.shape[1] // HEAD_DIM):
        for y in range(2):
            for zl in range(2):
                for zh in range(4):
                    for core in range(2):
                        row = (zh * 2 + zl) * 192 + y * 96 + core * ROWS
                        piece = value[row : row + ROWS, s * HEAD_DIM : (s + 1) * HEAD_DIM]
                        held[(block + s) * 4 + y * 2 + zl, zh, core] = piece.astype(BF16)


def weight_far_body(start, x_own, x_oth, near, g, *rest):
    out, held, sems = rest[-3:]
    copies = []
    for i, cols in enumerate(chunks(g.shape[1])):
        value = near[:, cols] + tn(x_own[...], g[:OWN, cols]) + tn(x_oth[...], g[OWN:, cols])
        spread(value, held, 2 * i)
        count = (cols.stop - cols.start) // 32
        copies.append(
            pltpu.make_async_copy(
                held.at[pl.ds(8 * i, count)], out.at[pl.ds(start + 8 * i, count)], sems.at[i]
            )
        )
        copies[-1].start()
    for copy in copies:
        copy.wait()


def weight_far(x_own, x_oth, near, g, before=None):
    width = g.shape[1]
    extra = [] if before is None else [before]
    return pl.pallas_call(
        functools.partial(weight_far_body, 0 if before is None else 12),
        in_specs=[VM] * 4 + [ANY] * len(extra),
        out_specs=ANY,
        out_shape=pltpu.HBM(PIECES, BF16),
        scratch_shapes=[
            pltpu.VMEM((width // 32,) + PIECES[1:], BF16),
            pltpu.SemaphoreType.DMA((2,)),
        ],
        input_output_aliases={4: 0} if extra else {},
        compiler_params=params(),
        cost_estimate=cost(2 * PAIR * D * width, 4 << 20),
        name="weight_far",
    )(x_own, x_oth, near, g, *extra)


def ordered(first, own, oth):
    return jnp.where(
        first, jnp.concatenate([own, oth], axis=1), jnp.concatenate([oth, own], axis=1)
    )


def grad_tokens_body(mix, dkv, mix_in, dkv_in, wq, wkv, out, ctx_out, done):
    done[...] = jnp.zeros_like(done)
    first = lax.axis_index("c") == 0
    dq = ordered(first, mix[:, QCOLS:], mix_in[:, QCOLS:])
    kv = dkv[...]
    kv_in = dkv_in[...]
    keys = ordered(first, kv[:, :HEAD_DIM], kv_in[:, :HEAD_DIM])
    vals = ordered(first, kv[:, HEAD_DIM:], kv_in[:, HEAD_DIM:])
    kv_full = jnp.concatenate([keys, vals], axis=1)
    for j in range(3):
        rows = slice(j * 512, (j + 1) * 512)
        out[:, rows] = (nt(dq, wq[rows, :]) + nt(kv_full, wkv[rows, :])).astype(BF16)
    ctx_out[...] = ordered(first, mix[:, :QCOLS], mix_in[:, :QCOLS])


def grad_tokens(mix, dkv, mix_in, dkv_in, w_query, w_keyval):
    return pl.pallas_call(
        grad_tokens_body,
        in_specs=[VM] * 6,
        out_specs=[VM] * 3,
        out_shape=[shape((OWN, D)), shape((OWN, D)), shape((8, 128), F32)],
        compiler_params=params(),
        cost_estimate=cost(2 * OWN * D * 2048, 8 << 20),
        name="grad_tokens",
    )(mix, dkv, mix_in, dkv_in, w_query, w_keyval)


def sum_plane_body(pieces, after, out):
    out[...] = jnp.sum(pieces[...].astype(F32), axis=0).astype(BF16)


def sum_plane(pieces, after):
    return pl.pallas_call(
        sum_plane_body,
        in_specs=[VM, VM],
        out_specs=VM,
        out_shape=shape(PIECES[1:]),
        compiler_params=params(),
        cost_estimate=cost(16 * 8 * ROWS * HEAD_DIM, 2 << 20),
        name="sum_plane",
    )(pieces, after)


def sum_line_body(lines, out):
    total = jnp.sum(lines[...].astype(F32), axis=0).astype(BF16)
    for s in range(8):
        out[s] = total


def sum_line(lines):
    return pl.pallas_call(
        sum_line_body,
        in_specs=[VM],
        out_specs=VM,
        out_shape=shape((8, 2, ROWS, HEAD_DIM)),
        compiler_params=params(),
        name="sum_line",
    )(lines)


def finish_body(blocks, query_w, keyval_w):
    for xh in range(2):
        for xl in range(2):
            for yh in range(2):
                for core in range(2):
                    rows = blocks[(xh * 2 + xl) * 2 + yh, core]
                    block = xh * 2 + yh
                    if block < 3:
                        at = (core * GROUP + xl * 3 + block) * HEAD_DIM
                        query_w[:, at : at + HEAD_DIM] = rows
                    else:
                        at = (xl * KV_HEADS + core) * HEAD_DIM
                        keyval_w[:, at : at + HEAD_DIM] = rows


def finish(blocks):
    return pl.pallas_call(
        finish_body,
        in_specs=[VM],
        out_specs=[VM, VM],
        out_shape=[shape((ROWS, D)), shape((ROWS, 512))],
        compiler_params=params(),
        name="finish",
    )(blocks)


def swap(value, axis="c"):
    return lax.ppermute(value, axis, [(0, 1), (1, 0)])


def shards(tokens, segments, w_query, w_keyval, grad_context):
    x_own = tokens[0]
    do_own = grad_context[0]
    x_oth = swap(x_own)
    do_oth = swap(do_own)
    count = 32
    ring = ("zh", "zl", "yl", "c")
    x_own, wkv_here, wq_here, q_own, kv_own = project_own(x_own, w_keyval, w_query)
    kv, kv_sent = project_kv(x_oth, kv_own, wkv_here)
    far_own = swap(x_own, "xl")
    halo = lax.ppermute(kv_sent, ring, [(i, i + 2) for i in range(count - 2)])
    q = project_q(x_oth, q_own, wq_here)
    segs = segments.reshape(-1, BLOCK)
    mix_last, dkv_last, low = attend_last(q, do_own, do_oth, kv, segs)
    mix, mix_oth, kept, sent, dkv, dkv_sent = attend(
        q, do_own, do_oth, kv, halo, low, mix_last, dkv_last
    )
    arrived = lax.ppermute(dkv_sent, ring, [(i + 2, i) for i in range(count - 2)])
    far = swap(sent, "xl")
    near = weight_near(x_own, x_oth, kept)
    far_own = relay(far_own, kept)
    far_oth = swap(far_own)
    dkv_own, dkv_oth, kept_kv, sent_kv = total_kv(dkv, arrived)
    far_kv = swap(sent_kv, "xl")
    near_kv = weight_near(x_own, x_oth, kept_kv)
    pieces = weight_far(far_own, far_oth, near, far)
    pieces = weight_far(far_own, far_oth, near_kv, far_kv, pieces)
    pieces = lax.all_to_all(pieces, ("xh", "yh", "yl", "zl"), 0, 0)
    mix_in = swap(mix_oth)
    dkv_in = swap(dkv_oth)
    grad_in, context, done = grad_tokens(mix, dkv_own, mix_in, dkv_in, w_query, w_keyval)
    plane = sum_plane(pieces, done)
    lines = lax.all_to_all(plane.reshape(8, ROWS, HEAD_DIM), ("zh", "c"), 0, 0)
    blocks = sum_line(lines.reshape(4, 2, ROWS, HEAD_DIM))
    blocks = lax.all_to_all(blocks, ("xh", "xl", "yh"), 0, 0)
    query_w, keyval_w = finish(blocks)
    return context[None], grad_in[None], query_w, keyval_w


def solution(mesh):
    names = ("xh", "xl", "yh", "zh", "zl", "yl", "c")
    fine = Mesh(mesh.devices.reshape(2, 2, 2, 4, 2, 2, 2), names)
    dp, ctx = names[:3], names[3:]
    return jax.shard_map(
        shards,
        mesh=fine,
        in_specs=(P(dp, ctx, None), P(dp, None), P(), P(), P(dp, ctx, None)),
        out_specs=(P(dp, ctx, None), P(dp, ctx, None), P(ctx, None), P(ctx, None)),
        check_vma=False,
    )
```

```python
import functools

import jax
import jax.numpy as jnp
from jax import lax
from jax.experimental import pallas as pl
from jax.experimental.pallas import tpu as pltpu
from jax.sharding import Mesh
from jax.sharding import PartitionSpec as P

HEAD_DIM = 128
GROUP = 6
KV_HEADS = 2
WINDOW = 512
BLOCK = 128
HALO = WINDOW - BLOCK
OWN = 256
PAIR = 2 * OWN
KEYS = HALO + PAIR
QCOLS = GROUP * HEAD_DIM
KVCOLS = 2 * HEAD_DIM
D = 1536
DOCS = 8
SCALE = HEAD_DIM ** (-0.5)
LOG2E = 1.4426950408889634
F32 = jnp.float32
BF16 = jnp.bfloat16
NT = (((1,), (1,)), ((), ()))
TN = (((0,), (0,)), ((), ()))
ROWS = 48
KEEP = 384
PIECES = (16, 4, 2, ROWS, HEAD_DIM)
LIMIT = 24 * 1024 * 1024
VM = pl.BlockSpec(memory_space=pltpu.VMEM)
ANY = pl.BlockSpec(memory_space=pl.ANY)


def params():
    return pltpu.CompilerParams(vmem_limit_bytes=LIMIT)


def cost(flops, moved, trans=0):
    return pl.CostEstimate(flops=flops, bytes_accessed=moved, transcendentals=trans)


def shape(dims, dtype=BF16):
    return jax.ShapeDtypeStruct(dims, dtype)


def nn(a, b):
    return jnp.dot(a, b, preferred_element_type=F32)


def nt(a, b):
    return lax.dot_general(a, b, NT, preferred_element_type=F32)


def tn(a, b):
    return lax.dot_general(a, b, TN, preferred_element_type=F32)


def eye(size):
    row = lax.broadcasted_iota(jnp.int32, (size, size), 0)
    col = lax.broadcasted_iota(jnp.int32, (size, size), 1)
    return jnp.where(row == col, 1.0, 0.0).astype(BF16)


def columns(start, width=HEAD_DIM):
    return pl.ds(pl.multiple_of(start, HEAD_DIM), width)


def project_own_body(x, wkv, wq, x_here, wkv_here, wq_here, q, kv, sems):
    c = lax.axis_index("c")
    chunk = 512
    copies = [
        pltpu.make_async_copy(x, x_here, sems.at[0]),
        pltpu.make_async_copy(wkv, wkv_here, sems.at[1]),
    ]
    for j in range(D // chunk):
        rows = pl.ds(j * chunk, chunk)
        copies.append(
            pltpu.make_async_copy(
                wq.at[rows, columns(c * QCOLS, QCOLS)], wq_here.at[rows], sems.at[2 + j]
            )
        )
    for copy in copies:
        copy.start()
    copies[0].wait()
    copies[1].wait()
    kv[...] = nn(x_here[...], head_columns(wkv_here, c)).astype(BF16)
    total = jnp.zeros((OWN, QCOLS), F32)
    for j in range(D // chunk):
        rows = slice(j * chunk, (j + 1) * chunk)
        copies[2 + j].wait()
        total = total + nn(x_here[:, rows], wq_here[rows, :])
    q[...] = total.astype(BF16)


def head_columns(wkv, c):
    keys_w = wkv[:, columns(c * HEAD_DIM)]
    vals_w = wkv[:, columns((KV_HEADS + c) * HEAD_DIM)]
    return jnp.concatenate([keys_w, vals_w], axis=1)


def project_own(x, w_keyval, w_query):
    return pl.pallas_call(
        project_own_body,
        in_specs=[ANY] * 3,
        out_specs=[VM] * 5,
        out_shape=[
            pltpu.VMEM((OWN, D), BF16),
            pltpu.VMEM((D, 512), BF16),
            pltpu.VMEM((D, QCOLS), BF16),
            shape((OWN, QCOLS)),
            shape((OWN, KVCOLS)),
        ],
        scratch_shapes=[pltpu.SemaphoreType.DMA((5,))],
        compiler_params=params(),
        cost_estimate=cost(2 * OWN * D * 1024, 5 << 20),
        name="project_own",
    )(*(pltpu.with_memory_space_constraint(v, pltpu.HBM) for v in (x, w_keyval, w_query)))


def project_kv_body(x_oth, kv_own, w, kv, sent):
    c = lax.axis_index("c")
    own = kv_own[...]
    oth = nn(x_oth[...], head_columns(w, c)).astype(BF16)
    low = jnp.where(c == 0, own, oth)
    high = jnp.where(c == 0, oth, own)
    kv[:OWN] = low
    kv[OWN:] = high
    sent[: HALO - OWN] = low[PAIR - HALO :]
    sent[HALO - OWN :] = high


def project_kv(x_oth, kv_own, w_keyval):
    return pl.pallas_call(
        project_kv_body,
        in_specs=[VM] * 3,
        out_specs=[VM] * 2,
        out_shape=[shape((PAIR, KVCOLS)), shape((HALO, KVCOLS))],
        compiler_params=params(),
        cost_estimate=cost(2 * OWN * D * KVCOLS, 2 << 20),
        name="project_kv",
    )(x_oth, kv_own, w_keyval)


def project_q_body(x_oth, q_own, w, q):
    q[:OWN] = q_own[...]
    for j in range(3):
        cols = slice(j * 256, (j + 1) * 256)
        q[OWN:, cols] = nn(x_oth[...], w[:, cols]).astype(BF16)


def project_q(x_oth, q_own, w_query):
    return pl.pallas_call(
        project_q_body,
        in_specs=[VM] * 3,
        out_specs=VM,
        out_shape=shape((PAIR, QCOLS)),
        compiler_params=params(),
        cost_estimate=cost(2 * OWN * D * QCOLS, 4 << 20),
        name="project_q",
    )(x_oth, q_own, w_query)


def attend_block(b, pairs, c, q, do_own, do_oth, keys, keys_t, vals_t, low, ones):
    half, inner = b // 2, (b % 2) * BLOCK
    own = half == c
    here = slice(inner, inner + BLOCK)
    q_rows = pl.ds(pl.multiple_of(jnp.where(own, 0, OWN) + inner, BLOCK), BLOCK)
    win = slice(b * BLOCK, b * BLOCK + WINDOW)
    k_win = keys[win, :HEAD_DIM]
    v_win = keys[win, HEAD_DIM:]
    v_more = jnp.concatenate([v_win, ones[:HEAD_DIM, :HEAD_DIM]], axis=0)
    kt_win = keys_t[:, win]
    vt_win = vals_t[:, win]
    j_pos = lax.broadcasted_iota(jnp.int32, (WINDOW, BLOCK), 0)
    i_pos = lax.broadcasted_iota(jnp.int32, (WINDOW, BLOCK), 1)
    seen = (j_pos + b * BLOCK >= low[b : b + 1, :]) & (j_pos <= i_pos + HALO)
    bias = jnp.where(seen, 0.0, -1e30)
    bias = jnp.concatenate([bias, bias], axis=1)
    q2s, do2s = [], []
    for pair in pairs:
        at = pair * 256
        q_two = q[q_rows, at : at + 256]
        do_cols = columns(c * QCOLS + at, 256)
        do_two = jnp.where(own, do_own[here, do_cols], do_oth[here, do_cols])
        q2s.append(jnp.concatenate([q_two[:, :HEAD_DIM], q_two[:, HEAD_DIM:]], axis=0))
        do2s.append(jnp.concatenate([do_two[:, :HEAD_DIM], do_two[:, HEAD_DIM:]], axis=0))
    raw = [nt(k_win, q2) for q2 in q2s]
    probs = []
    for scores in raw:
        scores = scores + bias
        top = jnp.max(scores, axis=0, keepdims=True)
        expo = jnp.exp2((scores - top) * (SCALE * LOG2E))
        probs.append(expo * (1.0 / jnp.sum(expo, axis=0, keepdims=True)))
    lows = [p.astype(BF16) for p in probs]
    dps = [nt(v_more, do2) for do2 in do2s]
    ctx_ts = [nn(vt_win, p).astype(BF16) for p in lows]
    deltas = [
        jnp.sum(dp[WINDOW:] * ctx_t.astype(F32), axis=0, keepdims=True)
        for dp, ctx_t in zip(dps, ctx_ts)
    ]
    dvs = [nn(p, do2) for p, do2 in zip(lows, do2s)]
    dss = [
        (p * (dp[:WINDOW] - delta) * SCALE).astype(BF16)
        for p, dp, delta in zip(probs, dps, deltas)
    ]
    dks = [nn(ds, q2) for ds, q2 in zip(dss, q2s)]
    dq_ts = [nn(kt_win, ds).astype(BF16) for ds in dss]
    ctx_parts, dq_parts = [], []
    for ctx_t, dq_t in zip(ctx_ts, dq_ts):
        turned = nt(ones, jnp.concatenate([ctx_t, dq_t], axis=0)).astype(BF16)
        ctx_parts += [turned[:BLOCK, :HEAD_DIM], turned[BLOCK:, :HEAD_DIM]]
        dq_parts += [turned[:BLOCK, HEAD_DIM:], turned[BLOCK:, HEAD_DIM:]]
    grads = jnp.concatenate([sum(dks[1:], dks[0]), sum(dvs[1:], dvs[0])], axis=1)
    return ctx_parts, dq_parts, grads


def turn_keys(ones, keys, keys_t, vals_t, rows):
    small = ones[:HEAD_DIM, :HEAD_DIM]
    keys_t[:, rows] = nt(small, keys[rows, :HEAD_DIM]).astype(BF16)
    vals_t[:, rows] = nt(small, keys[rows, HEAD_DIM:]).astype(BF16)


def lowest_keys(chip, segs, low):
    lines = []
    for t in range(KEYS // BLOCK):
        row = chip * (PAIR // BLOCK) - HALO // BLOCK + t
        line = segs[pl.ds(jnp.maximum(row, 0), 1), :]
        lines.append(jnp.where(row >= 0, line, -1))
    own = jnp.concatenate(lines[HALO // BLOCK :], axis=0)
    lines = jnp.concatenate(lines, axis=0)
    first = jnp.zeros_like(own)
    for d in range(DOCS):
        first = jnp.where(own == d, jnp.sum(jnp.where(lines < d, 1, 0)), first)
    low[: PAIR // BLOCK, :] = first


KEY_SCRATCH = [
    pltpu.VMEM((KEYS, KVCOLS), BF16),
    pltpu.VMEM((HEAD_DIM, KEYS), BF16),
    pltpu.VMEM((HEAD_DIM, KEYS), BF16),
]


def attend_last_body(q, do_own, do_oth, kv, segs, mix, dkv, low, keys, keys_t, vals_t):
    c = lax.axis_index("c")
    chip = lax.axis_index(("zh", "zl", "yl"))
    ones = eye(256)
    keys[HALO:] = kv[...]
    turn_keys(ones, keys, keys_t, vals_t, slice(HALO, KEYS))
    lowest_keys(chip, segs, low)
    ctx, dq, dkv[...] = attend_block(
        3, range(3), c, q, do_own, do_oth, keys, keys_t, vals_t, low, ones
    )
    mix[...] = jnp.concatenate(ctx + dq, axis=1)


def attend_last(q, do_own, do_oth, kv, segs):
    return pl.pallas_call(
        attend_last_body,
        in_specs=[VM] * 5,
        out_specs=[VM] * 3,
        out_shape=[
            shape((BLOCK, 2 * QCOLS)),
            shape((WINDOW, KVCOLS), F32),
            shape((8, BLOCK), jnp.int32),
        ],
        scratch_shapes=KEY_SCRATCH,
        compiler_params=params(),
        cost_estimate=cost(2 * BLOCK * WINDOW * QCOLS * 6, 3 << 20, BLOCK * WINDOW * GROUP),
        name="attend_last",
    )(q, do_own, do_oth, kv, segs)


def put(b, value, held, mix_own, mix_oth, kept, sent, sem):
    own = b // 2 == lax.axis_index("c")
    rows = pl.ds((b % 2) * BLOCK, BLOCK)
    held[b] = value

    @pl.when(own)
    def _():
        pltpu.make_async_copy(held.at[b], mix_own.at[rows], sem).start()

    @pl.when(jnp.logical_not(own))
    def _():
        pltpu.make_async_copy(held.at[b], mix_oth.at[rows], sem).start()

    first = lax.axis_index("xl") == 0
    rows = pl.ds(pl.multiple_of(jnp.where(own, 0, OWN) + (b % 2) * BLOCK, BLOCK), BLOCK)
    one = value[:, QCOLS : QCOLS + KEEP]
    two = value[:, QCOLS + KEEP :]
    kept[rows, :] = jnp.where(first, one, two)
    sent[rows, :] = jnp.where(first, two, one)


def attend_body(q, do_own, do_oth, kv, halo, low, mix_last, dkv_last, *rest):
    mix_own, mix_oth, kept, sent, dkv_out, dkv_sent, keys, keys_t, vals_t, dkv, held, sems = rest
    c = lax.axis_index("c")
    ones = eye(256)
    keys[:HALO] = halo[...]
    keys[HALO:] = kv[...]
    turn_keys(ones, keys, keys_t, vals_t, slice(0, KEYS))
    dkv[:HALO] = jnp.zeros((HALO, KVCOLS), F32)
    dkv[HALO:] = dkv_last[...]
    put(3, mix_last[...], held, mix_own, mix_oth, kept, sent, sems.at[3])
    for b in range(3):
        ctx, dq, grads = attend_block(
            b, range(3), c, q, do_own, do_oth, keys, keys_t, vals_t, low, ones
        )
        dkv[b * BLOCK : b * BLOCK + WINDOW, :] += grads
        put(b, jnp.concatenate(ctx + dq, axis=1), held, mix_own, mix_oth, kept, sent, sems.at[b])
    dkv_sent[...] = dkv[:HALO, :].astype(BF16)
    dkv_out[...] = dkv[HALO:, :]
    for b in range(4):
        pltpu.make_async_copy(held.at[b], mix_own.at[pl.ds(0, BLOCK)], sems.at[b]).wait()


def attend(q, do_own, do_oth, kv, halo, low, mix_last, dkv_last):
    return pl.pallas_call(
        attend_body,
        in_specs=[VM] * 8,
        out_specs=[ANY] * 2 + [VM] * 4,
        out_shape=[
            pltpu.HBM((OWN, 2 * QCOLS), BF16),
            pltpu.HBM((OWN, 2 * QCOLS), BF16),
            shape((PAIR, KEEP)),
            shape((PAIR, KEEP)),
            shape((PAIR, KVCOLS), F32),
            shape((HALO, KVCOLS)),
        ],
        scratch_shapes=KEY_SCRATCH
        + [
            pltpu.VMEM((KEYS, KVCOLS), F32),
            pltpu.VMEM((4, BLOCK, 2 * QCOLS), BF16),
            pltpu.SemaphoreType.DMA((4,)),
        ],
        compiler_params=params(),
        cost_estimate=cost(3 * 2 * BLOCK * WINDOW * QCOLS * 6, 5 << 20, 3 * BLOCK * WINDOW * 6),
        name="attend",
    )(q, do_own, do_oth, kv, halo, low, mix_last, dkv_last)


def total_kv_body(dkv, arrived, own_out, oth_out, kept, sent):
    c = lax.axis_index("c")
    low = dkv[:OWN]
    skip = PAIR - HALO
    low = jnp.concatenate([low[:skip], low[skip:] + arrived[: OWN - skip].astype(F32)], axis=0)
    high = dkv[OWN:] + arrived[OWN - skip :].astype(F32)
    low = low.astype(BF16)
    high = high.astype(BF16)
    own = jnp.where(c == 0, low, high)
    oth = jnp.where(c == 0, high, low)
    own_out[...] = own
    oth_out[...] = oth
    first = lax.axis_index("xl") == 0
    for rows, value in ((slice(0, OWN), own), (slice(OWN, PAIR), oth)):
        kept[rows, :] = jnp.where(first, value[:, :HEAD_DIM], value[:, HEAD_DIM:])
        sent[rows, :] = jnp.where(first, value[:, HEAD_DIM:], value[:, :HEAD_DIM])


def total_kv(dkv, arrived):
    return pl.pallas_call(
        total_kv_body,
        in_specs=[VM] * 2,
        out_specs=[VM] * 4,
        out_shape=[shape((OWN, KVCOLS))] * 2 + [shape((PAIR, HEAD_DIM))] * 2,
        compiler_params=params(),
        cost_estimate=cost(1, 1),
        name="total_kv",
    )(dkv, arrived)


def chunks(width):
    return [slice(at, min(at + 256, width)) for at in range(0, width, 256)]


def weight_near_body(x_own, x_oth, g, out):
    for cols in chunks(g.shape[1]):
        out[:, cols] = tn(x_own[...], g[:OWN, cols]) + tn(x_oth[...], g[OWN:, cols])


def weight_near(x_own, x_oth, g):
    width = g.shape[1]
    return pl.pallas_call(
        weight_near_body,
        in_specs=[VM] * 3,
        out_specs=VM,
        out_shape=shape((D, width), F32),
        compiler_params=params(),
        cost_estimate=cost(20 * PAIR * D * width, 30 << 20),
        name="weight_near",
    )(x_own, x_oth, g)


def relay_body(value, after, out):
    del value, after, out


def relay(value, after):
    return pl.pallas_call(
        relay_body,
        in_specs=[VM] * 2,
        out_specs=VM,
        out_shape=shape(value.shape),
        input_output_aliases={0: 0},
        compiler_params=params(),
        cost_estimate=cost(1, 1),
        name="relay",
    )(value, after)


def spread(value, held, block):
    for s in range(value.shape[1] // HEAD_DIM):
        for y in range(2):
            for zl in range(2):
                for zh in range(4):
                    for core in range(2):
                        row = (zh * 2 + zl) * 192 + y * 96 + core * ROWS
                        piece = value[row : row + ROWS, s * HEAD_DIM : (s + 1) * HEAD_DIM]
                        held[(block + s) * 4 + y * 2 + zl, zh, core] = piece.astype(BF16)


def weight_far_body(start, x_own, x_oth, near, g, *rest):
    out, held, sems = rest[-3:]
    copies = []
    for i, cols in enumerate(chunks(g.shape[1])):
        value = near[:, cols] + tn(x_own[...], g[:OWN, cols]) + tn(x_oth[...], g[OWN:, cols])
        spread(value, held, 2 * i)
        count = (cols.stop - cols.start) // 32
        copies.append(
            pltpu.make_async_copy(
                held.at[pl.ds(8 * i, count)], out.at[pl.ds(start + 8 * i, count)], sems.at[i]
            )
        )
        copies[-1].start()
    for copy in copies:
        copy.wait()


def weight_far(x_own, x_oth, near, g, before=None):
    width = g.shape[1]
    extra = [] if before is None else [before]
    return pl.pallas_call(
        functools.partial(weight_far_body, 0 if before is None else 12),
        in_specs=[VM] * 4 + [ANY] * len(extra),
        out_specs=ANY,
        out_shape=pltpu.HBM(PIECES, BF16),
        scratch_shapes=[
            pltpu.VMEM((width // 32,) + PIECES[1:], BF16),
            pltpu.SemaphoreType.DMA((2,)),
        ],
        input_output_aliases={4: 0} if extra else {},
        compiler_params=params(),
        cost_estimate=cost(2 * PAIR * D * width, 4 << 20),
        name="weight_far",
    )(x_own, x_oth, near, g, *extra)


def ordered(first, own, oth):
    return jnp.where(
        first, jnp.concatenate([own, oth], axis=1), jnp.concatenate([oth, own], axis=1)
    )


def grad_tokens_body(mix, dkv, mix_in, dkv_in, wq, wkv, out, ctx_out, done):
    done[...] = jnp.zeros_like(done)
    first = lax.axis_index("c") == 0
    dq = ordered(first, mix[:, QCOLS:], mix_in[:, QCOLS:])
    kv = dkv[...]
    kv_in = dkv_in[...]
    keys = ordered(first, kv[:, :HEAD_DIM], kv_in[:, :HEAD_DIM])
    vals = ordered(first, kv[:, HEAD_DIM:], kv_in[:, HEAD_DIM:])
    kv_full = jnp.concatenate([keys, vals], axis=1)
    for j in range(3):
        rows = slice(j * 512, (j + 1) * 512)
        out[:, rows] = (nt(dq, wq[rows, :]) + nt(kv_full, wkv[rows, :])).astype(BF16)
    ctx_out[...] = ordered(first, mix[:, :QCOLS], mix_in[:, :QCOLS])


def grad_tokens(mix, dkv, mix_in, dkv_in, w_query, w_keyval):
    return pl.pallas_call(
        grad_tokens_body,
        in_specs=[VM] * 6,
        out_specs=[VM] * 3,
        out_shape=[shape((OWN, D)), shape((OWN, D)), shape((8, 128), F32)],
        compiler_params=params(),
        cost_estimate=cost(2 * OWN * D * 2048, 8 << 20),
        name="grad_tokens",
    )(mix, dkv, mix_in, dkv_in, w_query, w_keyval)


def sum_plane_body(pieces, after, out):
    out[...] = jnp.sum(pieces[...].astype(F32), axis=0).astype(BF16)


def sum_plane(pieces, after):
    return pl.pallas_call(
        sum_plane_body,
        in_specs=[VM, VM],
        out_specs=VM,
        out_shape=shape(PIECES[1:]),
        compiler_params=params(),
        cost_estimate=cost(16 * 8 * ROWS * HEAD_DIM, 2 << 20),
        name="sum_plane",
    )(pieces, after)


def sum_line_body(lines, out):
    out[...] = jnp.sum(lines[...].astype(F32), axis=0).astype(BF16)


def sum_line(lines):
    return pl.pallas_call(
        sum_line_body,
        in_specs=[VM],
        out_specs=VM,
        out_shape=shape(lines.shape[1:]),
        compiler_params=params(),
        name="sum_line",
    )(lines)


def stack_body(near, far, out):
    first = lax.axis_index("yh") == 0
    one = near[...]
    two = far[...]
    out[0] = jnp.where(first, one, two)
    out[1] = jnp.where(first, two, one)


def stack(near, far):
    return pl.pallas_call(
        stack_body,
        in_specs=[VM] * 2,
        out_specs=VM,
        out_shape=shape((2,) + near.shape),
        compiler_params=params(),
        name="stack",
    )(near, far)


def finish_body(one, two, three, four, query_w, keyval_w):
    x = lax.axis_index(("xh", "xl"))
    for source in range(4):
        value = one[...]
        for turn, other in enumerate((two, three, four), 1):
            value = jnp.where((source + turn) % 4 == x, other[...], value)
        xh, xl = source // 2, source % 2
        for yh in range(2):
            for core in range(2):
                block = xh * 2 + yh
                if block < 3:
                    at = (core * GROUP + xl * 3 + block) * HEAD_DIM
                    query_w[:, at : at + HEAD_DIM] = value[yh, core]
                else:
                    at = (xl * KV_HEADS + core) * HEAD_DIM
                    keyval_w[:, at : at + HEAD_DIM] = value[yh, core]


def finish(blocks):
    return pl.pallas_call(
        finish_body,
        in_specs=[VM] * 4,
        out_specs=[VM, VM],
        out_shape=[shape((ROWS, D)), shape((ROWS, 512))],
        compiler_params=params(),
        name="finish",
    )(*blocks)


def swap(value, axis="c"):
    return lax.ppermute(value, axis, [(0, 1), (1, 0)])


def shards(tokens, segments, w_query, w_keyval, grad_context):
    x_own = tokens[0]
    do_own = grad_context[0]
    x_oth = swap(x_own)
    do_oth = swap(do_own)
    far_own = swap(x_own, "xl")
    count = 32
    ring = ("zh", "zl", "yl", "c")
    x_own, wkv_here, wq_here, q_own, kv_own = project_own(x_own, w_keyval, w_query)
    kv, kv_sent = project_kv(x_oth, kv_own, wkv_here)
    halo = lax.ppermute(kv_sent, ring, [(i, i + 2) for i in range(count - 2)])
    q = project_q(x_oth, q_own, wq_here)
    segs = segments.reshape(-1, BLOCK)
    mix_last, dkv_last, low = attend_last(q, do_own, do_oth, kv, segs)
    mix, mix_oth, kept, sent, dkv, dkv_sent = attend(
        q, do_own, do_oth, kv, halo, low, mix_last, dkv_last
    )
    arrived = lax.ppermute(dkv_sent, ring, [(i + 2, i) for i in range(count - 2)])
    far = swap(sent, "xl")
    near = weight_near(x_own, x_oth, kept)
    far_own = relay(far_own, kept)
    far_oth = swap(far_own)
    dkv_own, dkv_oth, kept_kv, sent_kv = total_kv(dkv, arrived)
    far_kv = swap(sent_kv, "xl")
    near_kv = weight_near(x_own, x_oth, kept_kv)
    pieces = weight_far(far_own, far_oth, near, far)
    pieces = weight_far(far_own, far_oth, near_kv, far_kv, pieces)
    pieces = lax.all_to_all(pieces, ("xh", "yh", "yl", "zl"), 0, 0)
    mix_in = swap(mix_oth)
    dkv_in = swap(dkv_oth)
    grad_in, context, done = grad_tokens(mix, dkv_own, mix_in, dkv_in, w_query, w_keyval)
    plane = sum_plane(pieces, done)
    lines = lax.all_to_all(plane.reshape(8, ROWS, HEAD_DIM), ("zh", "c"), 0, 0)
    blocks = sum_line(lines.reshape(4, 2, ROWS, HEAD_DIM))
    blocks = stack(blocks, swap(blocks, "yh"))
    around = [
        lax.ppermute(blocks, ("xh", "xl"), [(i, (i + turn) % 4) for i in range(4)])
        for turn in range(1, 4)
    ]
    query_w, keyval_w = finish([blocks] + around)
    return context[None], grad_in[None], query_w, keyval_w


def solution(mesh):
    names = ("xh", "xl", "yh", "zh", "zl", "yl", "c")
    fine = Mesh(mesh.devices.reshape(2, 2, 2, 4, 2, 2, 2), names)
    dp, ctx = names[:3], names[3:]
    return jax.shard_map(
        shards,
        mesh=fine,
        in_specs=(P(dp, ctx, None), P(dp, None), P(), P(), P(dp, ctx, None)),
        out_specs=(P(dp, ctx, None), P(dp, ctx, None), P(ctx, None), P(ctx, None)),
        check_vma=False,
    )
```

```python
import functools

import jax
import jax.numpy as jnp
from jax import lax
from jax.experimental import pallas as pl
from jax.experimental.pallas import tpu as pltpu
from jax.sharding import Mesh
from jax.sharding import PartitionSpec as P

HEAD_DIM = 128
GROUP = 6
KV_HEADS = 2
WINDOW = 512
BLOCK = 128
HALO = WINDOW - BLOCK
OWN = 256
PAIR = 2 * OWN
KEYS = HALO + PAIR
QCOLS = GROUP * HEAD_DIM
KVCOLS = 2 * HEAD_DIM
D = 1536
DOCS = 8
SCALE = HEAD_DIM ** (-0.5)
LOG2E = 1.4426950408889634
F32 = jnp.float32
BF16 = jnp.bfloat16
NT = (((1,), (1,)), ((), ()))
TN = (((0,), (0,)), ((), ()))
ROWS = 48
KEEP = 384
PIECES = (16, 4, 2, ROWS, HEAD_DIM)
LIMIT = 24 * 1024 * 1024
VM = pl.BlockSpec(memory_space=pltpu.VMEM)
ANY = pl.BlockSpec(memory_space=pl.ANY)


def params():
    return pltpu.CompilerParams(vmem_limit_bytes=LIMIT)


def cost(flops, moved, trans=0):
    return pl.CostEstimate(flops=flops, bytes_accessed=moved, transcendentals=trans)


def shape(dims, dtype=BF16):
    return jax.ShapeDtypeStruct(dims, dtype)


def nn(a, b):
    return jnp.dot(a, b, preferred_element_type=F32)


def nt(a, b):
    return lax.dot_general(a, b, NT, preferred_element_type=F32)


def tn(a, b):
    return lax.dot_general(a, b, TN, preferred_element_type=F32)


def eye(size):
    row = lax.broadcasted_iota(jnp.int32, (size, size), 0)
    col = lax.broadcasted_iota(jnp.int32, (size, size), 1)
    return jnp.where(row == col, 1.0, 0.0).astype(BF16)


def columns(start, width=HEAD_DIM):
    return pl.ds(pl.multiple_of(start, HEAD_DIM), width)


def project_own_body(x, wkv, wq, x_here, wkv_here, wq_here, q, kv, sems):
    c = lax.axis_index("c")
    chunk = 512
    copies = [
        pltpu.make_async_copy(x, x_here, sems.at[0]),
        pltpu.make_async_copy(wkv, wkv_here, sems.at[1]),
    ]
    for j in range(D // chunk):
        rows = pl.ds(j * chunk, chunk)
        copies.append(
            pltpu.make_async_copy(
                wq.at[rows, columns(c * QCOLS, QCOLS)], wq_here.at[rows], sems.at[2 + j]
            )
        )
    for copy in copies:
        copy.start()
    copies[0].wait()
    copies[1].wait()
    kv[...] = nn(x_here[...], head_columns(wkv_here, c)).astype(BF16)
    total = jnp.zeros((OWN, QCOLS), F32)
    for j in range(D // chunk):
        rows = slice(j * chunk, (j + 1) * chunk)
        copies[2 + j].wait()
        total = total + nn(x_here[:, rows], wq_here[rows, :])
    q[...] = total.astype(BF16)


def head_columns(wkv, c):
    keys_w = wkv[:, columns(c * HEAD_DIM)]
    vals_w = wkv[:, columns((KV_HEADS + c) * HEAD_DIM)]
    return jnp.concatenate([keys_w, vals_w], axis=1)


def project_own(x, w_keyval, w_query):
    return pl.pallas_call(
        project_own_body,
        in_specs=[ANY] * 3,
        out_specs=[VM] * 5,
        out_shape=[
            pltpu.VMEM((OWN, D), BF16),
            pltpu.VMEM((D, 512), BF16),
            pltpu.VMEM((D, QCOLS), BF16),
            shape((OWN, QCOLS)),
            shape((OWN, KVCOLS)),
        ],
        scratch_shapes=[pltpu.SemaphoreType.DMA((5,))],
        compiler_params=params(),
        cost_estimate=cost(2 * OWN * D * 1024, 5 << 20),
        name="project_own",
    )(*(pltpu.with_memory_space_constraint(v, pltpu.HBM) for v in (x, w_keyval, w_query)))


def project_kv_body(x_oth, kv_own, w, kv, sent):
    c = lax.axis_index("c")
    own = kv_own[...]
    oth = nn(x_oth[...], head_columns(w, c)).astype(BF16)
    low = jnp.where(c == 0, own, oth)
    high = jnp.where(c == 0, oth, own)
    kv[:OWN] = low
    kv[OWN:] = high
    sent[: HALO - OWN] = low[PAIR - HALO :]
    sent[HALO - OWN :] = high


def project_kv(x_oth, kv_own, w_keyval):
    return pl.pallas_call(
        project_kv_body,
        in_specs=[VM] * 3,
        out_specs=[VM] * 2,
        out_shape=[shape((PAIR, KVCOLS)), shape((HALO, KVCOLS))],
        compiler_params=params(),
        cost_estimate=cost(2 * OWN * D * KVCOLS, 2 << 20),
        name="project_kv",
    )(x_oth, kv_own, w_keyval)


def project_q_body(x_oth, q_own, w, q):
    q[:OWN] = q_own[...]
    for j in range(3):
        cols = slice(j * 256, (j + 1) * 256)
        q[OWN:, cols] = nn(x_oth[...], w[:, cols]).astype(BF16)


def project_q(x_oth, q_own, w_query):
    return pl.pallas_call(
        project_q_body,
        in_specs=[VM] * 3,
        out_specs=VM,
        out_shape=shape((PAIR, QCOLS)),
        compiler_params=params(),
        cost_estimate=cost(2 * OWN * D * QCOLS, 4 << 20),
        name="project_q",
    )(x_oth, q_own, w_query)


def attend_block(b, pairs, c, q, do_own, do_oth, keys, keys_t, vals_t, low, ones):
    half, inner = b // 2, (b % 2) * BLOCK
    own = half == c
    here = slice(inner, inner + BLOCK)
    q_rows = pl.ds(pl.multiple_of(jnp.where(own, 0, OWN) + inner, BLOCK), BLOCK)
    win = slice(b * BLOCK, b * BLOCK + WINDOW)
    k_win = keys[win, :HEAD_DIM]
    v_win = keys[win, HEAD_DIM:]
    v_more = jnp.concatenate([v_win, ones[:HEAD_DIM, :HEAD_DIM]], axis=0)
    kt_win = keys_t[:, win]
    vt_win = vals_t[:, win]
    j_pos = lax.broadcasted_iota(jnp.int32, (WINDOW, BLOCK), 0)
    i_pos = lax.broadcasted_iota(jnp.int32, (WINDOW, BLOCK), 1)
    seen = (j_pos + b * BLOCK >= low[b : b + 1, :]) & (j_pos <= i_pos + HALO)
    bias = jnp.where(seen, 0.0, -1e30)
    bias = jnp.concatenate([bias, bias], axis=1)
    q2s, do2s = [], []
    for pair in pairs:
        at = pair * 256
        q_two = q[q_rows, at : at + 256]
        do_cols = columns(c * QCOLS + at, 256)
        do_two = jnp.where(own, do_own[here, do_cols], do_oth[here, do_cols])
        q2s.append(jnp.concatenate([q_two[:, :HEAD_DIM], q_two[:, HEAD_DIM:]], axis=0))
        do2s.append(jnp.concatenate([do_two[:, :HEAD_DIM], do_two[:, HEAD_DIM:]], axis=0))
    raw = [nt(k_win, q2) for q2 in q2s]
    probs = []
    for scores in raw:
        scores = scores + bias
        top = jnp.max(scores, axis=0, keepdims=True)
        expo = jnp.exp2((scores - top) * (SCALE * LOG2E))
        probs.append(expo * (1.0 / jnp.sum(expo, axis=0, keepdims=True)))
    lows = [p.astype(BF16) for p in probs]
    dps = [nt(v_more, do2) for do2 in do2s]
    ctx_ts = [nn(vt_win, p).astype(BF16) for p in lows]
    deltas = [
        jnp.sum(dp[WINDOW:] * ctx_t.astype(F32), axis=0, keepdims=True)
        for dp, ctx_t in zip(dps, ctx_ts)
    ]
    dvs = [nn(p, do2) for p, do2 in zip(lows, do2s)]
    dss = [
        (p * (dp[:WINDOW] - delta) * SCALE).astype(BF16)
        for p, dp, delta in zip(probs, dps, deltas)
    ]
    dks = [nn(ds, q2) for ds, q2 in zip(dss, q2s)]
    dq_ts = [nn(kt_win, ds).astype(BF16) for ds in dss]
    ctx_parts, dq_parts = [], []
    for ctx_t, dq_t in zip(ctx_ts, dq_ts):
        turned = nt(ones, jnp.concatenate([ctx_t, dq_t], axis=0)).astype(BF16)
        ctx_parts += [turned[:BLOCK, :HEAD_DIM], turned[BLOCK:, :HEAD_DIM]]
        dq_parts += [turned[:BLOCK, HEAD_DIM:], turned[BLOCK:, HEAD_DIM:]]
    grads = jnp.concatenate([sum(dks[1:], dks[0]), sum(dvs[1:], dvs[0])], axis=1)
    return ctx_parts, dq_parts, grads


def turn_keys(ones, keys, keys_t, vals_t, rows):
    small = ones[:HEAD_DIM, :HEAD_DIM]
    keys_t[:, rows] = nt(small, keys[rows, :HEAD_DIM]).astype(BF16)
    vals_t[:, rows] = nt(small, keys[rows, HEAD_DIM:]).astype(BF16)


def lowest_keys(chip, segs, low):
    lines = []
    for t in range(KEYS // BLOCK):
        row = chip * (PAIR // BLOCK) - HALO // BLOCK + t
        line = segs[pl.ds(jnp.maximum(row, 0), 1), :]
        lines.append(jnp.where(row >= 0, line, -1))
    own = jnp.concatenate(lines[HALO // BLOCK :], axis=0)
    lines = jnp.concatenate(lines, axis=0)
    first = jnp.zeros_like(own)
    for d in range(DOCS):
        first = jnp.where(own == d, jnp.sum(jnp.where(lines < d, 1, 0)), first)
    low[: PAIR // BLOCK, :] = first


KEY_SCRATCH = [
    pltpu.VMEM((KEYS, KVCOLS), BF16),
    pltpu.VMEM((HEAD_DIM, KEYS), BF16),
    pltpu.VMEM((HEAD_DIM, KEYS), BF16),
]


def attend_last_body(q, do_own, do_oth, kv, segs, mix, dkv, low, keys, keys_t, vals_t):
    c = lax.axis_index("c")
    chip = lax.axis_index(("zh", "zl", "yl"))
    ones = eye(256)
    keys[HALO:] = kv[...]
    turn_keys(ones, keys, keys_t, vals_t, slice(HALO, KEYS))
    lowest_keys(chip, segs, low)
    ctx, dq, dkv[...] = attend_block(
        3, range(3), c, q, do_own, do_oth, keys, keys_t, vals_t, low, ones
    )
    mix[...] = jnp.concatenate(ctx + dq, axis=1)


def attend_last(q, do_own, do_oth, kv, segs):
    return pl.pallas_call(
        attend_last_body,
        in_specs=[VM] * 5,
        out_specs=[VM] * 3,
        out_shape=[
            shape((BLOCK, 2 * QCOLS)),
            shape((WINDOW, KVCOLS), F32),
            shape((8, BLOCK), jnp.int32),
        ],
        scratch_shapes=KEY_SCRATCH,
        compiler_params=params(),
        cost_estimate=cost(2 * BLOCK * WINDOW * QCOLS * 6, 3 << 20, BLOCK * WINDOW * GROUP),
        name="attend_last",
    )(q, do_own, do_oth, kv, segs)


def put(b, value, held, mix_own, mix_oth, kept, sent, sem):
    own = b // 2 == lax.axis_index("c")
    rows = pl.ds((b % 2) * BLOCK, BLOCK)
    held[b] = value

    @pl.when(own)
    def _():
        pltpu.make_async_copy(held.at[b], mix_own.at[rows], sem).start()

    @pl.when(jnp.logical_not(own))
    def _():
        pltpu.make_async_copy(held.at[b], mix_oth.at[rows], sem).start()

    first = lax.axis_index("xl") == 0
    rows = pl.ds(pl.multiple_of(jnp.where(own, 0, OWN) + (b % 2) * BLOCK, BLOCK), BLOCK)
    one = value[:, QCOLS : QCOLS + KEEP]
    two = value[:, QCOLS + KEEP :]
    kept[rows, :] = jnp.where(first, one, two)
    sent[rows, :] = jnp.where(first, two, one)


def attend_body(q, do_own, do_oth, kv, halo, low, mix_last, dkv_last, *rest):
    mix_own, mix_oth, kept, sent, dkv_out, dkv_sent, keys, keys_t, vals_t, dkv, held, sems = rest
    c = lax.axis_index("c")
    ones = eye(256)
    keys[:HALO] = halo[...]
    keys[HALO:] = kv[...]
    turn_keys(ones, keys, keys_t, vals_t, slice(0, KEYS))
    dkv[:HALO] = jnp.zeros((HALO, KVCOLS), F32)
    dkv[HALO:] = dkv_last[...]
    put(3, mix_last[...], held, mix_own, mix_oth, kept, sent, sems.at[3])
    for b in range(3):
        ctx, dq, grads = attend_block(
            b, range(3), c, q, do_own, do_oth, keys, keys_t, vals_t, low, ones
        )
        dkv[b * BLOCK : b * BLOCK + WINDOW, :] += grads
        put(b, jnp.concatenate(ctx + dq, axis=1), held, mix_own, mix_oth, kept, sent, sems.at[b])
    dkv_sent[...] = dkv[:HALO, :].astype(BF16)
    dkv_out[...] = dkv[HALO:, :]
    for b in range(4):
        pltpu.make_async_copy(held.at[b], mix_own.at[pl.ds(0, BLOCK)], sems.at[b]).wait()


def attend(q, do_own, do_oth, kv, halo, low, mix_last, dkv_last):
    return pl.pallas_call(
        attend_body,
        in_specs=[VM] * 8,
        out_specs=[ANY] * 2 + [VM] * 4,
        out_shape=[
            pltpu.HBM((OWN, 2 * QCOLS), BF16),
            pltpu.HBM((OWN, 2 * QCOLS), BF16),
            shape((PAIR, KEEP)),
            shape((PAIR, KEEP)),
            shape((PAIR, KVCOLS), F32),
            shape((HALO, KVCOLS)),
        ],
        scratch_shapes=KEY_SCRATCH
        + [
            pltpu.VMEM((KEYS, KVCOLS), F32),
            pltpu.VMEM((4, BLOCK, 2 * QCOLS), BF16),
            pltpu.SemaphoreType.DMA((4,)),
        ],
        compiler_params=params(),
        cost_estimate=cost(3 * 2 * BLOCK * WINDOW * QCOLS * 6, 5 << 20, 3 * BLOCK * WINDOW * 6),
        name="attend",
    )(q, do_own, do_oth, kv, halo, low, mix_last, dkv_last)


def total_kv_body(dkv, arrived, own_out, oth_out, kept, sent):
    c = lax.axis_index("c")
    low = dkv[:OWN]
    skip = PAIR - HALO
    low = jnp.concatenate([low[:skip], low[skip:] + arrived[: OWN - skip].astype(F32)], axis=0)
    high = dkv[OWN:] + arrived[OWN - skip :].astype(F32)
    low = low.astype(BF16)
    high = high.astype(BF16)
    own = jnp.where(c == 0, low, high)
    oth = jnp.where(c == 0, high, low)
    own_out[...] = own
    oth_out[...] = oth
    first = lax.axis_index("xl") == 0
    for rows, value in ((slice(0, OWN), own), (slice(OWN, PAIR), oth)):
        kept[rows, :] = jnp.where(first, value[:, :HEAD_DIM], value[:, HEAD_DIM:])
        sent[rows, :] = jnp.where(first, value[:, HEAD_DIM:], value[:, :HEAD_DIM])


def total_kv(dkv, arrived):
    return pl.pallas_call(
        total_kv_body,
        in_specs=[VM] * 2,
        out_specs=[VM] * 4,
        out_shape=[shape((OWN, KVCOLS))] * 2 + [shape((PAIR, HEAD_DIM))] * 2,
        compiler_params=params(),
        cost_estimate=cost(1, 1),
        name="total_kv",
    )(dkv, arrived)


def chunks(width):
    return [slice(at, min(at + 256, width)) for at in range(0, width, 256)]


def weight_near_body(x_own, x_oth, g, out):
    for cols in chunks(g.shape[1]):
        out[:, cols] = tn(x_own[...], g[:OWN, cols]) + tn(x_oth[...], g[OWN:, cols])


def weight_near(x_own, x_oth, g):
    width = g.shape[1]
    return pl.pallas_call(
        weight_near_body,
        in_specs=[VM] * 3,
        out_specs=VM,
        out_shape=shape((D, width), F32),
        compiler_params=params(),
        cost_estimate=cost(200 * PAIR * D * width, 300 << 20),
        name="weight_near",
    )(x_own, x_oth, g)


def relay_body(value, after, out):
    del value, after, out


def relay(value, after):
    return pl.pallas_call(
        relay_body,
        in_specs=[VM] * 2,
        out_specs=VM,
        out_shape=shape(value.shape),
        input_output_aliases={0: 0},
        compiler_params=params(),
        cost_estimate=cost(1, 1),
        name="relay",
    )(value, after)


def spread(value, held, block):
    for s in range(value.shape[1] // HEAD_DIM):
        for y in range(2):
            for zl in range(2):
                for zh in range(4):
                    for core in range(2):
                        row = (zh * 2 + zl) * 192 + y * 96 + core * ROWS
                        piece = value[row : row + ROWS, s * HEAD_DIM : (s + 1) * HEAD_DIM]
                        held[(block + s) * 4 + y * 2 + zl, zh, core] = piece.astype(BF16)


def weight_far_body(start, x_own, x_oth, near, g, *rest):
    out, held, sems = rest[-3:]
    copies = []
    for i, cols in enumerate(chunks(g.shape[1])):
        value = near[:, cols] + tn(x_own[...], g[:OWN, cols]) + tn(x_oth[...], g[OWN:, cols])
        spread(value, held, 2 * i)
        count = (cols.stop - cols.start) // 32
        copies.append(
            pltpu.make_async_copy(
                held.at[pl.ds(8 * i, count)], out.at[pl.ds(start + 8 * i, count)], sems.at[i]
            )
        )
        copies[-1].start()
    for copy in copies:
        copy.wait()


def weight_far(x_own, x_oth, near, g, before=None):
    width = g.shape[1]
    extra = [] if before is None else [before]
    return pl.pallas_call(
        functools.partial(weight_far_body, 0 if before is None else 12),
        in_specs=[VM] * 4 + [ANY] * len(extra),
        out_specs=ANY,
        out_shape=pltpu.HBM(PIECES, BF16),
        scratch_shapes=[
            pltpu.VMEM((width // 32,) + PIECES[1:], BF16),
            pltpu.SemaphoreType.DMA((2,)),
        ],
        input_output_aliases={4: 0} if extra else {},
        compiler_params=params(),
        cost_estimate=cost(2 * PAIR * D * width, 4 << 20),
        name="weight_far",
    )(x_own, x_oth, near, g, *extra)


def ordered(first, own, oth):
    return jnp.where(
        first, jnp.concatenate([own, oth], axis=1), jnp.concatenate([oth, own], axis=1)
    )


def grad_tokens_body(mix, dkv, mix_in, dkv_in, wq, wkv, out, ctx_out, done):
    done[...] = jnp.zeros_like(done)
    first = lax.axis_index("c") == 0
    dq = ordered(first, mix[:, QCOLS:], mix_in[:, QCOLS:])
    kv = dkv[...]
    kv_in = dkv_in[...]
    keys = ordered(first, kv[:, :HEAD_DIM], kv_in[:, :HEAD_DIM])
    vals = ordered(first, kv[:, HEAD_DIM:], kv_in[:, HEAD_DIM:])
    kv_full = jnp.concatenate([keys, vals], axis=1)
    for j in range(3):
        rows = slice(j * 512, (j + 1) * 512)
        out[:, rows] = (nt(dq, wq[rows, :]) + nt(kv_full, wkv[rows, :])).astype(BF16)
    ctx_out[...] = ordered(first, mix[:, :QCOLS], mix_in[:, :QCOLS])


def grad_tokens(mix, dkv, mix_in, dkv_in, w_query, w_keyval):
    return pl.pallas_call(
        grad_tokens_body,
        in_specs=[VM] * 6,
        out_specs=[VM] * 3,
        out_shape=[shape((OWN, D)), shape((OWN, D)), shape((8, 128), F32)],
        compiler_params=params(),
        cost_estimate=cost(2 * OWN * D * 2048, 8 << 20),
        name="grad_tokens",
    )(mix, dkv, mix_in, dkv_in, w_query, w_keyval)


def sum_plane_body(pieces, after, out):
    out[...] = jnp.sum(pieces[...].astype(F32), axis=0).astype(BF16)


def sum_plane(pieces, after):
    return pl.pallas_call(
        sum_plane_body,
        in_specs=[VM, VM],
        out_specs=VM,
        out_shape=shape(PIECES[1:]),
        compiler_params=params(),
        cost_estimate=cost(16 * 8 * ROWS * HEAD_DIM, 2 << 20),
        name="sum_plane",
    )(pieces, after)


def sum_line_body(lines, out):
    total = jnp.sum(lines[...].astype(F32), axis=0).astype(BF16)
    for s in range(8):
        out[s] = total


def sum_line(lines):
    return pl.pallas_call(
        sum_line_body,
        in_specs=[VM],
        out_specs=VM,
        out_shape=shape((8, 2, ROWS, HEAD_DIM)),
        compiler_params=params(),
        name="sum_line",
    )(lines)


def finish_body(blocks, query_w, keyval_w):
    for xh in range(2):
        for xl in range(2):
            for yh in range(2):
                for core in range(2):
                    rows = blocks[(xh * 2 + xl) * 2 + yh, core]
                    block = xh * 2 + yh
                    if block < 3:
                        at = (core * GROUP + xl * 3 + block) * HEAD_DIM
                        query_w[:, at : at + HEAD_DIM] = rows
                    else:
                        at = (xl * KV_HEADS + core) * HEAD_DIM
                        keyval_w[:, at : at + HEAD_DIM] = rows


def finish(blocks):
    return pl.pallas_call(
        finish_body,
        in_specs=[VM],
        out_specs=[VM, VM],
        out_shape=[shape((ROWS, D)), shape((ROWS, 512))],
        compiler_params=params(),
        name="finish",
    )(blocks)


def swap(value, axis="c"):
    return lax.ppermute(value, axis, [(0, 1), (1, 0)])


def shards(tokens, segments, w_query, w_keyval, grad_context):
    x_own = tokens[0]
    do_own = grad_context[0]
    x_oth = swap(x_own)
    do_oth = swap(do_own)
    far_own = swap(x_own, "xl")
    count = 32
    ring = ("zh", "zl", "yl", "c")
    x_own, wkv_here, wq_here, q_own, kv_own = project_own(x_own, w_keyval, w_query)
    kv, kv_sent = project_kv(x_oth, kv_own, wkv_here)
    halo = lax.ppermute(kv_sent, ring, [(i, i + 2) for i in range(count - 2)])
    q = project_q(x_oth, q_own, wq_here)
    segs = segments.reshape(-1, BLOCK)
    mix_last, dkv_last, low = attend_last(q, do_own, do_oth, kv, segs)
    mix, mix_oth, kept, sent, dkv, dkv_sent = attend(
        q, do_own, do_oth, kv, halo, low, mix_last, dkv_last
    )
    arrived = lax.ppermute(dkv_sent, ring, [(i + 2, i) for i in range(count - 2)])
    far = swap(sent, "xl")
    near = weight_near(x_own, x_oth, kept)
    far_own = relay(far_own, kept)
    far_oth = swap(far_own)
    dkv_own, dkv_oth, kept_kv, sent_kv = total_kv(dkv, arrived)
    far_kv = swap(sent_kv, "xl")
    near_kv = weight_near(x_own, x_oth, kept_kv)
    pieces = weight_far(far_own, far_oth, near, far)
    pieces = weight_far(far_own, far_oth, near_kv, far_kv, pieces)
    pieces = lax.all_to_all(pieces, ("xh", "yh", "yl", "zl"), 0, 0)
    mix_in = swap(mix_oth)
    dkv_in = swap(dkv_oth)
    grad_in, context, done = grad_tokens(mix, dkv_own, mix_in, dkv_in, w_query, w_keyval)
    plane = sum_plane(pieces, done)
    lines = lax.all_to_all(plane.reshape(8, ROWS, HEAD_DIM), ("zh", "c"), 0, 0)
    blocks = sum_line(lines.reshape(4, 2, ROWS, HEAD_DIM))
    blocks = lax.all_to_all(blocks, ("xh", "xl", "yh"), 0, 0)
    query_w, keyval_w = finish(blocks)
    return context[None], grad_in[None], query_w, keyval_w


def solution(mesh):
    names = ("xh", "xl", "yh", "zh", "zl", "yl", "c")
    fine = Mesh(mesh.devices.reshape(2, 2, 2, 4, 2, 2, 2), names)
    dp, ctx = names[:3], names[3:]
    return jax.shard_map(
        shards,
        mesh=fine,
        in_specs=(P(dp, ctx, None), P(dp, None), P(), P(), P(dp, ctx, None)),
        out_specs=(P(dp, ctx, None), P(dp, ctx, None), P(ctx, None), P(ctx, None)),
        check_vma=False,
    )
```
